128 devices in a mesh: ctx: 32 (over y, x_hi, z), fsdp: 4 (over x_lo, core).
Axes of the slice: x: 4 (x_hi: 2, x_lo: 2; x = x_hi * 2 + x_lo), y: 4, z: 4, core: 2. Of those that a mesh axis runs over, the one named last changes fastest.
Arguments:
- tokens: bfloat16 [4, 4096, 1536], P('fsdp', 'ctx'), may hold values from -6 to 6
- block_order: int32 [64], replicated, may hold values from 0 to 63, as said below
- gain_attn: bfloat16 [1536], P('fsdp'), may hold values from 0.5 to 1.5
- gain_mlp: bfloat16 [1536], P('fsdp'), may hold values from 0.5 to 1.5
- w_query: bfloat16 [1536, 1536], P('fsdp'), may hold values from -0.15625 to 0.15625
- w_key: bfloat16 [1536, 768], P('fsdp'), may hold values from -0.15625 to 0.15625
- w_value: bfloat16 [1536, 768], P('fsdp'), may hold values from -0.15625 to 0.15625
- w_out: bfloat16 [1536, 1536], P('fsdp'), may hold values from -0.875 to 0.875
- w_gate: bfloat16 [1536, 4096], P(None, 'fsdp'), may hold values from -0.15625 to 0.15625
- w_up: bfloat16 [1536, 4096], P(None, 'fsdp'), may hold values from -0.15625 to 0.15625
- w_down: bfloat16 [4096, 1536], P('fsdp'), may hold values from -0.09375 to 0.09375
- cotangent: bfloat16 [4, 4096, 1536], P('fsdp', 'ctx'), may hold values from -6 to 6
Outputs:
- layer_out: bfloat16 [4, 4096, 1536], P('fsdp', 'ctx')
- d_tokens: float32 [4, 4096, 1536], P('fsdp', 'ctx')
- grad_gain_attn: float32 [1536], P('fsdp')
- grad_gain_mlp: float32 [1536], P('fsdp')
- query_weight_gradient: float32 [1536, 1536], P('fsdp')
- grad_w_key: float32 [1536, 768], P('fsdp')
- grad_w_value: float32 [1536, 768], P('fsdp')
- grad_w_out: float32 [1536, 1536], P('fsdp')
- grad_w_gate: float32 [1536, 4096], P(None, 'fsdp')
- grad_w_up: float32 [1536, 4096], P(None, 'fsdp')
- grad_w_down: float32 [4096, 1536], P('fsdp')
The draws below stay inside these ranges and needn't reach their ends.
Inputs may be any that keep to these rules, and one draw needn't show every extreme that they name: `block_order`: places 2c and 2c+1 hold two blocks b and 63 - b (in either order); every block appears once.
All inputs are finite; a program needn't handle non-finite values.
Results may differ from the reference program's by a relative error of at most 0.03.
Values may be sent and summed in bfloat16 or wider, within the bound.
No kernel may reach another device: no remote copies, remote signals or barrier semaphores. Data moves between devices by JAX's collectives and lax.ppermute only.
A program may use at most 256 MiB of HBM per device.

```python
import math
import jax
import jax.numpy as jnp
from jax import lax

D = 1536
HEADS = 16
KV_HEADS = 8
HEAD_DIM = 96
FF = 4096
BLOCK = 64
SEQ = 4096
SEQS = 4
WINDOW = 2048


def draw_block_order(key, part):
    key = jax.random.fold_in(key, 7)
    count = SEQ // (2 * BLOCK)
    paired = jax.random.permutation(jax.random.fold_in(key, 1), count)
    flipped = jax.random.randint(jax.random.fold_in(key, 2), (count,), 0, 2)
    mirror = 2 * count - 1 - paired
    first = jnp.where(flipped == 1, mirror, paired)
    second = jnp.where(flipped == 1, paired, mirror)
    return jnp.stack([first, second], axis=1).reshape(-1).astype(jnp.int32)


def shard_levels(key, extent, pieces, least, largest):
    def one(position, blocks):
        draws = jax.random.uniform(jax.random.fold_in(jax.random.fold_in(key, 6), position), (blocks,), jnp.float32, least / len(pieces), largest / len(pieces))
        return jnp.repeat(jnp.exp(draws), extent[position] // blocks).reshape((-1,) + (1,) * (len(extent) - position - 1))

    level = one(*pieces[0])
    for cut in pieces[1:]:
        level = level * one(*cut)
    return level


def normal_values(own_key, shape, width, limit, pieces=(), dtype=jnp.bfloat16):
    drawn = width * jax.random.normal(own_key, shape, jnp.float32)
    if pieces:
        drawn = drawn * shard_levels(own_key, shape, pieces, -0.22, 0.18)
    return jnp.clip(drawn, -limit, limit).astype(dtype)


def setup_inputs(seed: int = 0) -> dict:
    streams_of = jax.random.split(jax.random.key(seed), 13)
    tokens = normal_values(streams_of[0], (SEQS, SEQ, D), 1.0, 6.0, ((0, 4), (1, 32)))
    block_order = draw_block_order(jax.random.fold_in(streams_of[12], 71), 0)
    gain_attn = jnp.clip(1.0 + 0.1 * jax.random.normal(streams_of[2], (D,), jnp.float32), 0.5, 1.5).astype(jnp.bfloat16)
    gain_mlp = jnp.clip(1.0 + 0.1 * jax.random.normal(streams_of[3], (D,), jnp.float32), 0.5, 1.5).astype(jnp.bfloat16)
    w_query = normal_values(streams_of[4], (D, HEADS * HEAD_DIM), D ** -0.5, 0.15625, ((0, 4),))
    w_key = normal_values(streams_of[5], (D, KV_HEADS * HEAD_DIM), D ** -0.5, 0.15625, ((0, 4),))
    w_value = normal_values(streams_of[6], (D, KV_HEADS * HEAD_DIM), D ** -0.5, 0.15625, ((0, 4),))
    w_out = normal_values(streams_of[7], (HEADS * HEAD_DIM, D), (HEADS * HEAD_DIM // 32) ** -0.5, 0.875, ((0, 4),))
    w_gate = normal_values(streams_of[8], (D, FF), D ** -0.5, 0.15625, ((1, 4),))
    w_up = normal_values(streams_of[9], (D, FF), D ** -0.5, 0.15625, ((1, 4),))
    w_down = normal_values(streams_of[10], (FF, D), FF ** -0.5, 0.09375, ((0, 4),))
    cotangent = normal_values(streams_of[11], (SEQS, SEQ, D), 1.0, 6.0, ((0, 4), (1, 32)))
    return {"tokens": tokens, "block_order": block_order, "gain_attn": gain_attn, "gain_mlp": gain_mlp, "w_query": w_query, "w_key": w_key, "w_value": w_value, "w_out": w_out, "w_gate": w_gate, "w_up": w_up, "w_down": w_down, "cotangent": cotangent}


EPS = 1e-05
ROPE_BASE = 10000.0
MASKED = -1e+30

@jax.custom_vjp
def low(v):
    return lax.optimization_barrier(v.astype(jnp.bfloat16)).astype(jnp.float32)

@jax.custom_vjp
def low_back(v):
    return v

def low_keep(v):
    return (low(v), None)

def low_pass(kept, grad):
    return (grad,)

def backward_retained(v):
    return (v, None)

def back_low(kept, grad):
    return (low(grad),)
low.defvjp(low_keep, low_pass)
low_back.defvjp(backward_retained, back_low)

def rope_tables(positions, head_size):
    half = head_size // 2
    freqs = ROPE_BASE ** (-jnp.arange(half).astype(jnp.float32) * 2.0 / head_size)
    angles = positions.astype(jnp.float32)[:, None] * freqs[None, :]
    angles = jnp.concatenate([angles, angles], axis=1)
    return (jnp.cos(angles), jnp.sin(angles))

def rotate(values, cosine, sine):
    half = values.shape[-1] // 2
    turned = jnp.concatenate([-values[..., half:], values[..., :half]], axis=-1)
    return values * cosine + turned * sine

def normed(values, gain):
    return values * lax.rsqrt(lax.optimization_barrier(jnp.mean(values * values, axis=-1, keepdims=True)) + EPS) * gain

def product(left_neighbor, right_neighbor):
    return jnp.einsum('xmt,tn->xmn', left_neighbor, right_neighbor, precision=lax.Precision.HIGHEST)

def attention(queries, keys, values, positions):
    seqs, length = (queries.shape[0], queries.shape[1])
    repeat = HEADS // KV_HEADS
    qblock = math.gcd(length, 128)
    count = length // qblock
    key_blk = positions // BLOCK
    split = queries.reshape(seqs, count, qblock, KV_HEADS, repeat, HEAD_DIM).transpose(1, 0, 2, 3, 4, 5)
    query_pos = positions.reshape(count, qblock)
    scale = HEAD_DIM ** (-0.5)

    def one_block(inputs):
        part, qpos = inputs
        raw = low_back(jnp.einsum('sqjrd,skjd->sjrqk', part, keys, precision=lax.Precision.HIGHEST))
        qblk = qpos // BLOCK
        same = qblk[:, None] == key_blk[None, :]
        earlier = (key_blk[None, :] < qblk[:, None]) & (qpos[:, None] - positions[None, :] < WINDOW)
        scores = jnp.where(same | earlier, raw * scale, MASKED)
        top = lax.optimization_barrier(jnp.max(scores, axis=-1, keepdims=True))
        expo = jnp.exp(scores - top)
        probs = expo / lax.optimization_barrier(jnp.sum(expo, axis=-1, keepdims=True))
        return jnp.einsum('sjrqk,skjd->sqjrd', low(probs), values, precision=lax.Precision.HIGHEST)
    result = lax.map(jax.checkpoint(one_block), (split, query_pos))
    return result.transpose(1, 0, 2, 3, 4, 5).reshape(seqs, length, HEADS * HEAD_DIM)

def reference(tokens, block_order, gain_attn, gain_mlp, w_query, w_key, w_value, w_out, w_gate, w_up, w_down, cotangent):
    offsets = jnp.arange(BLOCK).astype(jnp.int32)
    positions = (block_order[:, None] * BLOCK + offsets[None, :]).reshape(-1).astype(jnp.int32)
    cosine, sine = rope_tables(positions, HEAD_DIM)
    cosine = cosine[None, :, None, :]
    sine = sine[None, :, None, :]

    def forward(inputs, g_attn, g_mlp, m_query, m_key, m_value, m_out, m_gate, m_up, m_down):
        seqs, length = (inputs.shape[0], inputs.shape[1])
        x_attn = low(normed(inputs, g_attn))
        q_lin = low_back(product(x_attn, m_query)).reshape(seqs, length, HEADS, HEAD_DIM)
        k_lin = low_back(product(x_attn, m_key)).reshape(seqs, length, KV_HEADS, HEAD_DIM)
        values = low(low_back(product(x_attn, m_value))).reshape(seqs, length, KV_HEADS, HEAD_DIM)
        queries = low(rotate(q_lin, cosine, sine))
        keys = low(rotate(k_lin, cosine, sine))
        mixed = low(low_back(attention(queries, keys, values, positions)))
        hidden = inputs + low_back(product(mixed, m_out))
        x_mlp = low(normed(hidden, g_mlp))
        gate = low_back(product(x_mlp, m_gate))
        upper = low_back(product(x_mlp, m_up))
        activ = low(jax.nn.silu(gate) * upper)
        return hidden + low_back(product(activ, m_down))
    floats = (tokens, gain_attn, gain_mlp, w_query, w_key, w_value, w_out, w_gate, w_up, w_down)
    floats = tuple((item.astype(jnp.float32) for item in floats))
    result, pullback = jax.vjp(forward, *floats)
    grads = pullback(cotangent.astype(jnp.float32))
    return (result.astype(jnp.bfloat16), grads[0], grads[1], grads[2], grads[3], grads[4], grads[5], grads[6], grads[7], grads[8], grads[9])
```

```python
import functools

import jax
import jax.numpy as jnp
from jax import lax
from jax.experimental import pallas as pl
from jax.experimental.pallas import tpu as pltpu
from jax.sharding import Mesh, PartitionSpec as P

D = 1536
HEADS = 16
KV_HEADS = 8
HEAD_DIM = 96
HALF = HEAD_DIM // 2
FF = 4096
BLOCK = 64
SEQ = 4096
WINDOW_BLOCKS = 32
SHARDS = 4
ROWS = 128
TOK = SHARDS * ROWS
DS = D // SHARDS
FS = FF // SHARDS
EPS = 1e-05
ROPE_BASE = 10000.0
MASKED = -1e30
SCALE = HEAD_DIM ** (-0.5)
LOG2E = 1.4426950408889634
BF = jnp.bfloat16
F32 = jnp.float32

CHUNK_BLOCKS = 8
CHUNK = CHUNK_BLOCKS * BLOCK

SMEM_SPEC = pl.BlockSpec(memory_space=pltpu.SMEM)
VMEM_SPEC = pl.BlockSpec(memory_space=pltpu.VMEM)


def params(mib):
    return pltpu.CompilerParams(vmem_limit_bytes=mib * 1024 * 1024)


def call(kernel, outs, n_smem, n_vmem, mib, scratch=(), flops=0, nbytes=0):
    return pl.pallas_call(
        kernel,
        out_shape=outs,
        in_specs=[SMEM_SPEC] * n_smem + [VMEM_SPEC] * n_vmem,
        out_specs=jax.tree.map(lambda _: VMEM_SPEC, outs),
        scratch_shapes=list(scratch),
        compiler_params=params(mib),
        cost_estimate=pl.CostEstimate(flops=flops, bytes_accessed=nbytes, transcendentals=0),
    )


def sds(shape, dtype=BF):
    return jax.ShapeDtypeStruct(shape, dtype)


def dot(a, b):
    return jnp.dot(a, b, preferred_element_type=F32)


def dot_t(a, b):
    return lax.dot_general(a, b, (((1,), (1,)), ((), ())), preferred_element_type=F32)


def t_dot(a, b):
    return lax.dot_general(a, b, (((0,), (0,)), ((), ())), preferred_element_type=F32)


def swap_c(x):
    return lax.ppermute(x, "c", [(0, 1), (1, 0)])


def swap_xl(x):
    return lax.ppermute(x, "xl", [(0, 1), (1, 0)])


def swap_both(x):
    return lax.ppermute(x, ("xl", "c"), [(i, i ^ 3) for i in range(4)])


def swap_far(x):
    pairs = []
    for xh in range(2):
        for xl in range(2):
            place = 2 * xh + xl
            other = (place + 1) % 4 if xl else (place + 3) % 4
            for c in range(2):
                pairs.append((place * 2 + c, other * 2 + 1 - c))
    return lax.ppermute(x, ("xh", "xl", "c"), pairs)


def swap_e(x):
    return lax.ppermute(x, "xh", [(0, 1), (1, 0)])


NEAR = [(0, 1), (1, 0), (2, 3), (3, 2)]
AROUND = [(1, 2), (2, 1), (0, 3), (3, 0)]
CUBE = (("y", NEAR), ("y", AROUND), ("z", NEAR), ("z", AROUND))


def swap_cube(x, dim):
    axis, pairs = CUBE[dim % 4]
    return lax.ppermute(x, axis, pairs)


def from_z(x, m):
    return lax.ppermute(x, "z", [((i + m) % 4, i) for i in range(4)])


def to_z(x, m):
    return lax.ppermute(x, "z", [(i, (i + m) % 4) for i in range(4)])


def gather_slots(own):
    far = swap_xl(own)
    return own, swap_c(own), far, swap_c(far)


def scatter_slots(keep, send):
    got = swap_c(send)
    pair = keep.astype(F32) + got.astype(F32)
    far = swap_xl(pair[1].astype(BF))
    return pair[0], far.astype(F32)


def cube_reduce(keeps, sends):
    keeps, sends = list(keeps), list(sends)
    for step in range(4):
        for p in range(4):
            got = swap_cube(sends[p], p + step)
            total = (keeps[p].astype(F32) + got.astype(F32)).astype(BF)
            half = total.shape[0] // 2
            keeps[p], sends[p] = (total[:half], total[half:]) if step < 3 else (total, None)
    return [(k.astype(F32) + swap_e(k).astype(F32)).astype(BF) for k in keeps]


def cube_gather(parts):
    owns, gots = list(parts), [None] * 4
    for step in (3, 2, 1, 0):
        for p in range(4):
            if gots[p] is not None:
                owns[p] = jnp.concatenate([owns[p], gots[p]], axis=0)
            gots[p] = swap_cube(owns[p], p + step)
    return owns, gots


def cube_index(portion, bits):
    out = 0
    for t in range(4):
        out = out * 2 + bits[(portion + t) % 4]
    return out


def pack_weights_kernel(sc, wq, wk, wv, o0, o1, o2, o3, tmp):
    f = sc[0]
    for g in range(4):
        tmp[g, :, 0:DS] = wq[:, DS * g : DS * (g + 1)]
        tmp[g, :, DS : DS + 192] = wk[:, 192 * g : 192 * (g + 1)]
        tmp[g, :, DS + 192 : 768] = wv[:, 192 * g : 192 * (g + 1)]
    for k, out in enumerate((o0, o1, o2, o3)):
        out[...] = tmp[f ^ k]


def qkv_kernel(sc, x0, x1, x2, x3, gain, w0, w1, w2, w3, cos, sin, xa, qkv):
    f = sc[0]
    for k, x in enumerate((x0, x1, x2, x3)):
        u = x[...].astype(F32)
        r = lax.rsqrt(jnp.mean(u * u, axis=-1, keepdims=True) + EPS)
        xa[ROWS * k : ROWS * (k + 1), :] = (u * r * gain[...]).astype(BF)
    lin = jnp.zeros((TOK, 768), F32)
    for k, w in enumerate((w0, w1, w2, w3)):
        at = pl.multiple_of((f ^ k) * DS, 128)
        lin = lin + dot(xa[:, pl.ds(at, DS)], w[...])
    co, si = cos[...], sin[...]
    for k in range(4):
        part = lin[ROWS * k : ROWS * (k + 1)]
        for j in range(2):
            for n, at in enumerate((192 * j, 192 * j + 96, DS + 96 * j)):
                u = part[:, at : at + HEAD_DIM]
                turned = jnp.concatenate([-u[:, HALF:], u[:, :HALF]], axis=1)
                qkv[2 * k + j, :, 96 * n : 96 * (n + 1)] = (u * co + turned * si).astype(BF)
            at = DS + 192 + 96 * j
            qkv[2 * k + j, :, 288:384] = part[:, at : at + 96].astype(BF)


def attention_kernel(qb, kb, qkv, kv1, kv2, kv3, o, lse, ks, vs):
    def place(b, _):
        src = pl.multiple_of(b * BLOCK, BLOCK)
        for m, ref in enumerate((qkv, kv1, kv2, kv3)):
            at = 192 if m == 0 else 0
            dst = pl.multiple_of(kb[m * 16 + b] * BLOCK, BLOCK)
            ks[pl.ds(dst, BLOCK), :] = ref[pl.ds(src, BLOCK), at : at + 96]
            vs[pl.ds(dst, BLOCK), :] = ref[pl.ds(src, BLOCK), at + 96 : at + 192]
        return 0

    lax.fori_loop(0, 16, place, 0)
    two = SCALE * LOG2E

    def one(n, _):
        i = qb[n]
        row = pl.multiple_of(n * BLOCK, BLOCK)
        q2 = jnp.concatenate(
            [qkv[pl.ds(row, BLOCK), 0:96], qkv[pl.ds(row, BLOCK), 96:192]], axis=0
        )
        first = jnp.maximum(i - (WINDOW_BLOCKS - 1), 0)

        def update(carry, s, v):
            top, total, acc = carry
            new = jnp.maximum(top, jnp.max(s, axis=1, keepdims=True))
            p = jnp.exp2((s - new) * two)
            back = jnp.exp2((top - new) * two)
            total = total * back + jnp.sum(p, axis=1, keepdims=True)
            return new, total, acc * back + dot(p.astype(BF), v)

        def chunk(t, carry):
            at = pl.multiple_of((first + t * CHUNK_BLOCKS) * BLOCK, BLOCK)
            s = dot_t(q2, ks[pl.ds(at, CHUNK), :])
            key = lax.broadcasted_iota(jnp.int32, s.shape, 1)
            s = jnp.where(key < (i + 1) * BLOCK - at, s, MASKED)
            return update(carry, s, vs[pl.ds(at, CHUNK), :])

        def edge(t, carry):
            at = pl.multiple_of((i - WINDOW_BLOCKS) * BLOCK, BLOCK)
            s = dot_t(q2, ks[pl.ds(at, BLOCK), :])
            key = lax.broadcasted_iota(jnp.int32, s.shape, 1)
            query = lax.broadcasted_iota(jnp.int32, s.shape, 0) % BLOCK
            s = jnp.where(key > query, s, MASKED)
            return update(carry, s, vs[pl.ds(at, BLOCK), :])

        carry = (
            jnp.full((ROWS, 1), MASKED, F32),
            jnp.zeros((ROWS, 1), F32),
            jnp.zeros((ROWS, HEAD_DIM), F32),
        )
        carry = lax.fori_loop(0, (i - first) // CHUNK_BLOCKS + 1, chunk, carry)
        carry = lax.fori_loop(0, jnp.where(i >= WINDOW_BLOCKS, 1, 0), edge, carry)
        top, total, acc = carry
        out = (acc / total).astype(BF)
        o[pl.ds(row, BLOCK), 0:96] = out[:BLOCK]
        o[pl.ds(row, BLOCK), 96:192] = out[BLOCK:]
        tall = jnp.broadcast_to(top * two + jnp.log2(total), (ROWS, ROWS))
        lse[n] = tall.T[0:8]
        return 0

    lax.fori_loop(0, 16, one, 0)


def attention_back_kernel(
    qb, kb, qkv, d_o, o, lse, ks, vs, dq, g0, g1, g2, g3, dks, dvs
):
    dks[...] = jnp.zeros_like(dks)
    dvs[...] = jnp.zeros_like(dvs)
    two = SCALE * LOG2E

    def one(n, _):
        i = qb[n]
        row = pl.multiple_of(n * BLOCK, BLOCK)
        rows = pl.ds(row, BLOCK)
        q2 = jnp.concatenate([qkv[rows, 0:96], qkv[rows, 96:192]], axis=0)
        do2 = jnp.concatenate([d_o[rows, 0:96], d_o[rows, 96:192]], axis=0)
        o2 = jnp.concatenate([o[rows, 0:96], o[rows, 96:192]], axis=0)
        inner = do2.astype(F32) * o2.astype(F32)
        inner = jnp.broadcast_to(jnp.sum(inner, axis=1, keepdims=True), (ROWS, ROWS)).T[0:1]
        top = lse[n, 0:1]
        first = jnp.maximum(i - (WINDOW_BLOCKS - 1), 0)

        def update(acc, at, size, allowed):
            span = pl.ds(at, size)
            k, v = ks[span, :], vs[span, :]
            s = dot_t(k, q2)
            p = jnp.where(allowed(s.shape), jnp.exp2(s * two - top), 0.0)
            ds = (p * (dot_t(v, do2) - inner)).astype(BF)
            dks[span, :] += dot(ds, q2)
            dvs[span, :] += dot(p.astype(BF), do2)
            return acc + t_dot(ds, k)

        def chunk(t, acc):
            at = pl.multiple_of((first + t * CHUNK_BLOCKS) * BLOCK, BLOCK)
            limit = (i + 1) * BLOCK - at
            return update(
                acc, at, CHUNK, lambda sh: lax.broadcasted_iota(jnp.int32, sh, 0) < limit
            )

        def edge(t, acc):
            at = pl.multiple_of((i - WINDOW_BLOCKS) * BLOCK, BLOCK)
            return update(
                acc,
                at,
                BLOCK,
                lambda sh: lax.broadcasted_iota(jnp.int32, sh, 0)
                > lax.broadcasted_iota(jnp.int32, sh, 1) % BLOCK,
            )

        acc = jnp.zeros((ROWS, HEAD_DIM), F32)
        acc = lax.fori_loop(0, (i - first) // CHUNK_BLOCKS + 1, chunk, acc)
        acc = lax.fori_loop(0, jnp.where(i >= WINDOW_BLOCKS, 1, 0), edge, acc)
        acc = (acc * SCALE).astype(BF)
        dq[rows, 0:96] = acc[:BLOCK]
        dq[rows, 96:192] = acc[BLOCK:]
        return 0

    lax.fori_loop(0, 16, one, 0)

    def place(b, _):
        dst = pl.ds(pl.multiple_of(b * BLOCK, BLOCK), BLOCK)
        for m, ref in enumerate((g0, g1, g2, g3)):
            src = pl.ds(pl.multiple_of(kb[m * 16 + b] * BLOCK, BLOCK), BLOCK)
            ref[dst, 0:96] = (dks[src, :] * SCALE).astype(BF)
            ref[dst, 96:192] = dvs[src, :].astype(BF)
        return 0

    lax.fori_loop(0, 16, place, 0)


def out_kernel(o, w, keep, send):
    for k in range(4):
        total = dot(o[2 * k], w[0:192, :]) + dot(o[2 * k + 1], w[192:384, :])
        (keep, send)[k % 2][k // 2] = total.astype(BF)


def d_o_kernel(b0, b1, b2, b3, w, d_o):
    for k, b in enumerate((b0, b1, b2, b3)):
        d = dot_t(b[...], w[...]).astype(BF)
        d_o[2 * k] = d[:, 0:192]
        d_o[2 * k + 1] = d[:, 192:384]


FBLOCK = 256


def ffn_kernel(sc, x0, x1, x2, x3, y0, y1, y2, y3, wg, wu, wd, act, dg, du, keep, send, xs, ys, acc):
    n = pl.program_id(0)

    @pl.when(n == 0)
    def _():
        for k, (x, y) in enumerate(zip((x0, x1, x2, x3), (y0, y1, y2, y3))):
            xs[ROWS * k : ROWS * (k + 1), :] = x[...]
            ys[ROWS * k : ROWS * (k + 1), :] = y[...]

    gate = dot(xs[...], wg[...])
    up = dot(xs[...], wu[...])
    da = dot_t(ys[...], wd[...])
    sg = jax.nn.sigmoid(gate)
    act[...] = (gate * sg * up).astype(BF)
    d_gate = (da * up * sg * (1.0 + gate * (1.0 - sg))).astype(BF)
    d_up = (da * gate * sg).astype(BF)
    dg[...] = d_gate
    du[...] = d_up
    dx = dot_t(d_gate, wg[...]) + dot_t(d_up, wu[...])

    @pl.when(n == 0)
    def _():
        acc[...] = dx

    @pl.when(n > 0)
    def _():
        acc[...] += dx

    @pl.when(n == FS // FBLOCK - 1)
    def _():
        for k in range(4):
            (keep, send)[k % 2][k // 2] = acc[ROWS * k : ROWS * (k + 1), :].astype(BF)


def ffn(sc, xs, ys, wg, wu, wd):
    full = pl.BlockSpec((ROWS, D), lambda n, s: (0, 0))
    side = pl.BlockSpec((2, ROWS, D), lambda n, s: (0, 0, 0))
    cols = pl.BlockSpec((D, FBLOCK), lambda n, s: (0, n))
    rel = pl.BlockSpec((TOK, FBLOCK), lambda n, s: (0, n ^ s[2]))
    return pl.pallas_call(
        ffn_kernel,
        grid_spec=pltpu.PrefetchScalarGridSpec(
            num_scalar_prefetch=1,
            grid=(FS // FBLOCK,),
            in_specs=[full] * 8 + [cols, cols, pl.BlockSpec((FBLOCK, D), lambda n, s: (n, 0))],
            out_specs=[rel, rel, rel, side, side],
            scratch_shapes=[
                pltpu.VMEM((TOK, D), BF),
                pltpu.VMEM((TOK, D), BF),
                pltpu.VMEM((TOK, D), F32),
            ],
        ),
        out_shape=[sds((TOK, FS))] * 3 + [sds((2, ROWS, D))] * 2,
        compiler_params=params(44),
        cost_estimate=pl.CostEstimate(
            flops=2 * TOK * D * FS * 5, bytes_accessed=16_000_000, transcendentals=0
        ),
    )(sc, *xs, *ys, wg, wu, wd)


def mlp_out_kernel(sc, act, wd, keep, send):
    gz = sc[2]
    for k in range(4):
        total = jnp.zeros((ROWS, D), F32)
        for b in range(FS // FBLOCK):
            at = pl.multiple_of((b ^ gz) * FBLOCK, FBLOCK)
            total += dot(
                act[ROWS * k : ROWS * (k + 1), pl.ds(at, FBLOCK)],
                wd[FBLOCK * b : FBLOCK * (b + 1), :],
            )
        (keep, send)[k % 2][k // 2] = total.astype(BF)


def ffn_grads_kernel(sc, x0, x1, x2, x3, y0, y1, y2, y3, act, dg, du, *outs):
    gy = sc[1]
    keeps, sends = outs[:4], outs[4:8]

    def put(p, ra, rb, at, tile):
        index = cube_index(p, (ra & 1, ra >> 1, rb & 1, rb >> 1))
        ref = (keeps, sends)[index >> 3][p]
        ref[index & 7, at : at + tile.shape[0], :] = tile.astype(BF)

    for ra in range(4):
        cols = pl.ds(pl.multiple_of((ra ^ gy) * DS, 128), DS)
        xa = jnp.concatenate([x[:, cols] for x in (x0, x1, x2, x3)], axis=0)
        ya = jnp.concatenate([y[:, cols] for y in (y0, y1, y2, y3)], axis=0)
        for n, d in enumerate((dg, du)):
            for rb in range(4):
                tile = t_dot(xa, d[:, 256 * rb : 256 * (rb + 1)])
                for p in range(4):
                    lane, row = 128 * (p // 2), 192 * (p % 2)
                    put(p, ra, rb, 192 * n, tile[row : row + 192, lane : lane + 128])
        for rb in range(4):
            tile = t_dot(act[:, 256 * rb : 256 * (rb + 1)], ya)
            for p in range(4):
                at = 384
                row = 192 * p
                while row < 192 * (p + 1):
                    lane, r = row // 256, row % 256
                    size = min(256 - r, 192 * (p + 1) - row)
                    put(p, ra, rb, at, tile[r : r + size, 128 * lane : 128 * (lane + 1)])
                    at += size
                    row += size


def pick(owns, gots, p, bits, rows):
    index = cube_index(p, bits)
    rest = index & 7
    return jnp.where(index >= 8, gots[p][rest, rows, :], owns[p][rest, rows, :])


def ffn_place_kernel(sc, *refs):
    owns, gots = refs[0:4], refs[4:8]
    wg, wu, gate, up, down, gain = refs[8:]
    gy, gz = sc[1], sc[2]
    ra = pl.program_id(0) ^ gy
    for bb in range(4):
        rb = bb ^ gz
        bits = (ra & 1, ra >> 1, rb & 1, rb >> 1)
        for p in range(4):
            lane, row = 256 * bb + 128 * (p // 2), 192 * (p % 2)
            for n, ref in enumerate((gate, up)):
                tile = pick(owns, gots, p, bits, slice(192 * n, 192 * (n + 1)))
                ref[row : row + 192, lane : lane + 128] = tile.astype(F32)
            at, row = 384, 192 * p
            while row < 192 * (p + 1):
                lane, r = row // 256, row % 256
                size = min(256 - r, 192 * (p + 1) - row)
                tile = pick(owns, gots, p, bits, slice(at, at + size))
                down[256 * bb + r : 256 * bb + r + size, 128 * lane : 128 * (lane + 1)] = (
                    tile.astype(F32)
                )
                at += size
                row += size
    prod = wg[...].astype(F32) * gate[...] + wu[...].astype(F32) * up[...]
    gain[...] = jnp.sum(prod, axis=1, keepdims=True)


def ffn_place(sc, owns, gots, wg, wu):
    whole = pl.BlockSpec((8, 576, 128), lambda n, s: (0, 0, 0))
    rows = pl.BlockSpec((DS, FS), lambda n, s: (n, 0))
    return pl.pallas_call(
        ffn_place_kernel,
        grid_spec=pltpu.PrefetchScalarGridSpec(
            num_scalar_prefetch=1,
            grid=(4,),
            in_specs=[whole] * 8 + [rows, rows],
            out_specs=[
                rows,
                rows,
                pl.BlockSpec((FS, DS), lambda n, s: (0, n)),
                pl.BlockSpec((DS, 1), lambda n, s: (n, 0)),
            ],
        ),
        out_shape=[sds((D, FS), F32), sds((D, FS), F32), sds((FS, D), F32), sds((D, 1), F32)],
        compiler_params=params(56),
        cost_estimate=pl.CostEstimate(flops=0, bytes_accessed=35_000_000, transcendentals=0),
    )(sc, *owns, *gots, wg, wu)


OUT_ROWS = (80, 80, 64, 64)
OUT_AT = (0, 80, 160, 224)
QKV_ROWS = 144


def d_xa_kernel(sc, d, w0, w1, w2, w3, cos, sin, lin, keep, send, dq, dk, dv):
    f = sc[0]
    co, si = cos[...], sin[...]
    for k in range(4):
        rows = slice(ROWS * k, ROWS * (k + 1))
        for j in range(2):
            for n in range(3):
                g = d[2 * k + j, :, 96 * n : 96 * (n + 1)].astype(F32)
                w = g * si
                turned = jnp.concatenate([w[:, HALF:], -w[:, :HALF]], axis=1)
                g = (g * co + turned).astype(BF)
                lin[rows, 384 * j + 96 * n : 384 * j + 96 * (n + 1)] = g
                if n < 2:
                    dq[rows, 192 * j + 96 * n : 192 * j + 96 * (n + 1)] = g
                else:
                    dk[rows, 96 * j : 96 * (j + 1)] = g
            g = d[2 * k + j, :, 288:384]
            lin[rows, 384 * j + 288 : 384 * j + 384] = g
            dv[rows, 96 * j : 96 * (j + 1)] = g
    for k, w in enumerate((w0, w1, w2, w3)):
        cols = pl.ds(pl.multiple_of((f ^ k) * DS, 128), DS)
        total = dot_t(dq[...], w[:, 0:DS])
        total += dot_t(dk[...], w[:, DS : DS + 192])
        total += dot_t(dv[...], w[:, DS + 192 : 768])
        total = total.astype(BF)
        for s in range(4):
            (keep, send)[s % 2][s // 2, :, cols] = total[ROWS * s : ROWS * (s + 1)]


def attn_grads_kernel(sc, xa, lin, o, b0, b1, b2, b3, *refs):
    keeps, sends, tmp = refs[:4], refs[4:8], refs[8]
    f, gy, gz = sc[0], sc[1], sc[2]
    near = gy | ((gz & 1) << 2)
    side = gz >> 1

    def put(p, bits, at, tile):
        index = cube_index(p, bits)
        ref = (keeps, sends)[index >> 3][p]
        ref[index & 7, at : at + tile.shape[0], :] = tile.astype(BF)

    for p in range(4):
        cols = pl.ds(pl.multiple_of((f ^ p) * DS, 128), DS)
        tmp[:, 0:768] = t_dot(xa[:, cols], lin[...])
        for r in range(8):
            row = pl.multiple_of((r ^ near) * 48, 48)
            for c in range(2):
                at = pl.multiple_of((c ^ side) * DS, 128)
                for t in range(3):
                    tile = tmp[pl.ds(row, 48), pl.ds(pl.multiple_of(at + 128 * t, 128), 128)]
                    put(p, (r & 1, (r >> 1) & 1, r >> 2, c), 48 * t, tile)
    bs = jnp.concatenate([b0[...], b1[...], b2[...], b3[...]], axis=0)
    for j in range(2):
        oj = jnp.concatenate([o[2 * k + j] for k in range(4)], axis=0)
        tmp[192 * j : 192 * (j + 1), :] = t_dot(oj, bs)
    for ra in range(4):
        row = pl.multiple_of((ra ^ gy) * 96, 96)
        for rb in range(4):
            at = pl.multiple_of((rb ^ gz) * DS, 128)
            bits = (ra & 1, ra >> 1, rb & 1, rb >> 1)
            for p in range(4):
                start, put_at = OUT_AT[p], QKV_ROWS
                while start < OUT_AT[p] + OUT_ROWS[p]:
                    t, r = start // 96, start % 96
                    size = min(96 - r, OUT_AT[p] + OUT_ROWS[p] - start)
                    tile = tmp[
                        pl.ds(pl.multiple_of(row + r, 16), size),
                        pl.ds(pl.multiple_of(at + 128 * t, 128), 128),
                    ]
                    put(p, bits, put_at, tile)
                    put_at += size
                    start += size


def attn_place_kernel(sc, *refs):
    owns, gots = refs[0:4], refs[4:8]
    wq, wk, wv, gain_in, q, k, v, out, gain, tmp = refs[8:]
    f, gy, gz = sc[0], sc[1], sc[2]
    near = gy | ((gz & 1) << 2)
    side = gz >> 1
    for p in range(4):
        for rr in range(8):
            r = rr ^ near
            for cc in range(2):
                c = cc ^ side
                bits = (r & 1, (r >> 1) & 1, r >> 2, c)
                tile = pick(owns, gots, p, bits, slice(0, QKV_ROWS)).astype(F32)
                for t in range(3):
                    lane = 384 * cc + 128 * t
                    tmp[f ^ p, 48 * rr : 48 * (rr + 1), lane : lane + 128] = tile[
                        48 * t : 48 * (t + 1)
                    ]
    for g in range(4):
        for j in range(2):
            q[:, 384 * g + 192 * j : 384 * g + 192 * (j + 1)] = tmp[g, :, 384 * j : 384 * j + 192]
            k[:, 192 * g + 96 * j : 192 * g + 96 * (j + 1)] = tmp[
                g, :, 384 * j + 192 : 384 * j + 288
            ]
            v[:, 192 * g + 96 * j : 192 * g + 96 * (j + 1)] = tmp[
                g, :, 384 * j + 288 : 384 * j + 384
            ]
    total = jnp.sum(wq[...].astype(F32) * q[...], axis=1, keepdims=True)
    total += jnp.sum(wk[...].astype(F32) * k[...], axis=1, keepdims=True)
    total += jnp.sum(wv[...].astype(F32) * v[...], axis=1, keepdims=True)
    gain[...] = total / gain_in[...]
    for aa in range(4):
        ra = aa ^ gy
        for bb in range(4):
            rb = bb ^ gz
            bits = (ra & 1, ra >> 1, rb & 1, rb >> 1)
            for p in range(4):
                start, at = OUT_AT[p], QKV_ROWS
                while start < OUT_AT[p] + OUT_ROWS[p]:
                    t, r = start // 96, start % 96
                    size = min(96 - r, OUT_AT[p] + OUT_ROWS[p] - start)
                    tile = pick(owns, gots, p, bits, slice(at, at + size))
                    lane = 384 * bb + 128 * t
                    out[96 * aa + r : 96 * aa + r + size, lane : lane + 128] = tile.astype(F32)
                    at += size
                    start += size


def rope_tables(positions):
    freqs = ROPE_BASE ** (-jnp.arange(HALF).astype(F32) * 2.0 / HEAD_DIM)
    angles = positions.astype(F32)[:, None] * freqs[None, :]
    angles = jnp.concatenate([angles, angles], axis=1)
    return jnp.cos(angles), jnp.sin(angles)


def norm_factor(values):
    return lax.rsqrt(jnp.mean(values * values, axis=-1, keepdims=True) + EPS)


def norm_back(values, factor, gain, grads):
    weighted = grads * gain
    inner = jnp.mean(weighted * values, axis=-1, keepdims=True)
    return factor * weighted - values * (factor * factor * factor) * inner


def exchange(x):
    shape = x.shape
    x = x.reshape(-1, shape[-1])
    return lax.all_to_all(x, ("y", "xh"), 0, 0, tiled=True).reshape(shape)


def body(
    tokens,
    block_order,
    gain_attn,
    gain_mlp,
    w_query,
    w_key,
    w_value,
    w_out,
    w_gate,
    w_up,
    w_down,
    cotangent,
):
    y, xh, z = lax.axis_index("y"), lax.axis_index("xh"), lax.axis_index("z")
    xl, c = lax.axis_index("xl"), lax.axis_index("c")
    f = xl * 2 + c
    gy, gz = y ^ (y >> 1), z ^ (z >> 1)
    sc = jnp.stack([f, gy, gz, xh]).astype(jnp.int32)
    own_x, own_dy = tokens[0], cotangent[0]

    blocks = block_order.reshape(8, 4, 2)
    place = (y * 2 + xh) * 4 + z
    own_blocks = lax.dynamic_slice_in_dim(block_order, 2 * place, 2)
    positions = (own_blocks[:, None] * BLOCK + jnp.arange(BLOCK)).reshape(-1)
    cos, sin = rope_tables(positions)
    key_blocks = jnp.stack(
        [
            lax.dynamic_index_in_dim(blocks, (z + m) % 4, axis=1, keepdims=False).reshape(-1)
            for m in range(4)
        ]
    ).reshape(-1)
    query_blocks = key_blocks[:16]

    xs = gather_slots(own_x)
    gains = jnp.stack(gather_slots(jnp.stack([gain_attn, gain_mlp])))
    gains = jnp.where(c == 0, gains, gains[jnp.array([1, 0, 3, 2])])
    gains = jnp.where(xl == 0, gains, gains[jnp.array([2, 3, 0, 1])])
    gains = gains.transpose(1, 0, 2).reshape(2, 1, D).astype(F32)
    gain_a, gain_m = gains[0], gains[1]
    packs = call(
        pack_weights_kernel,
        [sds((DS, 768))] * 4,
        1,
        3,
        16,
        [pltpu.VMEM((4, DS, 768), BF)],
        0,
        5_000_000,
    )(sc, w_query, w_key, w_value)
    ws = (packs[0], swap_c(packs[1]), swap_xl(packs[2]), swap_far(packs[3]))

    xa, qkv = call(
        qkv_kernel,
        [sds((TOK, D)), sds((8, ROWS, 384))],
        1,
        11,
        32,
        (),
        2 * TOK * D * 768,
        6_000_000,
    )(sc, *xs, gain_a, *ws, cos, sin)

    qkv = exchange(qkv).reshape(8 * ROWS, 384)
    kv = qkv[:, 192:]
    kvs = [from_z(kv, m) for m in (1, 2, 3)]
    o, lse, ks, vs = call(
        attention_kernel,
        [sds((1024, 192)), sds((16, 8, ROWS), F32), sds((SEQ, 96)), sds((SEQ, 96))],
        2,
        4,
        32,
        (),
        2 * 1024 * 2 * 1600 * 96 * 2,
        5_000_000,
    )(query_blocks, key_blocks, qkv, *kvs)
    o_tok = exchange(o.reshape(8, ROWS, 192))

    keep, send = call(
        out_kernel, [sds((2, ROWS, D))] * 2, 0, 2, 16, (), 2 * TOK * D * DS, 3_000_000
    )(o_tok, w_out)
    near, far = scatter_slots(keep, send)
    x32 = own_x.astype(F32)
    hidden = x32 + near + far
    factor_m = norm_factor(hidden)
    xm = (hidden * factor_m * gain_m).astype(BF)
    xms = gather_slots(xm)
    dys = gather_slots(own_dy)
    act, dg, du, keep, send = ffn(sc, xms, dys, w_gate, w_up, w_down)
    near, far = scatter_slots(keep, send)
    d_xm = near + far
    d_hidden = own_dy.astype(F32) + norm_back(hidden, factor_m, gain_m, d_xm)
    d_br = d_hidden.astype(BF)
    d_brs = gather_slots(d_br)

    grads = call(
        ffn_grads_kernel,
        [sds((8, 576, 128))] * 8,
        1,
        11,
        44,
        (),
        2 * TOK * D * FS * 3,
        16_000_000,
    )(sc, *xms, *dys, act, dg, du)
    parts = cube_reduce(grads[:4], grads[4:])
    owns, gots = cube_gather(parts)
    g_gate, g_up, g_down, g_gain_m = ffn_place(sc, owns, gots, w_gate, w_up)
    g_gain_m = g_gain_m.reshape(4, 384)
    g_gain_m = [lax.dynamic_index_in_dim(g_gain_m, f ^ k, keepdims=False) for k in range(4)]
    g_gain_m = (
        g_gain_m[0] + swap_c(g_gain_m[1]) + swap_xl(g_gain_m[2]) + swap_both(g_gain_m[3])
    ) / gain_mlp.astype(F32)

    keep, send = call(
        mlp_out_kernel, [sds((2, ROWS, D))] * 2, 1, 2, 24, (), 2 * TOK * D * FS, 6_000_000
    )(sc, act, w_down)
    near, far = scatter_slots(keep, send)
    layer_out = (hidden + near + far).astype(BF)

    d_o = call(
        d_o_kernel, sds((8, ROWS, 192)), 0, 5, 16, (), 2 * TOK * D * DS, 4_000_000
    )(*d_brs, w_out)
    d_o = exchange(d_o).reshape(1024, 192)
    dq, g0, g1, g2, g3 = call(
        attention_back_kernel,
        [sds((1024, 192))] * 5,
        2,
        6,
        44,
        [pltpu.VMEM((SEQ, 96), F32), pltpu.VMEM((SEQ, 96), F32)],
        2 * 1024 * 2 * 1600 * 96 * 5,
        8_000_000,
    )(query_blocks, key_blocks, qkv, d_o, o, lse, ks, vs)
    d_kv = g0.astype(F32)
    for m, g in ((1, g1), (2, g2), (3, g3)):
        d_kv = d_kv + to_z(g, m).astype(F32)
    d_qkv = jnp.concatenate([dq, d_kv.astype(BF)], axis=1)
    d_qkv = exchange(d_qkv.reshape(8, ROWS, 384))

    lin, keep, send = call(
        d_xa_kernel,
        [sds((TOK, 768)), sds((2, ROWS, D)), sds((2, ROWS, D))],
        1,
        7,
        32,
        [pltpu.VMEM((TOK, DS), BF), pltpu.VMEM((TOK, 192), BF), pltpu.VMEM((TOK, 192), BF)],
        2 * TOK * D * 768,
        6_000_000,
    )(sc, d_qkv, *ws, cos, sin)
    near, far = scatter_slots(keep, send)
    d_xa = near + far
    factor_a = norm_factor(x32)
    d_tokens = d_hidden + norm_back(x32, factor_a, gain_a, d_xa)

    shapes = [sds((8, QKV_ROWS + n, 128)) for n in OUT_ROWS]
    grads = call(
        attn_grads_kernel,
        shapes + shapes,
        1,
        7,
        32,
        [pltpu.VMEM((DS, D), F32)],
        2 * TOK * D * (768 + DS),
        10_000_000,
    )(sc, xa, lin, o_tok, *d_brs)
    parts = cube_reduce(grads[:4], grads[4:])
    moved = [parts[0]]
    for p, swap in ((1, swap_c), (2, swap_xl), (3, swap_both)):
        got = swap(parts[p][:, :QKV_ROWS])
        moved.append(jnp.concatenate([got, parts[p][:, QKV_ROWS:]], axis=1))
    owns, gots = cube_gather(moved)
    g_query, g_key, g_value, g_out, g_gain_a = call(
        attn_place_kernel,
        [
            sds((DS, D), F32),
            sds((DS, 768), F32),
            sds((DS, 768), F32),
            sds((DS, D), F32),
            sds((DS, 1), F32),
        ],
        1,
        12,
        40,
        [pltpu.VMEM((4, DS, 768), F32)],
        0,
        16_000_000,
    )(sc, *owns, *gots, w_query, w_key, w_value, gain_attn.astype(F32).reshape(DS, 1))

    return (
        layer_out[None],
        d_tokens[None],
        g_gain_a.reshape(DS),
        g_gain_m.reshape(DS),
        g_query,
        g_key,
        g_value,
        g_out,
        g_gate,
        g_up,
        g_down,
    )


def solution(mesh):
    cube = Mesh(mesh.devices.reshape(4, 2, 4, 2, 2), ("y", "xh", "z", "xl", "c"))
    fsdp, ctx = ("xl", "c"), ("y", "xh", "z")
    return jax.shard_map(
        body,
        mesh=cube,
        in_specs=(
            P(fsdp, ctx, None),
            P(),
            P(fsdp),
            P(fsdp),
            P(fsdp, None),
            P(fsdp, None),
            P(fsdp, None),
            P(fsdp, None),
            P(None, fsdp),
            P(None, fsdp),
            P(fsdp, None),
            P(fsdp, ctx, None),
        ),
        out_specs=(
            P(fsdp, ctx, None),
            P(fsdp, ctx, None),
            P(fsdp),
            P(fsdp),
            P(fsdp, None),
            P(fsdp, None),
            P(fsdp, None),
            P(fsdp, None),
            P(None, fsdp),
            P(None, fsdp),
            P(fsdp, None),
        ),
        check_vma=False,
    )
```

```python
import functools

import jax
import jax.numpy as jnp
from jax import lax
from jax.experimental import pallas as pl
from jax.experimental.pallas import tpu as pltpu
from jax.sharding import Mesh, PartitionSpec as P

D = 1536
HEADS = 16
KV_HEADS = 8
HEAD_DIM = 96
HALF = HEAD_DIM // 2
FF = 4096
BLOCK = 64
SEQ = 4096
WINDOW_BLOCKS = 32
SHARDS = 4
ROWS = 128
TOK = SHARDS * ROWS
DS = D // SHARDS
FS = FF // SHARDS
EPS = 1e-05
ROPE_BASE = 10000.0
MASKED = -1e30
SCALE = HEAD_DIM ** (-0.5)
LOG2E = 1.4426950408889634
BF = jnp.bfloat16
F32 = jnp.float32

CHUNK_BLOCKS = 8
CHUNK = CHUNK_BLOCKS * BLOCK

SMEM_SPEC = pl.BlockSpec(memory_space=pltpu.SMEM)
VMEM_SPEC = pl.BlockSpec(memory_space=pltpu.VMEM)
ANY_SPEC = pl.BlockSpec(memory_space=pl.ANY)
PARAMS = pltpu.CompilerParams(vmem_limit_bytes=60 * 1024 * 1024)


def cost(us):
    flops, nbytes = int(us * 1_100_000_000), int(us * 3_000_000)
    return pl.CostEstimate(flops=flops, bytes_accessed=nbytes, transcendentals=0)


def call(kernel, outs, smem, vmem, us, scratch=(), deps=()):
    n, d = len(smem) + len(vmem), len(deps)

    def body(*refs):
        kernel(*refs[:n], *refs[n + d :])

    return pl.pallas_call(
        body,
        out_shape=outs,
        in_specs=[SMEM_SPEC] * len(smem) + [VMEM_SPEC] * len(vmem) + [ANY_SPEC] * d,
        out_specs=jax.tree.map(lambda _: VMEM_SPEC, outs),
        scratch_shapes=list(scratch),
        compiler_params=PARAMS,
        cost_estimate=cost(us),
    )(*smem, *vmem, *deps)


def sds(shape, dtype=BF):
    return jax.ShapeDtypeStruct(shape, dtype)


def dot(a, b):
    return jnp.dot(a, b, preferred_element_type=F32)


def dot_t(a, b):
    return lax.dot_general(a, b, (((1,), (1,)), ((), ())), preferred_element_type=F32)


def t_dot(a, b):
    return lax.dot_general(a, b, (((0,), (0,)), ((), ())), preferred_element_type=F32)


def swap_c(x):
    return lax.ppermute(x, "c", [(0, 1), (1, 0)])


def swap_xl(x):
    return lax.ppermute(x, "xl", [(0, 1), (1, 0)])


def swap_both(x):
    return lax.ppermute(x, ("xl", "c"), [(i, i ^ 3) for i in range(4)])


def swap_far(x, core):
    pairs = []
    for place in range(4):
        other = (place + 1) % 4 if place % 2 else (place + 3) % 4
        for c in range(2):
            pairs.append((place * 2 + c, other * 2 + (c ^ core)))
    return lax.ppermute(x, ("xh", "xl", "c"), pairs)


def swap_e(x):
    return lax.ppermute(x, "xh", [(0, 1), (1, 0)])


NEAR = [(0, 1), (1, 0), (2, 3), (3, 2)]
AROUND = [(1, 2), (2, 1), (0, 3), (3, 0)]
CUBE = (("y", NEAR), ("y", AROUND), ("z", NEAR), ("z", AROUND))


def swap_cube(x, dim):
    axis, pairs = CUBE[dim % 4]
    return lax.ppermute(x, axis, pairs)


def from_z(x, m):
    return lax.ppermute(x, "z", [((i + m) % 4, i) for i in range(4)])


def to_z(x, m):
    return lax.ppermute(x, "z", [(i, (i + m) % 4) for i in range(4)])


def gather_slots(own):
    far = swap_xl(own)
    return own, swap_c(own), far, swap_c(far)


def scatter_slots(keep, send):
    got = swap_c(send)
    other = (keep[1].astype(F32) + got[1].astype(F32)).astype(BF)
    return (keep, got, swap_xl(other)), other


CTX = ("y", "xh", "z")
FSDP = ("xl", "c")


def after(x, other):
    return lax.optimization_barrier((x, other))[0]


def shifts(x, axis):
    return [lax.ppermute(x, axis, [((i + m) % 4, i) for i in range(4)]) for m in (1, 2, 3)]


def exchange(x, axes):
    return lax.all_to_all(x, axes, 0, 0, tiled=True)


def cube_index(portion, bits):
    out = 0
    for t in range(4):
        out = out * 2 + bits[(portion + t) % 4]
    return out


def fold(x):
    tail = jnp.concatenate([x[0:64, 128:192], x[64:128, 128:192]], axis=1)
    return jnp.concatenate([x[:, 0:128], tail], axis=0)


def unfold(x):
    tail = jnp.concatenate([x[128:192, 0:64], x[128:192, 64:128]], axis=0)
    return jnp.concatenate([x[0:128], tail], axis=1)


def pack_kernel(sc, wq, wk, wv, gains, q0, q1, q2, q3, k0, k1, k2, k3, tmp):
    f = sc[0]
    for g in range(4):
        tmp[g, :, 0:192] = wk[:, 192 * g : 192 * (g + 1)]
        tmp[g, :, 192:384] = wv[:, 192 * g : 192 * (g + 1)]
    for k, (q, kv) in enumerate(((q0, k0), (q1, k1), (q2, k2), (q3, k3))):
        q[...] = wq[:, pl.ds(pl.multiple_of((f ^ k) * DS, 128), DS)]
        kv[0:DS] = tmp[f ^ k]
        kv[DS:] = gains[...]


def project(f, xa, ws):
    total = jnp.zeros((TOK, DS), F32)
    for k, w in enumerate(ws):
        at = pl.multiple_of((f ^ k) * DS, 128)
        total = total + dot(xa[:, pl.ds(at, DS)], w[0:DS])
    return total


def rotate(u, co, si):
    turned = jnp.concatenate([-u[:, HALF:], u[:, :HALF]], axis=1)
    return u * co + turned * si


def kv_kernel(sc, x0, x1, x2, x3, k0, k1, k2, k3, cos, sin, xa, kv, gain_a, gain_m):
    f = sc[0]
    for k, w in enumerate((k0, k1, k2, k3)):
        at = pl.ds(pl.multiple_of((f ^ k) * DS, 128), DS)
        rows = w[DS:].astype(F32)
        gain_a[:, at] = rows[0:1]
        gain_m[:, at] = rows[1:2]
    for k, x in enumerate((x0, x1, x2, x3)):
        u = x[...].astype(F32)
        r = lax.rsqrt(jnp.mean(u * u, axis=-1, keepdims=True) + EPS)
        xa[ROWS * k : ROWS * (k + 1), :] = (u * r * gain_a[...]).astype(BF)
    lin = project(f, xa, [w[0:DS] for w in (k0, k1, k2, k3)])
    co, si = cos[...], sin[...]
    for k in range(4):
        part = lin[ROWS * k : ROWS * (k + 1)]
        for j in range(2):
            key = rotate(part[:, 96 * j : 96 * (j + 1)], co, si)
            value = part[:, 192 + 96 * j : 192 + 96 * (j + 1)]
            kv[2 * k + j] = fold(jnp.concatenate([key, value], axis=1)).astype(BF)


def q_kernel(sc, xa, w0, w1, w2, w3, cos, sin, q):
    lin = project(sc[0], xa, (w0, w1, w2, w3))
    co, si = cos[...], sin[...]
    for k in range(4):
        part = lin[ROWS * k : ROWS * (k + 1)]
        heads = [rotate(part[:, 96 * h : 96 * (h + 1)], co, si) for h in range(4)]
        for j in range(2):
            q[2 * k + j] = fold(jnp.concatenate(heads[2 * j : 2 * j + 2], axis=1)).astype(BF)


def widen(x, *tail):
    zeros = jnp.zeros((x.shape[0], 128 - x.shape[1] - len(tail)), x.dtype)
    return jnp.concatenate([x, *tail, zeros], axis=1)


def stacked(x, t):
    rows = slice(BLOCK * t, BLOCK * (t + 1))
    return jnp.concatenate([x[rows, 0:96], x[rows, 96:192]], axis=0)


def side_by_side(a, b):
    rows = [jnp.concatenate([x[0:BLOCK, 0:96], x[BLOCK:, 0:96]], axis=1) for x in (a, b)]
    return fold(jnp.concatenate(rows, axis=0))


def low_high(qb, n):
    swapped = (qb[2 * n] >= WINDOW_BLOCKS).astype(jnp.int32)
    return 2 * n + swapped, 2 * n + 1 - swapped


def attention_kernel(qb, kb, q, kv0, kv1, kv2, kv3, o, o2, q2, lse, kv):
    ones = (lax.broadcasted_iota(jnp.int32, (BLOCK, 32), 1) < 4).astype(F32)

    def place(s, _):
        for m, ref in enumerate((kv0, kv1, kv2, kv3)):
            x = unfold(ref[s].astype(F32))
            for t in range(2):
                dst = pl.ds(pl.multiple_of(kb[m * 16 + 2 * s + t] * BLOCK, BLOCK), BLOCK)
                part = x[BLOCK * t : BLOCK * (t + 1)]
                both = jnp.concatenate([part[:, 0:96], ones, part[:, 96:192], ones], axis=1)
                kv[dst, :] = both.astype(BF)
        x = unfold(q[s].astype(F32))
        for t in range(2):
            q2[2 * s + t] = widen(stacked(x, t)).astype(BF)
        return 0

    lax.fori_loop(0, 8, place, 0)
    two = SCALE * LOG2E

    def scores(n, spans):
        return [dot_t(q2[n], kv[span, 0:128]) for span in spans]

    def finish(n, parts, spans):
        tops = [jnp.max(s, axis=1, keepdims=True) for s in parts]
        top = functools.reduce(jnp.maximum, tops) * two
        acc = jnp.zeros((ROWS, 128), F32)
        for s, span in zip(parts, spans):
            acc += dot(jnp.exp2(s * two - top).astype(BF), kv[span, 128:256])
        total = acc[:, 96:97]
        o2[n] = (acc / total).astype(BF)
        lse[n] = jnp.broadcast_to(top + jnp.log2(total), (ROWS, 8))

    def pair(n, _):
        low, high = low_high(qb, n)
        i_low, i_high = qb[low], qb[high]
        for count in range(1, 5):

            @pl.when(i_low // CHUNK_BLOCKS == count - 1)
            def _():
                edge = pl.ds(pl.multiple_of((i_high - WINDOW_BLOCKS) * BLOCK, BLOCK), BLOCK)
                at = pl.multiple_of((i_high - WINDOW_BLOCKS + 1) * BLOCK, BLOCK)
                spans_h = [edge] + [pl.ds(at + CHUNK * t, CHUNK) for t in range(4)]
                spans_l = [pl.ds(CHUNK * t, CHUNK) for t in range(count)]
                high_s = scores(high, spans_h)
                low_s = scores(low, spans_l)
                key = lax.broadcasted_iota(jnp.int32, (ROWS, BLOCK), 1)
                query = lax.broadcasted_iota(jnp.int32, (ROWS, BLOCK), 0) % BLOCK
                high_s[0] = jnp.where(key > query, high_s[0], MASKED)
                key = lax.broadcasted_iota(jnp.int32, (ROWS, CHUNK), 1)
                limit = (i_low + 1) * BLOCK - CHUNK * (count - 1)
                low_s[-1] = jnp.where(key < limit, low_s[-1], MASKED)
                finish(high, high_s, spans_h)
                finish(low, low_s, spans_l)

        return 0

    lax.fori_loop(0, 8, pair, 0)

    def gather(s, _):
        o[s] = side_by_side(o2[2 * s].astype(F32), o2[2 * s + 1].astype(F32)).astype(BF)
        return 0

    lax.fori_loop(0, 8, gather, 0)


def attention_back_kernel(qb, kb, q2s, d_o, o2s, lse, kv, dq2s, g, dkv, do2s):
    dkv[...] = jnp.zeros_like(dkv)

    def place(s, _):
        x = unfold(d_o[s].astype(F32))
        for t in range(2):
            do2s[2 * s + t] = stacked(x, t).astype(BF)
        return 0

    lax.fori_loop(0, 8, place, 0)
    two = SCALE * LOG2E

    def split(x):
        parts = []
        for _ in range(3):
            parts.append(x.astype(BF))
            x = x - parts[-1].astype(F32)
        return parts

    def weights(n):
        do2 = do2s[n]
        inner = do2.astype(F32) * o2s[n][:, 0:96].astype(F32)
        inner = jnp.sum(inner, axis=1, keepdims=True)
        q2 = widen(q2s[n][:, 0:96], *split(lse[n][:, 0:1] * (-1.0 / two)))
        do2 = widen(do2, *split(-inner))
        none = jnp.zeros((ROWS, 128), BF)
        return jnp.concatenate(
            [jnp.concatenate([q2, none], axis=1), jnp.concatenate([none, do2], axis=1)], axis=0
        )

    def factors(w, spans, masks):
        pairs = []
        for span, mask in zip(spans, masks):
            s = dot_t(kv[span, :], w)
            p = jnp.exp2(s[:, 0:128] * two)
            if mask is not None:
                p = jnp.where(mask, p, 0.0)
            ds = (p * s[:, 128:256]).astype(BF)
            pairs.append(jnp.concatenate([ds, p.astype(BF)], axis=1))
        return pairs

    def add(n, w, spans, pairs):
        acc = jnp.zeros((ROWS, 128), F32)
        for span, both in zip(spans, pairs):
            dkv[span, :] += dot(both, w)
            acc += t_dot(both[:, 0:128], kv[span, 0:128])
        dq2s[n] = (acc * SCALE).astype(BF)

    def pair(n, _):
        low, high = low_high(qb, n)
        i_low, i_high = qb[low], qb[high]
        for count in range(1, 5):

            @pl.when(i_low // CHUNK_BLOCKS == count - 1)
            def _():
                edge = pl.ds(pl.multiple_of((i_high - WINDOW_BLOCKS) * BLOCK, BLOCK), BLOCK)
                at = pl.multiple_of((i_high - WINDOW_BLOCKS + 1) * BLOCK, BLOCK)
                key = lax.broadcasted_iota(jnp.int32, (BLOCK, ROWS), 0)
                query = lax.broadcasted_iota(jnp.int32, (BLOCK, ROWS), 1) % BLOCK
                spans_h = [edge] + [pl.ds(at + CHUNK * t, CHUNK) for t in range(4)]
                masks_h = [key > query] + [None] * 4
                spans_l = [pl.ds(CHUNK * t, CHUNK) for t in range(count)]
                key = lax.broadcasted_iota(jnp.int32, (CHUNK, ROWS), 0)
                limit = (i_low + 1) * BLOCK - CHUNK * (count - 1)
                masks_l = [None] * (count - 1) + [key < limit]
                w_h, w_l = weights(high), weights(low)
                pairs_h = factors(w_h, spans_h, masks_h)
                pairs_l = factors(w_l, spans_l, masks_l)
                add(high, w_h, spans_h, pairs_h)
                add(low, w_l, spans_l, pairs_l)

        return 0

    lax.fori_loop(0, 8, pair, 0)

    def keys(s, _):
        parts = []
        for t in range(2):
            src = pl.ds(pl.multiple_of(kb[2 * s + t] * BLOCK, BLOCK), BLOCK)
            both = dkv[src, :]
            parts.append(jnp.concatenate([both[:, 0:96] * SCALE, both[:, 128:224]], axis=1))
        g[s] = fold(jnp.concatenate(parts, axis=0)).astype(BF)
        return 0

    lax.fori_loop(0, 32, keys, 0)


def fold_dq_kernel(dq2s, dq):
    for s in range(8):
        dq[s] = side_by_side(dq2s[2 * s].astype(F32), dq2s[2 * s + 1].astype(F32)).astype(BF)


def unfolded(o):
    return unfold(o.astype(F32)).astype(BF)


def out_kernel(o, w, keep, send):
    for k in range(4):
        total = dot(unfolded(o[2 * k]), w[0:192, :]) + dot(unfolded(o[2 * k + 1]), w[192:384, :])
        (keep, send)[k % 2][k // 2] = total.astype(BF)


def hidden_kernel(x, keep, got, far, gain, hidden, xm):
    h = x[...].astype(F32) + keep[0].astype(F32) + got[0].astype(F32) + far[...].astype(F32)
    hidden[...] = h
    r = lax.rsqrt(jnp.mean(h * h, axis=-1, keepdims=True) + EPS)
    xm[...] = (h * r * gain[...]).astype(BF)


def norm_back(values, gain, grads):
    factor = lax.rsqrt(jnp.mean(values * values, axis=-1, keepdims=True) + EPS)
    weighted = grads * gain
    inner = jnp.mean(weighted * values, axis=-1, keepdims=True)
    return factor * weighted - values * (factor * factor * factor) * inner


def d_hidden_kernel(dy, keep, got, far, hidden, gain, d_hidden, d_br, d_gain):
    grads = keep[0].astype(F32) + got[0].astype(F32) + far[...].astype(F32)
    h = hidden[...]
    d = dy[...].astype(F32) + norm_back(h, gain[...], grads)
    d_hidden[...] = d
    d_br[...] = d.astype(BF)
    r = lax.rsqrt(jnp.mean(h * h, axis=-1, keepdims=True) + EPS)
    total = jnp.sum(grads * h * r, axis=0, keepdims=True)
    rows = [total[:, 128 * t : 128 * (t + 1)] for t in range(12)]
    d_gain[...] = jnp.concatenate(rows + [jnp.zeros((4, 128), F32)], axis=0).astype(BF)


def d_tokens_kernel(x, keep, got, far, d_hidden, gain, d_tokens):
    grads = keep[0].astype(F32) + got[0].astype(F32) + far[...].astype(F32)
    d_tokens[...] = d_hidden[...] + norm_back(x[...].astype(F32), gain[...], grads)


def layer_out_kernel(hidden, keep, got, far, out):
    total = keep[0].astype(F32) + got[0].astype(F32) + far[...].astype(F32)
    out[...] = (hidden[...] + total).astype(BF)


def d_o_kernel(b0, b1, b2, b3, w, d_o):
    for k, b in enumerate((b0, b1, b2, b3)):
        d = dot_t(b[...], w[...])
        d_o[2 * k] = fold(d[:, 0:192]).astype(BF)
        d_o[2 * k + 1] = fold(d[:, 192:384]).astype(BF)


FBLOCK = 512


def d_act_kernel(y0, y1, y2, y3, wd, da):
    ys = jnp.concatenate([y0[...], y1[...], y2[...], y3[...]], axis=0)
    da[...] = dot_t(ys, wd[...])


def ffn_kernel(sc, x0, x1, x2, x3, da, wg, wu, act, dg, du, keep, send, xs, acc):
    n = pl.program_id(0)

    @pl.when(n == 0)
    def _():
        for k, x in enumerate((x0, x1, x2, x3)):
            xs[ROWS * k : ROWS * (k + 1), :] = x[...]

    gate = dot(xs[...], wg[...])
    up = dot(xs[...], wu[...])
    d = da[...]
    sg = jax.nn.sigmoid(gate)
    both = gate * sg
    a = (both * up).astype(BF)
    d_gate = (d * up * sg * (1.0 + gate * (1.0 - sg))).astype(BF)
    d_up = (d * both).astype(BF)
    for h in range(2):
        at = pl.multiple_of((h ^ (sc[2] & 1)) * 256, 256)
        for ref, tile in ((act, a), (dg, d_gate), (du, d_up)):
            ref[:, pl.ds(at, 256)] = tile[:, 256 * h : 256 * (h + 1)]
    dx = dot_t(d_gate, wg[...]) + dot_t(d_up, wu[...])

    @pl.when(n == 0)
    def _():
        acc[...] = dx

    @pl.when(n > 0)
    def _():
        total = acc[...] + dx
        for k in range(4):
            (keep, send)[k % 2][k // 2] = total[ROWS * k : ROWS * (k + 1), :].astype(BF)


def ffn(sc, xs, da, wg, wu):
    full = pl.BlockSpec((ROWS, D), lambda n, s: (0, 0))
    side = pl.BlockSpec((2, ROWS, D), lambda n, s: (0, 0, 0))
    cols = pl.BlockSpec((D, FBLOCK), lambda n, s: (0, n))
    rel = pl.BlockSpec((TOK, FBLOCK), lambda n, s: (0, n ^ (s[2] >> 1)))
    return pl.pallas_call(
        ffn_kernel,
        grid_spec=pltpu.PrefetchScalarGridSpec(
            num_scalar_prefetch=1,
            grid=(FS // FBLOCK,),
            in_specs=[full] * 4 + [pl.BlockSpec((TOK, FBLOCK), lambda n, s: (0, n)), cols, cols],
            out_specs=[rel, rel, rel, side, side],
            scratch_shapes=[pltpu.VMEM((TOK, D), BF), pltpu.VMEM((TOK, D), F32)],
        ),
        out_shape=[sds((TOK, FS))] * 3 + [sds((2, ROWS, D))] * 2,
        compiler_params=PARAMS,
        cost_estimate=cost(11),
    )(sc, *xs, da, wg, wu)


def mlp_out_kernel(sc, act, wd, keep, send):
    gz = sc[2]
    acts = [
        act[:, pl.ds(pl.multiple_of((b ^ gz) * 256, 256), 256)] for b in range(FS // 256)
    ]
    total = dot(jnp.concatenate(acts, axis=1), wd[...])
    for k in range(4):
        (keep, send)[k % 2][k // 2] = total[ROWS * k : ROWS * (k + 1)].astype(BF)


def ffn_grads_kernel(sc, x0, x1, x2, x3, y0, y1, y2, y3, act, dg, du, *refs):
    gy = sc[1]
    keeps, sends, ys = refs[:4], refs[4:8], refs[8]

    def put(p, ra, rb, at, tile):
        index = cube_index(p, (ra & 1, ra >> 1, rb & 1, rb >> 1))
        ref = (keeps, sends)[index >> 3][p]
        ref[index & 7, at : at + tile.shape[0], :] = tile.astype(BF)

    for ra in range(4):
        cols = pl.ds(pl.multiple_of((ra ^ gy) * DS, 128), DS)
        xa = jnp.concatenate([x[:, cols] for x in (x0, x1, x2, x3)], axis=0)
        for k, y in enumerate((y0, y1, y2, y3)):
            ys[ROWS * k : ROWS * (k + 1), DS * ra : DS * (ra + 1)] = y[:, cols]
        for n, d in enumerate((dg, du)):
            wide = t_dot(xa, d[...])
            for rb in range(4):
                for p in range(4):
                    lane, row = 256 * rb + 128 * (p // 2), 192 * (p % 2)
                    put(p, ra, rb, 192 * n, wide[row : row + 192, lane : lane + 128])
    for rb in range(4):
        wide = t_dot(act[:, 256 * rb : 256 * (rb + 1)], ys[...])
        for ra in range(4):
            for p in range(4):
                at = 384
                row = 192 * p
                while row < 192 * (p + 1):
                    lane, r = DS * ra + 128 * (row // 256), row % 256
                    size = min(256 - r, 192 * (p + 1) - row)
                    put(p, ra, rb, at, wide[r : r + size, lane : lane + 128])
                    at += size
                    row += size


OUT_ROWS = 288
OUT_SPLIT = (80, 80, 64, 64)
OUT_AT = (0, 80, 160, 224)
PART_ROWS = tuple(576 + n for n in OUT_SPLIT)
PART_AT = (0, 656, 1312, 1952)
GAIN_AT = 2592


def step_kernel(*refs):
    for p in range(4):
        kl, ku, gl, gu = refs[4 * p : 4 * p + 4]
        keep, send = refs[16 + 2 * p : 18 + 2 * p]
        keep[...] = (kl[...].astype(F32) + gl[...].astype(F32)).astype(BF)
        send[...] = (ku[...].astype(F32) + gu[...].astype(F32)).astype(BF)


def cube_step(keeps, gots, deps, us):
    half = keeps[0].shape[0] // 2
    lower = pl.BlockSpec((1, 576, 128), lambda n: (n, 0, 0))
    upper = pl.BlockSpec((1, 576, 128), lambda n: (n + half, 0, 0))

    def body(*refs):
        step_kernel(*refs[:16], *refs[16 + len(deps) :])

    args = []
    for k, g in zip(keeps, gots):
        args += [k, k, g, g]
    outs = pl.pallas_call(
        body,
        grid=(half,),
        in_specs=[lower, upper] * 8 + [ANY_SPEC] * len(deps),
        out_specs=[lower] * 8,
        out_shape=[sds((half, 576, 128))] * 8,
        compiler_params=PARAMS,
        cost_estimate=cost(us),
    )(*args, *deps)
    return outs[0::2], outs[1::2]


def last_step_kernel(k0, k1, k2, k3, g0, g1, g2, g3, out, total):
    for p, (k, g) in enumerate(((k0, g0), (k1, g1), (k2, g2), (k3, g3))):
        at = PART_AT[p]
        total[at : at + 576, :] = (k[0].astype(F32) + g[0].astype(F32)).astype(BF)
        total[at + 576 : at + PART_ROWS[p], :] = out[OUT_AT[p] : OUT_AT[p] + OUT_SPLIT[p]]
    total[GAIN_AT:, :] = out[OUT_ROWS:]


def join_kernel(own, got, p0, p1, p2, p3, gains):
    total = own[...].astype(F32) + got[...].astype(F32)
    for p, ref in enumerate((p0, p1, p2, p3)):
        ref[0] = total[PART_AT[p] : PART_AT[p] + PART_ROWS[p]].astype(BF)
    gains[...] = total[GAIN_AT:]


def stack_kernel(a0, a1, a2, a3, b0, b1, b2, b3, o0, o1, o2, o3):
    for a, b, o in ((a0, b0, o0), (a1, b1, o1), (a2, b2, o2), (a3, b3, o3)):
        o[0 : a.shape[0]] = a[...]
        o[a.shape[0] :] = b[...]


def cube_gather(owns, gots, us, deps):
    outs = [sds((2 * o.shape[0], *o.shape[1:])) for o in owns]
    return call(stack_kernel, outs, [], [*owns, *gots], us, deps=deps)


def pick(owns, gots, p, bits, rows):
    index = cube_index(p, bits)
    rest = index & 7
    return jnp.where(index >= 8, gots[p][rest, rows, :], owns[p][rest, rows, :])


def ffn_place_kernel(sc, *refs):
    owns, gots = refs[0:4], refs[4:8]
    gate, up, down, out, tmp = refs[8:]
    gy, gz = sc[1], sc[2]
    ra = pl.program_id(0) ^ gy
    for bb in range(4):
        rb = bb ^ gz
        bits = (ra & 1, ra >> 1, rb & 1, rb >> 1)
        for p in range(4):
            lane, row = 256 * bb + 128 * (p // 2), 192 * (p % 2)
            for n, ref in enumerate((gate, up)):
                tile = pick(owns, gots, p, bits, slice(192 * n, 192 * (n + 1)))
                ref[row : row + 192, lane : lane + 128] = tile.astype(F32)
            at, row = 384, 192 * p
            while row < 192 * (p + 1):
                lane, r = row // 256, row % 256
                size = min(256 - r, 192 * (p + 1) - row)
                tile = pick(owns, gots, p, bits, slice(at, at + size))
                down[256 * bb + r : 256 * bb + r + size, 128 * lane : 128 * (lane + 1)] = (
                    tile.astype(F32)
                )
                at += size
                row += size
            at = OUT_ROWS * (bb ^ (bb >> 1)) + OUT_AT[p]
            tile = pick(owns, gots, p, bits, slice(576, PART_ROWS[p]))
            tmp[at : at + OUT_SPLIT[p], :] = tile.astype(F32)
    for t in range(3):
        out[:, 128 * t : 128 * (t + 1)] = tmp[DS * t : DS * (t + 1), :]


def ffn_place(sc, owns, gots, deps):
    def body(*refs):
        ffn_place_kernel(*refs[:9], *refs[9 + len(deps) :])

    whole = [pl.BlockSpec((8, n, 128), lambda n, s: (0, 0, 0)) for n in PART_ROWS]
    rows = pl.BlockSpec((DS, FS), lambda n, s: (n, 0))
    return pl.pallas_call(
        body,
        grid_spec=pltpu.PrefetchScalarGridSpec(
            num_scalar_prefetch=1,
            grid=(4,),
            in_specs=whole * 2 + [ANY_SPEC] * len(deps),
            out_specs=[
                rows,
                rows,
                pl.BlockSpec((FS, DS), lambda n, s: (0, n)),
                pl.BlockSpec((DS, DS), lambda n, s: (0, n ^ (n >> 1))),
            ],
            scratch_shapes=[pltpu.VMEM((4 * OUT_ROWS, 128), F32)],
        ),
        out_shape=[sds((D, FS), F32), sds((D, FS), F32), sds((FS, D), F32), sds((DS, D), F32)],
        compiler_params=PARAMS,
        cost_estimate=cost(12),
    )(sc, *owns, *gots, *deps)


def out_grads_kernel(o, b0, b1, b2, b3, d_gain, pieces, tmp):
    bs = jnp.concatenate([b0[...], b1[...], b2[...], b3[...]], axis=0)
    for j in range(2):
        oj = jnp.concatenate([unfolded(o[2 * k + j]) for k in range(4)], axis=0)
        tmp[192 * j : 192 * (j + 1), :] = t_dot(oj, bs)
    for s in range(16):
        pieces[s, OUT_ROWS:, :] = d_gain[...]
        start, at = OUT_ROWS * s, 0
        while start < OUT_ROWS * (s + 1):
            lane, r = 128 * (start // DS), start % DS
            size = min(DS - r, OUT_ROWS * (s + 1) - start)
            pieces[s, at : at + size, :] = tmp[r : r + size, lane : lane + 128].astype(BF)
            at += size
            start += size


def sum_kernel(parts, out):
    out[...] = jnp.sum(parts[...].astype(F32), axis=0).astype(BF)


def repeat_kernel(part, out):
    for n in range(32):
        out[n] = part[...]


QKV_ROWS = 72
QKV_PAD = 80


def d_xa_kernel(sc, d_q, d_kv, q0, q1, q2, q3, k0, k1, k2, k3, cos, sin, lin, keep, send, dq, dkv):
    f = sc[0]
    co, si = cos[...], sin[...]

    def back(g):
        w = g * si
        turned = jnp.concatenate([w[:, HALF:], -w[:, :HALF]], axis=1)
        return (g * co + turned).astype(BF)

    for k in range(4):
        rows = slice(ROWS * k, ROWS * (k + 1))
        for j in range(2):
            i = 2 * k + j
            gq = unfold(d_q[i].astype(F32))
            gkv = d_kv[4 * i].astype(F32)
            for z in range(1, 4):
                gkv += d_kv[4 * i + z].astype(F32)
            gkv = unfold(gkv)
            for n in range(2):
                g = back(gq[:, 96 * n : 96 * (n + 1)])
                lin[rows, 384 * j + 96 * n : 384 * j + 96 * (n + 1)] = g
                dq[rows, 192 * j + 96 * n : 192 * j + 96 * (n + 1)] = g
            g = back(gkv[:, 0:96])
            lin[rows, 384 * j + 192 : 384 * j + 288] = g
            dkv[rows, 96 * j : 96 * (j + 1)] = g
            g = gkv[:, 96:192].astype(BF)
            lin[rows, 384 * j + 288 : 384 * j + 384] = g
            dkv[rows, 192 + 96 * j : 192 + 96 * (j + 1)] = g
    for k, (wq, wkv) in enumerate(((q0, k0), (q1, k1), (q2, k2), (q3, k3))):
        cols = pl.ds(pl.multiple_of((f ^ k) * DS, 128), DS)
        total = (dot_t(dq[...], wq[...]) + dot_t(dkv[...], wkv[0:DS])).astype(BF)
        for s in range(4):
            (keep, send)[s % 2][s // 2, :, cols] = total[ROWS * s : ROWS * (s + 1)]


def flat_pieces(n):
    out, start = [], QKV_ROWS * n
    while start < QKV_ROWS * (n + 1):
        r = start % DS
        size = min(DS - r, QKV_ROWS * (n + 1) - start)
        out.append((128 * (start // DS), r, size))
        start += size
    return out


def qkv_grads_kernel(xa, lin, pieces, tmp):
    zeros = jnp.zeros((QKV_PAD - QKV_ROWS, 128), F32)
    for g in range(4):
        tmp[...] = t_dot(xa[:, DS * g : DS * (g + 1)], lin[...])
        for n in range(32):
            tiles = [tmp[r : r + size, lane : lane + 128] for lane, r, size in flat_pieces(n)]
            pieces[n, g] = jnp.concatenate(tiles + [zeros], axis=0).astype(BF)


def attn_place_kernel(got, wq, wk, wv, gain_in, q, k, v, gain, tmp):
    for g in range(4):
        for n in range(32):
            tile, at = got[n, g].astype(F32), 0
            for lane, r, size in flat_pieces(n):
                tmp[r : r + size, lane : lane + 128] = tile[at : at + size]
                at += size
        for j in range(2):
            at = 384 * j
            q[:, 384 * g + 192 * j : 384 * g + 192 * (j + 1)] = tmp[:, at : at + 192]
            k[:, 192 * g + 96 * j : 192 * g + 96 * (j + 1)] = tmp[:, at + 192 : at + 288]
            v[:, 192 * g + 96 * j : 192 * g + 96 * (j + 1)] = tmp[:, at + 288 : at + 384]
    total = jnp.sum(wq[...].astype(F32) * q[...], axis=1, keepdims=True)
    total += jnp.sum(wk[...].astype(F32) * k[...], axis=1, keepdims=True)
    total += jnp.sum(wv[...].astype(F32) * v[...], axis=1, keepdims=True)
    gain[...] = total / gain_in[...]


def rope_tables(positions):
    freqs = ROPE_BASE ** (-jnp.arange(HALF).astype(F32) * 2.0 / HEAD_DIM)
    angles = positions.astype(F32)[:, None] * freqs[None, :]
    angles = jnp.concatenate([angles, angles], axis=1)
    return jnp.cos(angles), jnp.sin(angles)


def body(
    tokens,
    block_order,
    gain_attn,
    gain_mlp,
    w_query,
    w_key,
    w_value,
    w_out,
    w_gate,
    w_up,
    w_down,
    cotangent,
):
    y, xh, z = lax.axis_index("y"), lax.axis_index("xh"), lax.axis_index("z")
    xl, c = lax.axis_index("xl"), lax.axis_index("c")
    f = xl * 2 + c
    gy, gz = y ^ (y >> 1), z ^ (z >> 1)
    sc = jnp.stack([f, gy, gz]).astype(jnp.int32)
    own_x, own_dy = tokens[0], cotangent[0]

    place = (y * 2 + xh) * 4 + z
    own_blocks = lax.dynamic_slice_in_dim(block_order, 2 * place, 2)
    positions = (own_blocks[:, None] * BLOCK + jnp.arange(BLOCK)).reshape(-1)
    cos, sin = rope_tables(positions)
    blocks = block_order.reshape(8, 4, 2)
    key_blocks = jnp.stack(
        [
            lax.dynamic_index_in_dim(blocks, (z + m) % 4, axis=1, keepdims=False).reshape(-1)
            for m in range(4)
        ]
    ).reshape(-1)
    query_blocks = key_blocks[:16]

    xs = gather_slots(own_x)
    packs = call(
        pack_kernel,
        [sds((DS, DS))] * 4 + [sds((DS + 16, DS))] * 4,
        [sc],
        [w_query, w_key, w_value, jnp.pad(jnp.stack([gain_attn, gain_mlp]), ((0, 14), (0, 0)))],
        3,
        [pltpu.VMEM((4, DS, DS), BF)],
    )
    wkvs = (packs[4], swap_c(packs[5]), swap_xl(packs[6]), swap_far(packs[7], 1))
    wqs = (packs[0], swap_c(packs[1]), swap_far(packs[2], 0), swap_far(packs[3], 1))

    folded, heads = (8, 192, 128), ("y", "xh")
    xa, kv, gain_a, gain_m = call(
        kv_kernel,
        [sds((TOK, D)), sds(folded), sds((1, D), F32), sds((1, D), F32)],
        [sc],
        [*xs, *wkvs, cos, sin],
        5,
    )
    q = call(q_kernel, sds(folded), [sc], [xa, *wqs, cos, sin], 4)
    kv = exchange(kv, heads)
    kvs = shifts(kv, "z")
    q = exchange(q, heads)
    o, o2, q2, lse, kv_sorted = call(
        attention_kernel,
        [
            sds(folded),
            sds((16, ROWS, 128)),
            sds((16, ROWS, 128)),
            sds((16, ROWS, 8), F32),
            sds((SEQ, 256)),
        ],
        [query_blocks, key_blocks],
        [q, kv, *kvs],
        13,
    )
    o_tok = exchange(o, heads)

    dys = gather_slots(own_dy)
    d_act = call(d_act_kernel, sds((TOK, FS), F32), [], [*dys, w_down], 4, deps=[o])
    side = [sds((2, ROWS, D))] * 2
    keep, send = call(out_kernel, side, [], [o_tok, w_out], 2, deps=[d_act])
    terms, _ = scatter_slots(keep, send)
    hidden, xm = call(
        hidden_kernel, [sds((ROWS, D), F32), sds((ROWS, D))], [], [own_x, *terms, gain_m], 2
    )
    xms = gather_slots(xm)
    act, dg, du, keep, send = ffn(sc, xms, d_act, w_gate, w_up)
    terms, moving = scatter_slots(keep, send)

    grads = call(
        ffn_grads_kernel,
        [sds((8, 576, 128))] * 8,
        [sc],
        [*xms, *dys, act, dg, du],
        9,
        [pltpu.VMEM((TOK, D), BF)],
        [moving],
    )
    keeps, sends = grads[:4], grads[4:]
    gots = [swap_cube(s, p) for p, s in enumerate(sends)]
    d_hidden, d_br, d_gain = call(
        d_hidden_kernel,
        [sds((ROWS, D), F32), sds((ROWS, D)), sds((16, 128))],
        [],
        [own_dy, *terms, hidden, gain_m],
        2,
        deps=[sends[0]],
    )
    d_brs = gather_slots(d_br)
    d_o = call(d_o_kernel, sds(folded), [], [*d_brs, w_out], 2)
    d_o_att = exchange(d_o, heads)
    out_pieces = call(
        out_grads_kernel,
        sds((16, OUT_ROWS + 16, 128)),
        [],
        [o_tok, *d_brs, d_gain],
        2,
        [pltpu.VMEM((DS, D), F32)],
        [d_o],
    )
    keeps, sends = cube_step(keeps, gots, [out_pieces], 5)
    gots = [swap_cube(s, p + 1) for p, s in enumerate(sends)]
    out_got = exchange(out_pieces, ("y", "z"))
    dq2, dkv = call(
        attention_back_kernel,
        [sds((16, ROWS, 128)), sds((32, 192, 128))],
        [query_blocks, block_order],
        [q2, d_o_att, o2, lse, kv_sorted],
        24,
        [pltpu.VMEM((SEQ, 256), F32), pltpu.VMEM((16, ROWS, 96), BF)],
        [sends[0]],
    )
    dkv_tok = exchange(dkv, CTX)
    keeps, sends = cube_step(keeps, gots, [dq2], 4)
    gots = [swap_cube(s, p + 2) for p, s in enumerate(sends)]
    out_sum = call(
        sum_kernel, sds((OUT_ROWS + 16, 128)), [], [out_got], 2, deps=[sends[0]]
    )
    keeps, sends = cube_step(keeps, gots, [out_sum], 3)
    gots = [swap_cube(s, p + 3) for p, s in enumerate(sends)]
    dq = call(fold_dq_kernel, sds(folded), [], [dq2], 2, deps=[sends[0], dkv_tok])
    dq_tok = exchange(dq, heads)
    keep, send = call(mlp_out_kernel, side, [sc], [act, w_down], 5, deps=[dq])
    mlp_terms, _ = scatter_slots(keep, send)
    total = call(
        last_step_kernel, sds((GAIN_AT + 16, 128)), [], [*keeps, *gots, out_sum], 2, deps=[keep]
    )
    total_got = swap_e(total)

    lin, keep, send = call(
        d_xa_kernel,
        [sds((TOK, 768)), *side],
        [sc],
        [dq_tok, dkv_tok, *wqs, *wkvs, cos, sin],
        7,
        [pltpu.VMEM((TOK, DS), BF), pltpu.VMEM((TOK, DS), BF)],
        [total],
    )
    *owns, gains_sum = call(
        join_kernel,
        [sds((1, n, 128)) for n in PART_ROWS] + [sds((16, 128), F32)],
        [],
        [total, total_got],
        2,
        deps=[lin],
    )
    gots = [swap_cube(o, p + 3) for p, o in enumerate(owns)]
    terms, moving = scatter_slots(keep, send)
    pieces = call(
        qkv_grads_kernel,
        sds((32, 4, QKV_PAD, 128)),
        [],
        [xa, lin],
        5,
        [pltpu.VMEM((DS, 768), F32)],
        [owns[0]],
    )
    pieces_got = exchange(pieces, CTX)
    owns = cube_gather(owns, gots, 2, [pieces])
    gots = [swap_cube(o, p + 2) for p, o in enumerate(owns)]
    layer_out = call(
        layer_out_kernel, sds((ROWS, D)), [], [hidden, *mlp_terms], 2, deps=[owns[0]]
    )
    d_tokens = call(
        d_tokens_kernel,
        sds((ROWS, D), F32),
        [],
        [own_x, *terms, d_hidden, gain_a],
        2,
        deps=[layer_out],
    )
    owns = cube_gather(owns, gots, 3, [d_tokens])
    gots = [swap_cube(o, p + 1) for p, o in enumerate(owns)]

    part = call(sum_kernel, sds((4, QKV_PAD, 128)), [], [pieces_got], 3, deps=[owns[0]])
    owns = cube_gather(owns, gots, 5, [part])
    gots = [swap_cube(o, p) for p, o in enumerate(owns)]
    part = exchange(part, FSDP)
    parts = call(repeat_kernel, sds((32, 4, QKV_PAD, 128)), [], [part], 3, deps=[owns[0]])
    parts = exchange(parts, CTX)
    g_gain_m = gains_sum[0:12].reshape(4, DS)
    g_gain_m = [lax.dynamic_index_in_dim(g_gain_m, f ^ k, keepdims=False) for k in range(4)]
    g_gain_m = g_gain_m[0] + swap_c(g_gain_m[1]) + swap_xl(g_gain_m[2]) + swap_both(g_gain_m[3])
    g_query, g_key, g_value, g_gain_a = call(
        attn_place_kernel,
        [sds((DS, D), F32), sds((DS, 768), F32), sds((DS, 768), F32), sds((DS, 1), F32)],
        [],
        [parts, w_query, w_key, w_value, gain_attn.astype(F32).reshape(DS, 1)],
        5,
        [pltpu.VMEM((DS, 768), F32)],
    )
    g_gate, g_up, g_down, g_out = ffn_place(sc, owns, gots, [g_gain_a])

    return (
        layer_out[None],
        d_tokens[None],
        g_gain_a.reshape(DS),
        g_gain_m.reshape(DS),
        g_query,
        g_key,
        g_value,
        g_out,
        g_gate,
        g_up,
        g_down,
    )


def solution(mesh):
    cube = Mesh(mesh.devices.reshape(4, 2, 4, 2, 2), ("y", "xh", "z", "xl", "c"))
    fsdp, ctx = ("xl", "c"), ("y", "xh", "z")
    return jax.shard_map(
        body,
        mesh=cube,
        in_specs=(
            P(fsdp, ctx, None),
            P(),
            P(fsdp),
            P(fsdp),
            P(fsdp, None),
            P(fsdp, None),
            P(fsdp, None),
            P(fsdp, None),
            P(None, fsdp),
            P(None, fsdp),
            P(fsdp, None),
            P(fsdp, ctx, None),
        ),
        out_specs=(
            P(fsdp, ctx, None),
            P(fsdp, ctx, None),
            P(fsdp),
            P(fsdp),
            P(fsdp, None),
            P(fsdp, None),
            P(fsdp, None),
            P(fsdp, None),
            P(None, fsdp),
            P(None, fsdp),
            P(fsdp, None),
        ),
        check_vma=False,
    )
```

```python
import functools

import jax
import jax.numpy as jnp
from jax import lax
from jax.experimental import pallas as pl
from jax.experimental.pallas import tpu as pltpu
from jax.sharding import Mesh, PartitionSpec as P

D = 1536
HEADS = 16
KV_HEADS = 8
HEAD_DIM = 96
HALF = HEAD_DIM // 2
FF = 4096
BLOCK = 64
SEQ = 4096
WINDOW_BLOCKS = 32
SHARDS = 4
ROWS = 128
TOK = SHARDS * ROWS
DS = D // SHARDS
FS = FF // SHARDS
EPS = 1e-05
ROPE_BASE = 10000.0
MASKED = -1e30
SCALE = HEAD_DIM ** (-0.5)
LOG2E = 1.4426950408889634
BF = jnp.bfloat16
F32 = jnp.float32

CHUNK_BLOCKS = 8
CHUNK = CHUNK_BLOCKS * BLOCK

SMEM_SPEC = pl.BlockSpec(memory_space=pltpu.SMEM)
VMEM_SPEC = pl.BlockSpec(memory_space=pltpu.VMEM)
ANY_SPEC = pl.BlockSpec(memory_space=pl.ANY)
PARAMS = pltpu.CompilerParams(vmem_limit_bytes=60 * 1024 * 1024)


def cost(us):
    flops, nbytes = int(us * 1_100_000_000), int(us * 3_000_000)
    return pl.CostEstimate(flops=flops, bytes_accessed=nbytes, transcendentals=0)


def call(kernel, outs, smem, vmem, us, scratch=(), deps=()):
    n, d = len(smem) + len(vmem), len(deps)

    def body(*refs):
        kernel(*refs[:n], *refs[n + d :])

    return pl.pallas_call(
        body,
        out_shape=outs,
        in_specs=[SMEM_SPEC] * len(smem) + [VMEM_SPEC] * len(vmem) + [ANY_SPEC] * d,
        out_specs=jax.tree.map(lambda _: VMEM_SPEC, outs),
        scratch_shapes=list(scratch),
        compiler_params=PARAMS,
        cost_estimate=cost(us),
        name=getattr(kernel, "__name__", "part"),
    )(*smem, *vmem, *deps)


def sds(shape, dtype=BF):
    return jax.ShapeDtypeStruct(shape, dtype)


def dot(a, b):
    return jnp.dot(a, b, preferred_element_type=F32)


def dot_t(a, b):
    return lax.dot_general(a, b, (((1,), (1,)), ((), ())), preferred_element_type=F32)


def t_dot(a, b):
    return lax.dot_general(a, b, (((0,), (0,)), ((), ())), preferred_element_type=F32)


def swap_c(x):
    return lax.ppermute(x, "c", [(0, 1), (1, 0)])


def swap_xl(x):
    return lax.ppermute(x, "xl", [(0, 1), (1, 0)])


def swap_both(x):
    return lax.ppermute(x, ("xl", "c"), [(i, i ^ 3) for i in range(4)])


def swap_far(x, core):
    pairs = []
    for place in range(4):
        other = (place + 1) % 4 if place % 2 else (place + 3) % 4
        for c in range(2):
            pairs.append((place * 2 + c, other * 2 + (c ^ core)))
    return lax.ppermute(x, ("xh", "xl", "c"), pairs)


def swap_e(x):
    return lax.ppermute(x, "xh", [(0, 1), (1, 0)])


NEAR = [(0, 1), (1, 0), (2, 3), (3, 2)]
AROUND = [(1, 2), (2, 1), (0, 3), (3, 0)]
CUBE = (("y", NEAR), ("y", AROUND), ("z", NEAR), ("z", AROUND))


def swap_cube(x, dim):
    axis, pairs = CUBE[dim % 4]
    return lax.ppermute(x, axis, pairs)


def from_z(x, m):
    return lax.ppermute(x, "z", [((i + m) % 4, i) for i in range(4)])


def to_z(x, m):
    return lax.ppermute(x, "z", [(i, (i + m) % 4) for i in range(4)])


def gather_slots(own):
    far = swap_xl(own)
    return own, swap_c(own), far, swap_c(far)


def scatter_slots(keep, send):
    got = swap_c(send)
    other = (keep[1].astype(F32) + got[1].astype(F32)).astype(BF)
    return (keep, got, swap_xl(other)), other


CTX = ("y", "xh", "z")
FSDP = ("xl", "c")


def after(x, other):
    return lax.optimization_barrier((x, other))[0]


def shifts(x, axis):
    return [lax.ppermute(x, axis, [((i + m) % 4, i) for i in range(4)]) for m in (1, 2, 3)]


def exchange(x, axes):
    return lax.all_to_all(x, axes, 0, 0, tiled=True)


def cube_index(portion, bits):
    out = 0
    for t in range(4):
        out = out * 2 + bits[(portion + t) % 4]
    return out


def fold(x):
    tail = jnp.concatenate([x[0:64, 128:192], x[64:128, 128:192]], axis=1)
    return jnp.concatenate([x[:, 0:128], tail], axis=0)


def unfold(x):
    tail = jnp.concatenate([x[128:192, 0:64], x[128:192, 64:128]], axis=0)
    return jnp.concatenate([x[0:128], tail], axis=1)


def pack_kernel(sc, wq, wk, wv, gains, q0, q1, q2, q3, k0, k1, k2, k3, tmp):
    f = sc[0]
    for g in range(4):
        tmp[g, :, 0:192] = wk[:, 192 * g : 192 * (g + 1)]
        tmp[g, :, 192:384] = wv[:, 192 * g : 192 * (g + 1)]
    for k, (q, kv) in enumerate(((q0, k0), (q1, k1), (q2, k2), (q3, k3))):
        q[...] = wq[:, pl.ds(pl.multiple_of((f ^ k) * DS, 128), DS)]
        kv[0:DS] = tmp[f ^ k]
        kv[DS:] = gains[...]


def project(f, xa, ws):
    total = jnp.zeros((TOK, DS), F32)
    for k, w in enumerate(ws):
        at = pl.multiple_of((f ^ k) * DS, 128)
        total = total + dot(xa[:, pl.ds(at, DS)], w[0:DS])
    return total


def rotate(u, co, si):
    turned = jnp.concatenate([-u[:, HALF:], u[:, :HALF]], axis=1)
    return u * co + turned * si


def kv_kernel(sc, x0, x1, x2, x3, k0, k1, k2, k3, cos, sin, xa, kv, gain_a, gain_m):
    f = sc[0]
    for k, w in enumerate((k0, k1, k2, k3)):
        at = pl.ds(pl.multiple_of((f ^ k) * DS, 128), DS)
        rows = w[DS:].astype(F32)
        gain_a[:, at] = rows[0:1]
        gain_m[:, at] = rows[1:2]
    for k, x in enumerate((x0, x1, x2, x3)):
        u = x[...].astype(F32)
        r = lax.rsqrt(jnp.mean(u * u, axis=-1, keepdims=True) + EPS)
        xa[ROWS * k : ROWS * (k + 1), :] = (u * r * gain_a[...]).astype(BF)
    lin = project(f, xa, [w[0:DS] for w in (k0, k1, k2, k3)])
    co, si = cos[...], sin[...]
    for k in range(4):
        part = lin[ROWS * k : ROWS * (k + 1)]
        for j in range(2):
            key = rotate(part[:, 96 * j : 96 * (j + 1)], co, si)
            value = part[:, 192 + 96 * j : 192 + 96 * (j + 1)]
            kv[2 * k + j] = fold(jnp.concatenate([key, value], axis=1)).astype(BF)


def q_kernel(sc, xa, w0, w1, w2, w3, cos, sin, q):
    lin = project(sc[0], xa, (w0, w1, w2, w3))
    co, si = cos[...], sin[...]
    for k in range(4):
        part = lin[ROWS * k : ROWS * (k + 1)]
        heads = [rotate(part[:, 96 * h : 96 * (h + 1)], co, si) for h in range(4)]
        for j in range(2):
            q[2 * k + j] = fold(jnp.concatenate(heads[2 * j : 2 * j + 2], axis=1)).astype(BF)


def widen(x, *tail):
    zeros = jnp.zeros((x.shape[0], 128 - x.shape[1] - len(tail)), x.dtype)
    return jnp.concatenate([x, *tail, zeros], axis=1)


def stacked(x, t):
    rows = slice(BLOCK * t, BLOCK * (t + 1))
    return jnp.concatenate([x[rows, 0:96], x[rows, 96:192]], axis=0)


def side_by_side(a, b):
    rows = [jnp.concatenate([x[0:BLOCK, 0:96], x[BLOCK:, 0:96]], axis=1) for x in (a, b)]
    return fold(jnp.concatenate(rows, axis=0))


def low_high(qb, n):
    swapped = (qb[2 * n] >= WINDOW_BLOCKS).astype(jnp.int32)
    return 2 * n + swapped, 2 * n + 1 - swapped


def attention_kernel(qb, kb, q, kv0, kv1, kv2, kv3, o, o2, q2, lse, kv):
    ones = (lax.broadcasted_iota(jnp.int32, (BLOCK, 32), 1) < 4).astype(F32)

    def place(s, _):
        for m, ref in enumerate((kv0, kv1, kv2, kv3)):
            x = unfold(ref[s].astype(F32))
            for t in range(2):
                dst = pl.ds(pl.multiple_of(kb[m * 16 + 2 * s + t] * BLOCK, BLOCK), BLOCK)
                part = x[BLOCK * t : BLOCK * (t + 1)]
                both = jnp.concatenate([part[:, 0:96], ones, part[:, 96:192], ones], axis=1)
                kv[dst, :] = both.astype(BF)
        x = unfold(q[s].astype(F32))
        for t in range(2):
            q2[2 * s + t] = widen(stacked(x, t)).astype(BF)
        return 0

    lax.fori_loop(0, 8, place, 0)
    two = SCALE * LOG2E

    def scores(n, spans):
        return [dot_t(q2[n], kv[span, 0:128]) for span in spans]

    def finish(n, parts, spans):
        tops = [jnp.max(s, axis=1, keepdims=True) for s in parts]
        top = functools.reduce(jnp.maximum, tops) * two
        acc = jnp.zeros((ROWS, 128), F32)
        for s, span in zip(parts, spans):
            acc += dot(jnp.exp2(s * two - top).astype(BF), kv[span, 128:256])
        total = acc[:, 96:97]
        o2[n] = (acc / total).astype(BF)
        lse[n] = jnp.broadcast_to(top + jnp.log2(total), (ROWS, 8))

    def pair(n, _):
        low, high = low_high(qb, n)
        i_low, i_high = qb[low], qb[high]
        for count in range(1, 5):

            @pl.when(i_low // CHUNK_BLOCKS == count - 1)
            def _():
                edge = pl.ds(pl.multiple_of((i_high - WINDOW_BLOCKS) * BLOCK, BLOCK), BLOCK)
                at = pl.multiple_of((i_high - WINDOW_BLOCKS + 1) * BLOCK, BLOCK)
                spans_h = [edge] + [pl.ds(at + CHUNK * t, CHUNK) for t in range(4)]
                spans_l = [pl.ds(CHUNK * t, CHUNK) for t in range(count)]
                high_s = scores(high, spans_h)
                low_s = scores(low, spans_l)
                key = lax.broadcasted_iota(jnp.int32, (ROWS, BLOCK), 1)
                query = lax.broadcasted_iota(jnp.int32, (ROWS, BLOCK), 0) % BLOCK
                high_s[0] = jnp.where(key > query, high_s[0], MASKED)
                key = lax.broadcasted_iota(jnp.int32, (ROWS, CHUNK), 1)
                limit = (i_low + 1) * BLOCK - CHUNK * (count - 1)
                low_s[-1] = jnp.where(key < limit, low_s[-1], MASKED)
                finish(high, high_s, spans_h)
                finish(low, low_s, spans_l)

        return 0

    lax.fori_loop(0, 8, pair, 0)

    def gather(s, _):
        o[s] = side_by_side(o2[2 * s].astype(F32), o2[2 * s + 1].astype(F32)).astype(BF)
        return 0

    lax.fori_loop(0, 8, gather, 0)


def attention_back_kernel(qb, kb, q2s, d_o, o2s, lse, kv, dq2s, g, dkv, do2s):
    dkv[...] = jnp.zeros_like(dkv)

    def place(s, _):
        x = unfold(d_o[s].astype(F32))
        for t in range(2):
            do2s[2 * s + t] = stacked(x, t).astype(BF)
        return 0

    lax.fori_loop(0, 8, place, 0)
    two = SCALE * LOG2E

    def split(x):
        parts = []
        for _ in range(3):
            parts.append(x.astype(BF))
            x = x - parts[-1].astype(F32)
        return parts

    def weights(n):
        do2 = do2s[n]
        inner = do2.astype(F32) * o2s[n][:, 0:96].astype(F32)
        inner = jnp.sum(inner, axis=1, keepdims=True)
        q2 = widen(q2s[n][:, 0:96], *split(lse[n][:, 0:1] * (-1.0 / two)))
        do2 = widen(do2, *split(-inner))
        none = jnp.zeros((ROWS, 128), BF)
        return jnp.concatenate(
            [jnp.concatenate([q2, none], axis=1), jnp.concatenate([none, do2], axis=1)], axis=0
        )

    def factors(w, spans, masks):
        pairs = []
        for span, mask in zip(spans, masks):
            s = dot_t(kv[span, :], w)
            p = jnp.exp2(s[:, 0:128] * two)
            if mask is not None:
                p = jnp.where(mask, p, 0.0)
            ds = (p * s[:, 128:256]).astype(BF)
            pairs.append(jnp.concatenate([ds, p.astype(BF)], axis=1))
        return pairs

    def add(n, w, spans, pairs):
        acc = jnp.zeros((ROWS, 128), F32)
        for span, both in zip(spans, pairs):
            dkv[span, :] += dot(both, w)
            acc += t_dot(both[:, 0:128], kv[span, 0:128])
        dq2s[n] = (acc * SCALE).astype(BF)

    def pair(n, _):
        low, high = low_high(qb, n)
        i_low, i_high = qb[low], qb[high]
        for count in range(1, 5):

            @pl.when(i_low // CHUNK_BLOCKS == count - 1)
            def _():
                edge = pl.ds(pl.multiple_of((i_high - WINDOW_BLOCKS) * BLOCK, BLOCK), BLOCK)
                at = pl.multiple_of((i_high - WINDOW_BLOCKS + 1) * BLOCK, BLOCK)
                key = lax.broadcasted_iota(jnp.int32, (BLOCK, ROWS), 0)
                query = lax.broadcasted_iota(jnp.int32, (BLOCK, ROWS), 1) % BLOCK
                spans_h = [edge] + [pl.ds(at + CHUNK * t, CHUNK) for t in range(4)]
                masks_h = [key > query] + [None] * 4
                spans_l = [pl.ds(CHUNK * t, CHUNK) for t in range(count)]
                key = lax.broadcasted_iota(jnp.int32, (CHUNK, ROWS), 0)
                limit = (i_low + 1) * BLOCK - CHUNK * (count - 1)
                masks_l = [None] * (count - 1) + [key < limit]
                w_h, w_l = weights(high), weights(low)
                pairs_h = factors(w_h, spans_h, masks_h)
                pairs_l = factors(w_l, spans_l, masks_l)
                add(high, w_h, spans_h, pairs_h)
                add(low, w_l, spans_l, pairs_l)

        return 0

    lax.fori_loop(0, 8, pair, 0)

    def keys(s, _):
        parts = []
        for t in range(2):
            src = pl.ds(pl.multiple_of(kb[2 * s + t] * BLOCK, BLOCK), BLOCK)
            both = dkv[src, :]
            parts.append(jnp.concatenate([both[:, 0:96] * SCALE, both[:, 128:224]], axis=1))
        g[s] = fold(jnp.concatenate(parts, axis=0)).astype(BF)
        return 0

    lax.fori_loop(0, 32, keys, 0)


def fold_dq_kernel(dq2s, dq):
    for s in range(8):
        dq[s] = side_by_side(dq2s[2 * s].astype(F32), dq2s[2 * s + 1].astype(F32)).astype(BF)


def unfolded(o):
    return unfold(o.astype(F32)).astype(BF)


def out_kernel(o, w, keep, send):
    for k in range(4):
        total = dot(unfolded(o[2 * k]), w[0:192, :]) + dot(unfolded(o[2 * k + 1]), w[192:384, :])
        (keep, send)[k % 2][k // 2] = total.astype(BF)


def hidden_kernel(x, keep, got, far, gain, hidden, xm):
    h = x[...].astype(F32) + keep[0].astype(F32) + got[0].astype(F32) + far[...].astype(F32)
    hidden[...] = h
    r = lax.rsqrt(jnp.mean(h * h, axis=-1, keepdims=True) + EPS)
    xm[...] = (h * r * gain[...]).astype(BF)


def norm_back(values, gain, grads):
    factor = lax.rsqrt(jnp.mean(values * values, axis=-1, keepdims=True) + EPS)
    weighted = grads * gain
    inner = jnp.mean(weighted * values, axis=-1, keepdims=True)
    return factor * weighted - values * (factor * factor * factor) * inner


def d_hidden_kernel(dy, keep, got, far, hidden, gain, d_hidden, d_br, d_gain):
    grads = keep[0].astype(F32) + got[0].astype(F32) + far[...].astype(F32)
    h = hidden[...]
    d = dy[...].astype(F32) + norm_back(h, gain[...], grads)
    d_hidden[...] = d
    d_br[...] = d.astype(BF)
    r = lax.rsqrt(jnp.mean(h * h, axis=-1, keepdims=True) + EPS)
    total = jnp.sum(grads * h * r, axis=0, keepdims=True)
    rows = [total[:, 128 * t : 128 * (t + 1)] for t in range(12)]
    d_gain[...] = jnp.concatenate(rows + [jnp.zeros((4, 128), F32)], axis=0).astype(BF)


def last_kernel(x, keep, got, far, hidden, d_hidden, gain, layer_out, d_tokens):
    total = keep[0].astype(F32) + got[0].astype(F32) + far[0].astype(F32)
    layer_out[...] = (hidden[...] + total).astype(BF)
    grads = keep[1].astype(F32) + got[1].astype(F32) + far[1].astype(F32)
    d_tokens[...] = d_hidden[...] + norm_back(x[...].astype(F32), gain[...], grads)


def d_o_kernel(b0, b1, b2, b3, w, d_o):
    for k, b in enumerate((b0, b1, b2, b3)):
        d = dot_t(b[...], w[...])
        d_o[2 * k] = fold(d[:, 0:192]).astype(BF)
        d_o[2 * k + 1] = fold(d[:, 192:384]).astype(BF)


FBLOCK = 512


def d_act_kernel(y0, y1, y2, y3, wd, da):
    ys = jnp.concatenate([y0[...], y1[...], y2[...], y3[...]], axis=0)
    da[...] = dot_t(ys, wd[...])


def ffn_kernel(sc, x0, x1, x2, x3, da, wg, wu, act, dg, du, keep, send, xs, acc):
    n = pl.program_id(0)

    @pl.when(n == 0)
    def _():
        for k, x in enumerate((x0, x1, x2, x3)):
            xs[ROWS * k : ROWS * (k + 1), :] = x[...]

    gate = dot(xs[...], wg[...])
    up = dot(xs[...], wu[...])
    d = da[...]
    sg = jax.nn.sigmoid(gate)
    both = gate * sg
    a = (both * up).astype(BF)
    d_gate = (d * up * sg * (1.0 + gate * (1.0 - sg))).astype(BF)
    d_up = (d * both).astype(BF)
    for h in range(2):
        at = pl.multiple_of((h ^ (sc[2] & 1)) * 256, 256)
        for ref, tile in ((act, a), (dg, d_gate), (du, d_up)):
            ref[:, pl.ds(at, 256)] = tile[:, 256 * h : 256 * (h + 1)]
    dx = dot_t(d_gate, wg[...]) + dot_t(d_up, wu[...])

    @pl.when(n == 0)
    def _():
        acc[...] = dx

    @pl.when(n > 0)
    def _():
        total = acc[...] + dx
        for k in range(4):
            (keep, send)[k % 2][k // 2] = total[ROWS * k : ROWS * (k + 1), :].astype(BF)


def ffn(sc, xs, da, wg, wu):
    full = pl.BlockSpec((ROWS, D), lambda n, s: (0, 0))
    side = pl.BlockSpec((2, ROWS, D), lambda n, s: (0, 0, 0))
    cols = pl.BlockSpec((D, FBLOCK), lambda n, s: (0, n))
    rel = pl.BlockSpec((TOK, FBLOCK), lambda n, s: (0, n ^ (s[2] >> 1)))
    return pl.pallas_call(
        ffn_kernel,
        grid_spec=pltpu.PrefetchScalarGridSpec(
            num_scalar_prefetch=1,
            grid=(FS // FBLOCK,),
            in_specs=[full] * 4 + [pl.BlockSpec((TOK, FBLOCK), lambda n, s: (0, n)), cols, cols],
            out_specs=[rel, rel, rel, side, side],
            scratch_shapes=[pltpu.VMEM((TOK, D), BF), pltpu.VMEM((TOK, D), F32)],
        ),
        out_shape=[sds((TOK, FS))] * 3 + [sds((2, ROWS, D))] * 2,
        compiler_params=PARAMS,
        cost_estimate=cost(11),
    )(sc, *xs, da, wg, wu)


def mlp_out_kernel(sc, act, wd, keep_in, send_in, keep, send):
    gz = sc[2]
    acts = [
        act[:, pl.ds(pl.multiple_of((b ^ gz) * 256, 256), 256)] for b in range(FS // 256)
    ]
    total = dot(jnp.concatenate(acts, axis=1), wd[...])
    for k in range(4):
        (keep, send)[k % 2][2 * (k // 2)] = total[ROWS * k : ROWS * (k + 1)].astype(BF)
    for k in range(2):
        keep[2 * k + 1] = keep_in[k]
        send[2 * k + 1] = send_in[k]


def ffn_grads_kernel(sc, x0, x1, x2, x3, y0, y1, y2, y3, act, dg, du, *refs):
    gy = sc[1]
    keeps, sends, ys = refs[:4], refs[4:8], refs[8]

    def put(p, ra, rb, at, tile):
        index = cube_index(p, (ra & 1, ra >> 1, rb & 1, rb >> 1))
        ref = (keeps, sends)[index >> 3][p]
        ref[index & 7, at : at + tile.shape[0], :] = tile.astype(BF)

    for ra in range(4):
        cols = pl.ds(pl.multiple_of((ra ^ gy) * DS, 128), DS)
        xa = jnp.concatenate([x[:, cols] for x in (x0, x1, x2, x3)], axis=0)
        for k, y in enumerate((y0, y1, y2, y3)):
            ys[ROWS * k : ROWS * (k + 1), DS * ra : DS * (ra + 1)] = y[:, cols]
        for n, d in enumerate((dg, du)):
            wide = t_dot(xa, d[...])
            for rb in range(4):
                for p in range(4):
                    lane, row = 256 * rb + 128 * (p // 2), 192 * (p % 2)
                    put(p, ra, rb, 192 * n, wide[row : row + 192, lane : lane + 128])
    for rb in range(4):
        wide = t_dot(act[:, 256 * rb : 256 * (rb + 1)], ys[...])
        for ra in range(4):
            for p in range(4):
                at = 384
                row = 192 * p
                while row < 192 * (p + 1):
                    lane, r = DS * ra + 128 * (row // 256), row % 256
                    size = min(256 - r, 192 * (p + 1) - row)
                    put(p, ra, rb, at, wide[r : r + size, lane : lane + 128])
                    at += size
                    row += size


OUT_ROWS = 288
OUT_SPLIT = (80, 80, 64, 64)
OUT_AT = (0, 80, 160, 224)
PART_ROWS = tuple(576 + n for n in OUT_SPLIT)
PART_AT = (0, 656, 1312, 1952)
GAIN_AT = 2592


def first_step(keeps, gots, deps, us):
    def body(*refs):
        for p in range(4):
            k, g, out = refs[2 * p], refs[2 * p + 1], refs[8 + len(deps) + p]
            out[...] = (k[...].astype(F32) + g[...].astype(F32)).astype(BF)

    args = [x for pair in zip(keeps, gots) for x in pair]
    return pl.pallas_call(
        body,
        grid=(4,),
        in_specs=[pl.BlockSpec((1, 576, 128), lambda n: (n + 4, 0, 0))] * 8
        + [ANY_SPEC] * len(deps),
        out_specs=[pl.BlockSpec((1, 576, 128), lambda n: (n, 0, 0))] * 4,
        out_shape=[sds((4, 576, 128))] * 4,
        compiler_params=PARAMS,
        cost_estimate=cost(us),
    )(*args, *deps)


def cube_step(terms, deps, us):
    count = len(terms[0])
    half = terms[0][-1].shape[0] // 2
    lower = pl.BlockSpec((1, 576, 128), lambda n: (n, 0, 0))
    upper = pl.BlockSpec((1, 576, 128), lambda n: (n + half, 0, 0))
    used = 8 * count

    def body(*refs):
        outs = refs[used + len(deps) :]
        for p in range(4):
            mine = refs[2 * count * p : 2 * count * (p + 1)]
            for side in range(2):
                total = mine[side][...].astype(F32)
                for t in range(1, count):
                    total += mine[2 * t + side][...].astype(F32)
                outs[2 * p + side][...] = total.astype(BF)

    args = [x for portion in terms for term in portion for x in (term, term)]
    outs = pl.pallas_call(
        body,
        grid=(half,),
        in_specs=[lower, upper] * (4 * count) + [ANY_SPEC] * len(deps),
        out_specs=[lower] * 8,
        out_shape=[sds((half, 576, 128))] * 8,
        compiler_params=PARAMS,
        cost_estimate=cost(us),
    )(*args, *deps)
    return outs[0::2], outs[1::2]


def last_step_kernel(k0, k1, k2, k3, g0, g1, g2, g3, out, total):
    for p, (k, g) in enumerate(((k0, g0), (k1, g1), (k2, g2), (k3, g3))):
        at = PART_AT[p]
        total[at : at + 576, :] = (k[0].astype(F32) + g[0].astype(F32)).astype(BF)
        total[at + 576 : at + PART_ROWS[p], :] = out[OUT_AT[p] : OUT_AT[p] + OUT_SPLIT[p]]
    total[GAIN_AT:, :] = out[OUT_ROWS:]


def join_kernel(own, got, p0, p1, p2, p3, gains):
    total = own[...].astype(F32) + got[...].astype(F32)
    for p, ref in enumerate((p0, p1, p2, p3)):
        ref[0] = total[PART_AT[p] : PART_AT[p] + PART_ROWS[p]].astype(BF)
    gains[...] = total[GAIN_AT:]


def stack_kernel(a0, a1, a2, a3, b0, b1, b2, b3, o0, o1, o2, o3):
    for a, b, o in ((a0, b0, o0), (a1, b1, o1), (a2, b2, o2), (a3, b3, o3)):
        o[0 : a.shape[0]] = a[...]
        o[a.shape[0] :] = b[...]


def cube_gather(owns, gots, us, deps):
    outs = [sds((2 * o.shape[0], *o.shape[1:])) for o in owns]
    return call(stack_kernel, outs, [], [*owns, *gots], us, deps=deps)


def pick(owns, gots, p, bits, rows):
    index = cube_index(p, bits)
    rest = index & 7
    return jnp.where(index >= 8, gots[p][rest, rows, :], owns[p][rest, rows, :])


def ffn_place_kernel(sc, *refs):
    owns, gots = refs[0:4], refs[4:8]
    gate, up, down, out, tmp = refs[8:]
    gy, gz = sc[1], sc[2]
    ra = pl.program_id(0) ^ gy
    for bb in range(4):
        rb = bb ^ gz
        bits = (ra & 1, ra >> 1, rb & 1, rb >> 1)
        for p in range(4):
            lane, row = 256 * bb + 128 * (p // 2), 192 * (p % 2)
            for n, ref in enumerate((gate, up)):
                tile = pick(owns, gots, p, bits, slice(192 * n, 192 * (n + 1)))
                ref[row : row + 192, lane : lane + 128] = tile.astype(F32)
            at, row = 384, 192 * p
            while row < 192 * (p + 1):
                lane, r = row // 256, row % 256
                size = min(256 - r, 192 * (p + 1) - row)
                tile = pick(owns, gots, p, bits, slice(at, at + size))
                down[256 * bb + r : 256 * bb + r + size, 128 * lane : 128 * (lane + 1)] = (
                    tile.astype(F32)
                )
                at += size
                row += size
            at = OUT_ROWS * (bb ^ (bb >> 1)) + OUT_AT[p]
            tile = pick(owns, gots, p, bits, slice(576, PART_ROWS[p]))
            tmp[at : at + OUT_SPLIT[p], :] = tile.astype(F32)
    for t in range(3):
        out[:, 128 * t : 128 * (t + 1)] = tmp[DS * t : DS * (t + 1), :]


def ffn_place(sc, owns, gots, deps):
    def body(*refs):
        ffn_place_kernel(*refs[:9], *refs[9 + len(deps) :])

    whole = [pl.BlockSpec((8, n, 128), lambda n, s: (0, 0, 0)) for n in PART_ROWS]
    rows = pl.BlockSpec((DS, FS), lambda n, s: (n, 0))
    return pl.pallas_call(
        body,
        grid_spec=pltpu.PrefetchScalarGridSpec(
            num_scalar_prefetch=1,
            grid=(4,),
            in_specs=whole * 2 + [ANY_SPEC] * len(deps),
            out_specs=[
                rows,
                rows,
                pl.BlockSpec((FS, DS), lambda n, s: (0, n)),
                pl.BlockSpec((DS, DS), lambda n, s: (0, n ^ (n >> 1))),
            ],
            scratch_shapes=[pltpu.VMEM((4 * OUT_ROWS, 128), F32)],
        ),
        out_shape=[sds((D, FS), F32), sds((D, FS), F32), sds((FS, D), F32), sds((DS, D), F32)],
        compiler_params=PARAMS,
        cost_estimate=cost(12),
    )(sc, *owns, *gots, *deps)


def out_grads_kernel(o, b0, b1, b2, b3, d_gain, pieces, tmp):
    bs = jnp.concatenate([b0[...], b1[...], b2[...], b3[...]], axis=0)
    for j in range(2):
        oj = jnp.concatenate([unfolded(o[2 * k + j]) for k in range(4)], axis=0)
        tmp[192 * j : 192 * (j + 1), :] = t_dot(oj, bs)
    for s in range(16):
        pieces[s, OUT_ROWS:, :] = d_gain[...]
        start, at = OUT_ROWS * s, 0
        while start < OUT_ROWS * (s + 1):
            lane, r = 128 * (start // DS), start % DS
            size = min(DS - r, OUT_ROWS * (s + 1) - start)
            pieces[s, at : at + size, :] = tmp[r : r + size, lane : lane + 128].astype(BF)
            at += size
            start += size


def sum_kernel(parts, out):
    out[...] = jnp.sum(parts[...].astype(F32), axis=0).astype(BF)


def sum_slots_kernel(sc, parts, gains, o0, o1, o2, o3):
    for k, out in enumerate((o0, o1, o2, o3)):
        g = sc[0] ^ k
        total = parts[0, g].astype(F32)
        for n in range(1, 32):
            total += parts[n, g].astype(F32)
        rows = [gains[pl.ds(3 * g + t, 1), :] for t in range(3)]
        rows = [total, *rows, jnp.zeros((5, 128), F32)]
        out[...] = jnp.concatenate(rows, axis=0).astype(BF)


def repeat_kernel(sc, p0, p1, p2, p3, out, gain):
    total = jnp.zeros((8, 128), F32)
    for k, part in enumerate((p0, p1, p2, p3)):
        whole = part[...].astype(F32)
        total += whole[QKV_ROWS:]
        mine = whole[:QKV_ROWS].astype(BF)
        for n in range(32):
            out[n, sc[0] ^ k] = mine
    gain[...] = total


QKV_ROWS = 72


def d_xa_kernel(sc, d_q, d_kv, q0, q1, q2, q3, k0, k1, k2, k3, cos, sin, lin, keep, send, dq, dkv):
    f = sc[0]
    co, si = cos[...], sin[...]

    def back(g):
        w = g * si
        turned = jnp.concatenate([w[:, HALF:], -w[:, :HALF]], axis=1)
        return (g * co + turned).astype(BF)

    for k in range(4):
        rows = slice(ROWS * k, ROWS * (k + 1))
        for j in range(2):
            i = 2 * k + j
            gq = unfold(d_q[i].astype(F32))
            gkv = d_kv[4 * i].astype(F32)
            for z in range(1, 4):
                gkv += d_kv[4 * i + z].astype(F32)
            gkv = unfold(gkv)
            for n in range(2):
                g = back(gq[:, 96 * n : 96 * (n + 1)])
                lin[rows, 384 * j + 96 * n : 384 * j + 96 * (n + 1)] = g
                dq[rows, 192 * j + 96 * n : 192 * j + 96 * (n + 1)] = g
            g = back(gkv[:, 0:96])
            lin[rows, 384 * j + 192 : 384 * j + 288] = g
            dkv[rows, 96 * j : 96 * (j + 1)] = g
            g = gkv[:, 96:192].astype(BF)
            lin[rows, 384 * j + 288 : 384 * j + 384] = g
            dkv[rows, 192 + 96 * j : 192 + 96 * (j + 1)] = g
    for k, (wq, wkv) in enumerate(((q0, k0), (q1, k1), (q2, k2), (q3, k3))):
        cols = pl.ds(pl.multiple_of((f ^ k) * DS, 128), DS)
        total = (dot_t(dq[...], wq[...]) + dot_t(dkv[...], wkv[0:DS])).astype(BF)
        for s in range(4):
            (keep, send)[s % 2][s // 2, :, cols] = total[ROWS * s : ROWS * (s + 1)]


def flat_pieces(n):
    out, start = [], QKV_ROWS * n
    while start < QKV_ROWS * (n + 1):
        r = start % DS
        size = min(DS - r, QKV_ROWS * (n + 1) - start)
        out.append((128 * (start // DS), r, size))
        start += size
    return out


def qkv_grads_kernel(xa, lin, pieces, tmp):
    for g in range(4):
        tmp[...] = t_dot(xa[:, DS * g : DS * (g + 1)], lin[...])
        for n in range(32):
            tiles = [tmp[r : r + size, lane : lane + 128] for lane, r, size in flat_pieces(n)]
            pieces[n, g] = jnp.concatenate(tiles, axis=0).astype(BF)


def attn_place_kernel(got, wq, wk, wv, gain_in, q, k, v, gain, tmp):
    for g in range(4):
        for n in range(32):
            tile, at = got[n, g].astype(F32), 0
            for lane, r, size in flat_pieces(n):
                tmp[r : r + size, lane : lane + 128] = tile[at : at + size]
                at += size
        for j in range(2):
            at = 384 * j
            q[:, 384 * g + 192 * j : 384 * g + 192 * (j + 1)] = tmp[:, at : at + 192]
            k[:, 192 * g + 96 * j : 192 * g + 96 * (j + 1)] = tmp[:, at + 192 : at + 288]
            v[:, 192 * g + 96 * j : 192 * g + 96 * (j + 1)] = tmp[:, at + 288 : at + 384]
    total = jnp.sum(wq[...].astype(F32) * q[...], axis=1, keepdims=True)
    total += jnp.sum(wk[...].astype(F32) * k[...], axis=1, keepdims=True)
    total += jnp.sum(wv[...].astype(F32) * v[...], axis=1, keepdims=True)
    gain[...] = total / gain_in[...]


def rope_tables(positions):
    freqs = ROPE_BASE ** (-jnp.arange(HALF).astype(F32) * 2.0 / HEAD_DIM)
    angles = positions.astype(F32)[:, None] * freqs[None, :]
    angles = jnp.concatenate([angles, angles], axis=1)
    return jnp.cos(angles), jnp.sin(angles)


def body(
    tokens,
    block_order,
    gain_attn,
    gain_mlp,
    w_query,
    w_key,
    w_value,
    w_out,
    w_gate,
    w_up,
    w_down,
    cotangent,
):
    y, xh, z = lax.axis_index("y"), lax.axis_index("xh"), lax.axis_index("z")
    xl, c = lax.axis_index("xl"), lax.axis_index("c")
    f = xl * 2 + c
    gy, gz = y ^ (y >> 1), z ^ (z >> 1)
    sc = jnp.stack([f, gy, gz]).astype(jnp.int32)
    own_x, own_dy = tokens[0], cotangent[0]

    place = (y * 2 + xh) * 4 + z
    own_blocks = lax.dynamic_slice_in_dim(block_order, 2 * place, 2)
    positions = (own_blocks[:, None] * BLOCK + jnp.arange(BLOCK)).reshape(-1)
    cos, sin = rope_tables(positions)
    blocks = block_order.reshape(8, 4, 2)
    key_blocks = jnp.stack(
        [
            lax.dynamic_index_in_dim(blocks, (z + m) % 4, axis=1, keepdims=False).reshape(-1)
            for m in range(4)
        ]
    ).reshape(-1)
    query_blocks = key_blocks[:16]

    xs = gather_slots(own_x)
    packs = call(
        pack_kernel,
        [sds((DS, DS))] * 4 + [sds((DS + 16, DS))] * 4,
        [sc],
        [w_query, w_key, w_value, jnp.pad(jnp.stack([gain_attn, gain_mlp]), ((0, 14), (0, 0)))],
        3,
        [pltpu.VMEM((4, DS, DS), BF)],
    )
    wkvs = (packs[4], swap_c(packs[5]), swap_xl(packs[6]), swap_far(packs[7], 1))
    wqs = (packs[0], swap_c(packs[1]), swap_far(packs[2], 0), swap_far(packs[3], 1))

    folded, heads = (8, 192, 128), ("y", "xh")
    xa, kv, gain_a, gain_m = call(
        kv_kernel,
        [sds((TOK, D)), sds(folded), sds((1, D), F32), sds((1, D), F32)],
        [sc],
        [*xs, *wkvs, cos, sin],
        5,
    )
    q = call(q_kernel, sds(folded), [sc], [xa, *wqs, cos, sin], 4)
    kv = exchange(kv, heads)
    kvs = shifts(kv, "z")
    q = exchange(q, heads)
    o, o2, q2, lse, kv_sorted = call(
        attention_kernel,
        [
            sds(folded),
            sds((16, ROWS, 128)),
            sds((16, ROWS, 128)),
            sds((16, ROWS, 8), F32),
            sds((SEQ, 256)),
        ],
        [query_blocks, key_blocks],
        [q, kv, *kvs],
        13,
    )
    o_tok = exchange(o, heads)

    dys = gather_slots(own_dy)
    d_act = call(d_act_kernel, sds((TOK, FS), F32), [], [*dys, w_down], 4, deps=[o])
    side = [sds((2, ROWS, D))] * 2
    keep, send = call(out_kernel, side, [], [o_tok, w_out], 2, deps=[d_act])
    terms, _ = scatter_slots(keep, send)
    hidden, xm = call(
        hidden_kernel, [sds((ROWS, D), F32), sds((ROWS, D))], [], [own_x, *terms, gain_m], 2
    )
    xms = gather_slots(xm)
    act, dg, du, keep, send = ffn(sc, xms, d_act, w_gate, w_up)
    terms, moving = scatter_slots(keep, send)

    grads = call(
        ffn_grads_kernel,
        [sds((8, 576, 128))] * 8,
        [sc],
        [*xms, *dys, act, dg, du],
        9,
        [pltpu.VMEM((TOK, D), BF)],
        [moving],
    )
    keeps, sends = grads[:4], grads[4:]
    gots = [swap_cube(s, p) for p, s in enumerate(sends)]
    d_hidden, d_br, d_gain = call(
        d_hidden_kernel,
        [sds((ROWS, D), F32), sds((ROWS, D)), sds((16, 128))],
        [],
        [own_dy, *terms, hidden, gain_m],
        2,
        deps=[sends[0]],
    )
    d_brs = gather_slots(d_br)
    d_o = call(d_o_kernel, sds(folded), [], [*d_brs, w_out], 2)
    d_o_att = exchange(d_o, heads)
    out_pieces = call(
        out_grads_kernel,
        sds((16, OUT_ROWS + 16, 128)),
        [],
        [o_tok, *d_brs, d_gain],
        2,
        [pltpu.VMEM((DS, D), F32)],
        [d_o],
    )
    sends = first_step(keeps, gots, [out_pieces], 4)
    more = [swap_cube(s, p + 1) for p, s in enumerate(sends)]
    out_got = exchange(out_pieces, ("y", "z"))
    dq2, dkv = call(
        attention_back_kernel,
        [sds((16, ROWS, 128)), sds((32, 192, 128))],
        [query_blocks, block_order],
        [q2, d_o_att, o2, lse, kv_sorted],
        24,
        [pltpu.VMEM((SEQ, 256), F32), pltpu.VMEM((16, ROWS, 96), BF)],
        [sends[0]],
    )
    dkv_tok = exchange(dkv, CTX)
    keeps, sends = cube_step(list(zip(keeps, gots, more)), [dq2], 5)
    gots = [swap_cube(s, p + 2) for p, s in enumerate(sends)]
    out_sum = call(
        sum_kernel, sds((OUT_ROWS + 16, 128)), [], [out_got], 40, deps=[sends[0]]
    )
    dq = call(fold_dq_kernel, sds(folded), [], [dq2], 2, deps=[out_sum, dkv_tok])
    dq_tok = exchange(dq, heads)
    keeps, sends = cube_step(list(zip(keeps, gots)), [out_sum], 3)
    gots = [swap_cube(s, p + 3) for p, s in enumerate(sends)]
    total = call(
        last_step_kernel, sds((GAIN_AT + 16, 128)), [], [*keeps, *gots, out_sum], 2
    )
    total_got = swap_e(total)

    lin, keep, send = call(
        d_xa_kernel,
        [sds((TOK, 768)), *side],
        [sc],
        [dq_tok, dkv_tok, *wqs, *wkvs, cos, sin],
        7,
        [pltpu.VMEM((TOK, DS), BF), pltpu.VMEM((TOK, DS), BF)],
        [total],
    )
    *owns, gains_sum = call(
        join_kernel,
        [sds((1, n, 128)) for n in PART_ROWS] + [sds((16, 128), F32)],
        [],
        [total, total_got],
        2,
        deps=[lin],
    )
    gots = [swap_cube(o, p + 3) for p, o in enumerate(owns)]
    pieces = call(
        qkv_grads_kernel,
        sds((32, 4, QKV_ROWS, 128)),
        [],
        [xa, lin],
        5,
        [pltpu.VMEM((DS, 768), F32)],
        [owns[0]],
    )
    pieces_got = exchange(pieces, CTX)
    keep, send = call(
        mlp_out_kernel,
        [sds((4, ROWS, D))] * 2,
        [sc],
        [act, w_down, keep, send],
        6,
        deps=[pieces],
    )
    got = swap_c(send)
    far = swap_xl((keep[2:].astype(F32) + got[2:].astype(F32)).astype(BF))
    owns = cube_gather(owns, gots, 2, [keep])
    gots = [swap_cube(o, p + 2) for p, o in enumerate(owns)]
    part = call(
        sum_slots_kernel,
        [sds((QKV_ROWS + 8, 128))] * 4,
        [sc],
        [pieces_got, gains_sum],
        3,
        deps=[owns[0]],
    )
    part_got = [part[0], swap_c(part[1]), swap_xl(part[2]), swap_both(part[3])]
    owns = cube_gather(owns, gots, 3, [part[0]])
    gots = [swap_cube(o, p + 1) for p, o in enumerate(owns)]
    parts, g_gain_m = call(
        repeat_kernel,
        [sds((32, 4, QKV_ROWS, 128)), sds((8, 128), F32)],
        [sc],
        part_got,
        3,
        deps=[owns[0]],
    )
    parts_got = exchange(parts, CTX)
    owns = cube_gather(owns, gots, 60, [parts])
    gots = [swap_cube(o, p) for p, o in enumerate(owns)]
    layer_out, d_tokens = call(
        last_kernel,
        [sds((ROWS, D)), sds((ROWS, D), F32)],
        [],
        [own_x, keep, got, far, hidden, d_hidden, gain_a],
        5,
        deps=[owns[0]],
    )
    g_query, g_key, g_value, g_gain_a = call(
        attn_place_kernel,
        [sds((DS, D), F32), sds((DS, 768), F32), sds((DS, 768), F32), sds((DS, 1), F32)],
        [],
        [parts_got, w_query, w_key, w_value, gain_attn.astype(F32).reshape(DS, 1)],
        6,
        [pltpu.VMEM((DS, 768), F32)],
        [d_tokens],
    )
    g_gate, g_up, g_down, g_out = ffn_place(sc, owns, gots, [g_query])

    return (
        layer_out[None],
        d_tokens[None],
        g_gain_a.reshape(DS),
        g_gain_m[0:3].reshape(DS),
        g_query,
        g_key,
        g_value,
        g_out,
        g_gate,
        g_up,
        g_down,
    )


def solution(mesh):
    cube = Mesh(mesh.devices.reshape(4, 2, 4, 2, 2), ("y", "xh", "z", "xl", "c"))
    fsdp, ctx = ("xl", "c"), ("y", "xh", "z")
    return jax.shard_map(
        body,
        mesh=cube,
        in_specs=(
            P(fsdp, ctx, None),
            P(),
            P(fsdp),
            P(fsdp),
            P(fsdp, None),
            P(fsdp, None),
            P(fsdp, None),
            P(fsdp, None),
            P(None, fsdp),
            P(None, fsdp),
            P(fsdp, None),
            P(fsdp, ctx, None),
        ),
        out_specs=(
            P(fsdp, ctx, None),
            P(fsdp, ctx, None),
            P(fsdp),
            P(fsdp),
            P(fsdp, None),
            P(fsdp, None),
            P(fsdp, None),
            P(fsdp, None),
            P(None, fsdp),
            P(None, fsdp),
            P(fsdp, None),
        ),
        check_vma=False,
    )
```

```python
import functools

import jax
import jax.numpy as jnp
from jax import lax
from jax.experimental import pallas as pl
from jax.experimental.pallas import tpu as pltpu
from jax.sharding import Mesh, PartitionSpec as P

D = 1536
HEADS = 16
KV_HEADS = 8
HEAD_DIM = 96
HALF = HEAD_DIM // 2
FF = 4096
BLOCK = 64
SEQ = 4096
WINDOW_BLOCKS = 32
SHARDS = 4
ROWS = 128
TOK = SHARDS * ROWS
DS = D // SHARDS
FS = FF // SHARDS
EPS = 1e-05
ROPE_BASE = 10000.0
MASKED = -1e30
SCALE = HEAD_DIM ** (-0.5)
LOG2E = 1.4426950408889634
BF = jnp.bfloat16
F32 = jnp.float32

CHUNK_BLOCKS = 8
CHUNK = CHUNK_BLOCKS * BLOCK

SMEM_SPEC = pl.BlockSpec(memory_space=pltpu.SMEM)
VMEM_SPEC = pl.BlockSpec(memory_space=pltpu.VMEM)
ANY_SPEC = pl.BlockSpec(memory_space=pl.ANY)
PARAMS = pltpu.CompilerParams(vmem_limit_bytes=60 * 1024 * 1024)


def cost(us):
    flops, nbytes = int(us * 1_100_000_000), int(us * 3_000_000)
    return pl.CostEstimate(flops=flops, bytes_accessed=nbytes, transcendentals=0)


def call(kernel, outs, smem, vmem, us, scratch=(), deps=()):
    n, d = len(smem) + len(vmem), len(deps)

    def body(*refs):
        kernel(*refs[:n], *refs[n + d :])

    return pl.pallas_call(
        body,
        out_shape=outs,
        in_specs=[SMEM_SPEC] * len(smem) + [VMEM_SPEC] * len(vmem) + [ANY_SPEC] * d,
        out_specs=jax.tree.map(lambda _: VMEM_SPEC, outs),
        scratch_shapes=list(scratch),
        compiler_params=PARAMS,
        cost_estimate=cost(us),
        name=getattr(kernel, "__name__", "part"),
    )(*smem, *vmem, *deps)


def sds(shape, dtype=BF):
    return jax.ShapeDtypeStruct(shape, dtype)


def dot(a, b):
    return jnp.dot(a, b, preferred_element_type=F32)


def dot_t(a, b):
    return lax.dot_general(a, b, (((1,), (1,)), ((), ())), preferred_element_type=F32)


def t_dot(a, b):
    return lax.dot_general(a, b, (((0,), (0,)), ((), ())), preferred_element_type=F32)


def swap_c(x):
    return lax.ppermute(x, "c", [(0, 1), (1, 0)])


def swap_xl(x):
    return lax.ppermute(x, "xl", [(0, 1), (1, 0)])


def swap_both(x):
    return lax.ppermute(x, ("xl", "c"), [(i, i ^ 3) for i in range(4)])


def swap_far(x, core):
    pairs = []
    for place in range(4):
        other = (place + 1) % 4 if place % 2 else (place + 3) % 4
        for c in range(2):
            pairs.append((place * 2 + c, other * 2 + (c ^ core)))
    return lax.ppermute(x, ("xh", "xl", "c"), pairs)


def swap_e(x):
    return lax.ppermute(x, "xh", [(0, 1), (1, 0)])


NEAR = [(0, 1), (1, 0), (2, 3), (3, 2)]
AROUND = [(1, 2), (2, 1), (0, 3), (3, 0)]
CUBE = (("y", NEAR), ("y", AROUND), ("z", NEAR), ("z", AROUND))


def swap_cube(x, dim):
    axis, pairs = CUBE[dim % 4]
    return lax.ppermute(x, axis, pairs)


def from_z(x, m):
    return lax.ppermute(x, "z", [((i + m) % 4, i) for i in range(4)])


def to_z(x, m):
    return lax.ppermute(x, "z", [(i, (i + m) % 4) for i in range(4)])


def gather_slots(own):
    far = swap_xl(own)
    return own, swap_c(own), far, swap_c(far)


def scatter_slots(keep, send):
    got = swap_c(send)
    other = (keep[1].astype(F32) + got[1].astype(F32)).astype(BF)
    return (keep, got, swap_xl(other)), other


CTX = ("y", "xh", "z")
FSDP = ("xl", "c")


def after(x, other):
    return lax.optimization_barrier((x, other))[0]


def shifts(x, axis):
    return [lax.ppermute(x, axis, [((i + m) % 4, i) for i in range(4)]) for m in (1, 2, 3)]


def exchange(x, axes):
    return lax.all_to_all(x, axes, 0, 0, tiled=True)


def cube_index(portion, bits):
    out = 0
    for t in range(4):
        out = out * 2 + bits[(portion + t) % 4]
    return out


def fold(x):
    tail = jnp.concatenate([x[0:64, 128:192], x[64:128, 128:192]], axis=1)
    return jnp.concatenate([x[:, 0:128], tail], axis=0)


def unfold(x):
    tail = jnp.concatenate([x[128:192, 0:64], x[128:192, 64:128]], axis=0)
    return jnp.concatenate([x[0:128], tail], axis=1)


def pack_kernel(sc, wq, wk, wv, gains, q0, q1, q2, q3, k0, k1, k2, k3, tmp):
    f = sc[0]
    for g in range(4):
        tmp[g, :, 0:192] = wk[:, 192 * g : 192 * (g + 1)]
        tmp[g, :, 192:384] = wv[:, 192 * g : 192 * (g + 1)]
    for k, (q, kv) in enumerate(((q0, k0), (q1, k1), (q2, k2), (q3, k3))):
        q[...] = wq[:, pl.ds(pl.multiple_of((f ^ k) * DS, 128), DS)]
        kv[0:DS] = tmp[f ^ k]
        kv[DS:] = gains[...]


def project(f, xa, ws):
    total = jnp.zeros((TOK, DS), F32)
    for k, w in enumerate(ws):
        at = pl.multiple_of((f ^ k) * DS, 128)
        total = total + dot(xa[:, pl.ds(at, DS)], w[0:DS])
    return total


def rotate(u, co, si):
    turned = jnp.concatenate([-u[:, HALF:], u[:, :HALF]], axis=1)
    return u * co + turned * si


def kv_kernel(sc, x0, x1, x2, x3, k0, k1, k2, k3, cos, sin, xa, kv, gain_a, gain_m):
    f = sc[0]
    for k, w in enumerate((k0, k1, k2, k3)):
        at = pl.ds(pl.multiple_of((f ^ k) * DS, 128), DS)
        rows = w[DS:].astype(F32)
        gain_a[:, at] = rows[0:1]
        gain_m[:, at] = rows[1:2]
    for k, x in enumerate((x0, x1, x2, x3)):
        u = x[...].astype(F32)
        r = lax.rsqrt(jnp.mean(u * u, axis=-1, keepdims=True) + EPS)
        xa[ROWS * k : ROWS * (k + 1), :] = (u * r * gain_a[...]).astype(BF)
    lin = project(f, xa, [w[0:DS] for w in (k0, k1, k2, k3)])
    co, si = cos[...], sin[...]
    for k in range(4):
        part = lin[ROWS * k : ROWS * (k + 1)]
        for j in range(2):
            key = rotate(part[:, 96 * j : 96 * (j + 1)], co, si)
            value = part[:, 192 + 96 * j : 192 + 96 * (j + 1)]
            kv[2 * k + j] = fold(jnp.concatenate([key, value], axis=1)).astype(BF)


def q_kernel(sc, xa, w0, w1, w2, w3, cos, sin, q):
    lin = project(sc[0], xa, (w0, w1, w2, w3))
    co, si = cos[...], sin[...]
    for k in range(4):
        part = lin[ROWS * k : ROWS * (k + 1)]
        heads = [rotate(part[:, 96 * h : 96 * (h + 1)], co, si) for h in range(4)]
        for j in range(2):
            q[2 * k + j] = fold(jnp.concatenate(heads[2 * j : 2 * j + 2], axis=1)).astype(BF)


def widen(x, *tail):
    zeros = jnp.zeros((x.shape[0], 128 - x.shape[1] - len(tail)), x.dtype)
    return jnp.concatenate([x, *tail, zeros], axis=1)


def stacked(x, t):
    rows = slice(BLOCK * t, BLOCK * (t + 1))
    return jnp.concatenate([x[rows, 0:96], x[rows, 96:192]], axis=0)


def side_by_side(a, b):
    rows = [jnp.concatenate([x[0:BLOCK, 0:96], x[BLOCK:, 0:96]], axis=1) for x in (a, b)]
    return fold(jnp.concatenate(rows, axis=0))


def low_high(qb, n):
    swapped = (qb[2 * n] >= WINDOW_BLOCKS).astype(jnp.int32)
    return 2 * n + swapped, 2 * n + 1 - swapped


def attention_kernel(qb, kb, q, kv0, kv1, kv2, kv3, o, o2, q2, lse, kv):
    ones = (lax.broadcasted_iota(jnp.int32, (BLOCK, 32), 1) < 4).astype(F32)

    def place(s, _):
        for m, ref in enumerate((kv0, kv1, kv2, kv3)):
            x = unfold(ref[s].astype(F32))
            for t in range(2):
                dst = pl.ds(pl.multiple_of(kb[m * 16 + 2 * s + t] * BLOCK, BLOCK), BLOCK)
                part = x[BLOCK * t : BLOCK * (t + 1)]
                both = jnp.concatenate([part[:, 0:96], ones, part[:, 96:192], ones], axis=1)
                kv[dst, :] = both.astype(BF)
        x = unfold(q[s].astype(F32))
        for t in range(2):
            q2[2 * s + t] = widen(stacked(x, t)).astype(BF)
        return 0

    lax.fori_loop(0, 8, place, 0)
    two = SCALE * LOG2E

    def scores(n, spans):
        return [dot_t(q2[n], kv[span, 0:128]) for span in spans]

    def finish(n, parts, spans):
        tops = [jnp.max(s, axis=1, keepdims=True) for s in parts]
        top = functools.reduce(jnp.maximum, tops) * two
        acc = jnp.zeros((ROWS, 128), F32)
        for s, span in zip(parts, spans):
            acc += dot(jnp.exp2(s * two - top).astype(BF), kv[span, 128:256])
        total = acc[:, 96:97]
        o2[n] = (acc / total).astype(BF)
        lse[n] = jnp.broadcast_to(top + jnp.log2(total), (ROWS, 8))

    def pair(n, _):
        low, high = low_high(qb, n)
        i_low, i_high = qb[low], qb[high]
        for count in range(1, 5):

            @pl.when(i_low // CHUNK_BLOCKS == count - 1)
            def _():
                edge = pl.ds(pl.multiple_of((i_high - WINDOW_BLOCKS) * BLOCK, BLOCK), BLOCK)
                at = pl.multiple_of((i_high - WINDOW_BLOCKS + 1) * BLOCK, BLOCK)
                spans_h = [edge] + [pl.ds(at + CHUNK * t, CHUNK) for t in range(4)]
                spans_l = [pl.ds(CHUNK * t, CHUNK) for t in range(count)]
                high_s = scores(high, spans_h)
                low_s = scores(low, spans_l)
                key = lax.broadcasted_iota(jnp.int32, (ROWS, BLOCK), 1)
                query = lax.broadcasted_iota(jnp.int32, (ROWS, BLOCK), 0) % BLOCK
                high_s[0] = jnp.where(key > query, high_s[0], MASKED)
                key = lax.broadcasted_iota(jnp.int32, (ROWS, CHUNK), 1)
                limit = (i_low + 1) * BLOCK - CHUNK * (count - 1)
                low_s[-1] = jnp.where(key < limit, low_s[-1], MASKED)
                finish(high, high_s, spans_h)
                finish(low, low_s, spans_l)

        return 0

    lax.fori_loop(0, 8, pair, 0)

    def gather(s, _):
        o[s] = side_by_side(o2[2 * s].astype(F32), o2[2 * s + 1].astype(F32)).astype(BF)
        return 0

    lax.fori_loop(0, 8, gather, 0)


def attention_back_kernel(qb, kb, q2s, d_o, o2s, lse, kv, dq2s, g, dkv, do2s):
    dkv[...] = jnp.zeros_like(dkv)

    def place(s, _):
        x = unfold(d_o[s].astype(F32))
        for t in range(2):
            do2s[2 * s + t] = stacked(x, t).astype(BF)
        return 0

    lax.fori_loop(0, 8, place, 0)
    two = SCALE * LOG2E

    def split(x):
        parts = []
        for _ in range(3):
            parts.append(x.astype(BF))
            x = x - parts[-1].astype(F32)
        return parts

    def weights(n):
        do2 = do2s[n]
        inner = do2.astype(F32) * o2s[n][:, 0:96].astype(F32)
        inner = jnp.sum(inner, axis=1, keepdims=True)
        q2 = widen(q2s[n][:, 0:96], *split(lse[n][:, 0:1] * (-1.0 / two)))
        do2 = widen(do2, *split(-inner))
        none = jnp.zeros((ROWS, 128), BF)
        return jnp.concatenate(
            [jnp.concatenate([q2, none], axis=1), jnp.concatenate([none, do2], axis=1)], axis=0
        )

    def factors(w, spans, masks):
        pairs = []
        for span, mask in zip(spans, masks):
            s = dot_t(kv[span, :], w)
            p = jnp.exp2(s[:, 0:128] * two)
            if mask is not None:
                p = jnp.where(mask, p, 0.0)
            ds = (p * s[:, 128:256]).astype(BF)
            pairs.append(jnp.concatenate([ds, p.astype(BF)], axis=1))
        return pairs

    def add(n, w, spans, pairs):
        acc = jnp.zeros((ROWS, 128), F32)
        for span, both in zip(spans, pairs):
            dkv[span, :] += dot(both, w)
            acc += t_dot(both[:, 0:128], kv[span, 0:128])
        dq2s[n] = (acc * SCALE).astype(BF)

    def pair(n, _):
        low, high = low_high(qb, n)
        i_low, i_high = qb[low], qb[high]
        for count in range(1, 5):

            @pl.when(i_low // CHUNK_BLOCKS == count - 1)
            def _():
                edge = pl.ds(pl.multiple_of((i_high - WINDOW_BLOCKS) * BLOCK, BLOCK), BLOCK)
                at = pl.multiple_of((i_high - WINDOW_BLOCKS + 1) * BLOCK, BLOCK)
                key = lax.broadcasted_iota(jnp.int32, (BLOCK, ROWS), 0)
                query = lax.broadcasted_iota(jnp.int32, (BLOCK, ROWS), 1) % BLOCK
                spans_h = [edge] + [pl.ds(at + CHUNK * t, CHUNK) for t in range(4)]
                masks_h = [key > query] + [None] * 4
                spans_l = [pl.ds(CHUNK * t, CHUNK) for t in range(count)]
                key = lax.broadcasted_iota(jnp.int32, (CHUNK, ROWS), 0)
                limit = (i_low + 1) * BLOCK - CHUNK * (count - 1)
                masks_l = [None] * (count - 1) + [key < limit]
                w_h, w_l = weights(high), weights(low)
                pairs_h = factors(w_h, spans_h, masks_h)
                pairs_l = factors(w_l, spans_l, masks_l)
                add(high, w_h, spans_h, pairs_h)
                add(low, w_l, spans_l, pairs_l)

        return 0

    lax.fori_loop(0, 8, pair, 0)

    def keys(s, _):
        parts = []
        for t in range(2):
            src = pl.ds(pl.multiple_of(kb[2 * s + t] * BLOCK, BLOCK), BLOCK)
            both = dkv[src, :]
            parts.append(jnp.concatenate([both[:, 0:96] * SCALE, both[:, 128:224]], axis=1))
        g[s] = fold(jnp.concatenate(parts, axis=0)).astype(BF)
        return 0

    lax.fori_loop(0, 32, keys, 0)


def fold_dq_kernel(dq2s, dq):
    for s in range(8):
        dq[s] = side_by_side(dq2s[2 * s].astype(F32), dq2s[2 * s + 1].astype(F32)).astype(BF)


def unfolded(o):
    return unfold(o.astype(F32)).astype(BF)


def out_kernel(o, w, keep, send):
    for k in range(4):
        total = dot(unfolded(o[2 * k]), w[0:192, :]) + dot(unfolded(o[2 * k + 1]), w[192:384, :])
        (keep, send)[k % 2][k // 2] = total.astype(BF)


def hidden_kernel(x, keep, got, far, gain, hidden, xm):
    h = x[...].astype(F32) + keep[0].astype(F32) + got[0].astype(F32) + far[...].astype(F32)
    hidden[...] = h
    r = lax.rsqrt(jnp.mean(h * h, axis=-1, keepdims=True) + EPS)
    xm[...] = (h * r * gain[...]).astype(BF)


def norm_back(values, gain, grads):
    factor = lax.rsqrt(jnp.mean(values * values, axis=-1, keepdims=True) + EPS)
    weighted = grads * gain
    inner = jnp.mean(weighted * values, axis=-1, keepdims=True)
    return factor * weighted - values * (factor * factor * factor) * inner


def d_hidden_kernel(dy, keep, got, far, hidden, gain, d_hidden, d_br, d_gain):
    grads = keep[0].astype(F32) + got[0].astype(F32) + far[...].astype(F32)
    h = hidden[...]
    d = dy[...].astype(F32) + norm_back(h, gain[...], grads)
    d_hidden[...] = d
    d_br[...] = d.astype(BF)
    r = lax.rsqrt(jnp.mean(h * h, axis=-1, keepdims=True) + EPS)
    total = jnp.sum(grads * h * r, axis=0, keepdims=True)
    rows = [total[:, 128 * t : 128 * (t + 1)] for t in range(12)]
    d_gain[...] = jnp.concatenate(rows + [jnp.zeros((4, 128), F32)], axis=0).astype(BF)


def pair_kernel(keep, got, out):
    out[...] = (keep[2:].astype(F32) + got[2:].astype(F32)).astype(BF)


def last_kernel(x, keep, got, far, hidden, d_hidden, gain, layer_out, d_tokens):
    total = keep[0].astype(F32) + got[0].astype(F32) + far[0].astype(F32)
    layer_out[...] = (hidden[...] + total).astype(BF)
    grads = keep[1].astype(F32) + got[1].astype(F32) + far[1].astype(F32)
    d_tokens[...] = d_hidden[...] + norm_back(x[...].astype(F32), gain[...], grads)


def d_o_kernel(b0, b1, b2, b3, w, d_o):
    for k, b in enumerate((b0, b1, b2, b3)):
        d = dot_t(b[...], w[...])
        d_o[2 * k] = fold(d[:, 0:192]).astype(BF)
        d_o[2 * k + 1] = fold(d[:, 192:384]).astype(BF)


FBLOCK = 512


def d_act_kernel(y0, y1, y2, y3, wd, da):
    ys = jnp.concatenate([y0[...], y1[...], y2[...], y3[...]], axis=0)
    da[...] = dot_t(ys, wd[...])


def ffn_kernel(sc, x0, x1, x2, x3, da, wg, wu, act, dg, du, keep, send, xs, acc):
    n = pl.program_id(0)

    @pl.when(n == 0)
    def _():
        for k, x in enumerate((x0, x1, x2, x3)):
            xs[ROWS * k : ROWS * (k + 1), :] = x[...]

    gate = dot(xs[...], wg[...])
    up = dot(xs[...], wu[...])
    d = da[...]
    sg = jax.nn.sigmoid(gate)
    both = gate * sg
    a = (both * up).astype(BF)
    d_gate = (d * up * sg * (1.0 + gate * (1.0 - sg))).astype(BF)
    d_up = (d * both).astype(BF)
    for h in range(2):
        at = pl.multiple_of((h ^ (sc[2] & 1)) * 256, 256)
        for ref, tile in ((act, a), (dg, d_gate), (du, d_up)):
            ref[:, pl.ds(at, 256)] = tile[:, 256 * h : 256 * (h + 1)]
    dx = dot_t(d_gate, wg[...]) + dot_t(d_up, wu[...])

    @pl.when(n == 0)
    def _():
        acc[...] = dx

    @pl.when(n > 0)
    def _():
        total = acc[...] + dx
        for k in range(4):
            (keep, send)[k % 2][k // 2] = total[ROWS * k : ROWS * (k + 1), :].astype(BF)


def ffn(sc, xs, da, wg, wu):
    full = pl.BlockSpec((ROWS, D), lambda n, s: (0, 0))
    side = pl.BlockSpec((2, ROWS, D), lambda n, s: (0, 0, 0))
    cols = pl.BlockSpec((D, FBLOCK), lambda n, s: (0, n))
    rel = pl.BlockSpec((TOK, FBLOCK), lambda n, s: (0, n ^ (s[2] >> 1)))
    return pl.pallas_call(
        ffn_kernel,
        grid_spec=pltpu.PrefetchScalarGridSpec(
            num_scalar_prefetch=1,
            grid=(FS // FBLOCK,),
            in_specs=[full] * 4 + [pl.BlockSpec((TOK, FBLOCK), lambda n, s: (0, n)), cols, cols],
            out_specs=[rel, rel, rel, side, side],
            scratch_shapes=[pltpu.VMEM((TOK, D), BF), pltpu.VMEM((TOK, D), F32)],
        ),
        out_shape=[sds((TOK, FS))] * 3 + [sds((2, ROWS, D))] * 2,
        compiler_params=PARAMS,
        cost_estimate=cost(11),
    )(sc, *xs, da, wg, wu)


def mlp_out_kernel(sc, act, wd, keep_in, send_in, keep, send):
    gz = sc[2]
    acts = [
        act[:, pl.ds(pl.multiple_of((b ^ gz) * 256, 256), 256)] for b in range(FS // 256)
    ]
    total = dot(jnp.concatenate(acts, axis=1), wd[...])
    for k in range(4):
        (keep, send)[k % 2][2 * (k // 2)] = total[ROWS * k : ROWS * (k + 1)].astype(BF)
    for k in range(2):
        keep[2 * k + 1] = keep_in[k]
        send[2 * k + 1] = send_in[k]


def ffn_grads_kernel(sc, x0, x1, x2, x3, y0, y1, y2, y3, act, dg, du, *refs):
    gy = sc[1]
    keeps, sends, ys = refs[:4], refs[4:8], refs[8]

    def put(p, ra, rb, at, tile):
        index = cube_index(p, (ra & 1, ra >> 1, rb & 1, rb >> 1))
        ref = (keeps, sends)[index >> 3][p]
        ref[index & 7, at : at + tile.shape[0], :] = tile.astype(BF)

    for ra in range(4):
        cols = pl.ds(pl.multiple_of((ra ^ gy) * DS, 128), DS)
        xa = jnp.concatenate([x[:, cols] for x in (x0, x1, x2, x3)], axis=0)
        for k, y in enumerate((y0, y1, y2, y3)):
            ys[ROWS * k : ROWS * (k + 1), DS * ra : DS * (ra + 1)] = y[:, cols]
        for n, d in enumerate((dg, du)):
            wide = t_dot(xa, d[...])
            for rb in range(4):
                for p in range(4):
                    lane, row = 256 * rb + 128 * (p // 2), 192 * (p % 2)
                    put(p, ra, rb, 192 * n, wide[row : row + 192, lane : lane + 128])
    for rb in range(4):
        wide = t_dot(act[:, 256 * rb : 256 * (rb + 1)], ys[...])
        for ra in range(4):
            for p in range(4):
                at = 384
                row = 192 * p
                while row < 192 * (p + 1):
                    lane, r = DS * ra + 128 * (row // 256), row % 256
                    size = min(256 - r, 192 * (p + 1) - row)
                    put(p, ra, rb, at, wide[r : r + size, lane : lane + 128])
                    at += size
                    row += size


OUT_ROWS = 288
OUT_SPLIT = (80, 80, 64, 64)
OUT_AT = (0, 80, 160, 224)
PART_ROWS = tuple(576 + n for n in OUT_SPLIT)
PART_AT = (0, 656, 1312, 1952)
GAIN_AT = 2592


def first_step(keeps, gots, deps, us):
    def body(*refs):
        for p in range(4):
            k, g, out = refs[2 * p], refs[2 * p + 1], refs[8 + len(deps) + p]
            out[...] = (k[...].astype(F32) + g[...].astype(F32)).astype(BF)

    args = [x for pair in zip(keeps, gots) for x in pair]
    return pl.pallas_call(
        body,
        grid=(4,),
        in_specs=[pl.BlockSpec((1, 576, 128), lambda n: (n + 4, 0, 0))] * 8
        + [ANY_SPEC] * len(deps),
        out_specs=[pl.BlockSpec((1, 576, 128), lambda n: (n, 0, 0))] * 4,
        out_shape=[sds((4, 576, 128))] * 4,
        compiler_params=PARAMS,
        cost_estimate=cost(us),
    )(*args, *deps)


def cube_step(terms, deps, us):
    count = len(terms[0])
    half = terms[0][-1].shape[0] // 2
    lower = pl.BlockSpec((1, 576, 128), lambda n: (n, 0, 0))
    upper = pl.BlockSpec((1, 576, 128), lambda n: (n + half, 0, 0))
    used = 8 * count

    def body(*refs):
        outs = refs[used + len(deps) :]
        for p in range(4):
            mine = refs[2 * count * p : 2 * count * (p + 1)]
            for side in range(2):
                total = mine[side][...].astype(F32)
                for t in range(1, count):
                    total += mine[2 * t + side][...].astype(F32)
                outs[2 * p + side][...] = total.astype(BF)

    args = [x for portion in terms for term in portion for x in (term, term)]
    outs = pl.pallas_call(
        body,
        grid=(half,),
        in_specs=[lower, upper] * (4 * count) + [ANY_SPEC] * len(deps),
        out_specs=[lower] * 8,
        out_shape=[sds((half, 576, 128))] * 8,
        compiler_params=PARAMS,
        cost_estimate=cost(us),
    )(*args, *deps)
    return outs[0::2], outs[1::2]


def last_step_kernel(k0, k1, k2, k3, g0, g1, g2, g3, out, total):
    for p, (k, g) in enumerate(((k0, g0), (k1, g1), (k2, g2), (k3, g3))):
        at = PART_AT[p]
        total[at : at + 576, :] = (k[0].astype(F32) + g[0].astype(F32)).astype(BF)
        total[at + 576 : at + PART_ROWS[p], :] = out[OUT_AT[p] : OUT_AT[p] + OUT_SPLIT[p]]
    total[GAIN_AT:, :] = out[OUT_ROWS:]


def join_kernel(own, got, p0, p1, p2, p3, gains):
    total = own[...].astype(F32) + got[...].astype(F32)
    for p, ref in enumerate((p0, p1, p2, p3)):
        ref[0] = total[PART_AT[p] : PART_AT[p] + PART_ROWS[p]].astype(BF)
    gains[...] = total[GAIN_AT:]


def stack_kernel(a0, a1, a2, a3, b0, b1, b2, b3, o0, o1, o2, o3):
    for a, b, o in ((a0, b0, o0), (a1, b1, o1), (a2, b2, o2), (a3, b3, o3)):
        o[0 : a.shape[0]] = a[...]
        o[a.shape[0] :] = b[...]


def cube_gather(owns, gots, us, deps):
    outs = [sds((2 * o.shape[0], *o.shape[1:])) for o in owns]
    return call(stack_kernel, outs, [], [*owns, *gots], us, deps=deps)


def pick(owns, gots, p, bits, rows):
    index = cube_index(p, bits)
    rest = index & 7
    return jnp.where(index >= 8, gots[p][rest, rows, :], owns[p][rest, rows, :])


def ffn_place_kernel(sc, *refs):
    owns, gots = refs[0:4], refs[4:8]
    gate, up, down, out, tmp = refs[8:]
    gy, gz = sc[1], sc[2]
    ra = pl.program_id(0) ^ gy
    for bb in range(4):
        rb = bb ^ gz
        bits = (ra & 1, ra >> 1, rb & 1, rb >> 1)
        for p in range(4):
            lane, row = 256 * bb + 128 * (p // 2), 192 * (p % 2)
            for n, ref in enumerate((gate, up)):
                tile = pick(owns, gots, p, bits, slice(192 * n, 192 * (n + 1)))
                ref[row : row + 192, lane : lane + 128] = tile.astype(F32)
            at, row = 384, 192 * p
            while row < 192 * (p + 1):
                lane, r = row // 256, row % 256
                size = min(256 - r, 192 * (p + 1) - row)
                tile = pick(owns, gots, p, bits, slice(at, at + size))
                down[256 * bb + r : 256 * bb + r + size, 128 * lane : 128 * (lane + 1)] = (
                    tile.astype(F32)
                )
                at += size
                row += size
            at = OUT_ROWS * (bb ^ (bb >> 1)) + OUT_AT[p]
            tile = pick(owns, gots, p, bits, slice(576, PART_ROWS[p]))
            tmp[at : at + OUT_SPLIT[p], :] = tile.astype(F32)
    for t in range(3):
        out[:, 128 * t : 128 * (t + 1)] = tmp[DS * t : DS * (t + 1), :]


def ffn_place(sc, owns, gots, deps):
    def body(*refs):
        ffn_place_kernel(*refs[:9], *refs[9 + len(deps) :])

    whole = [pl.BlockSpec((8, n, 128), lambda n, s: (0, 0, 0)) for n in PART_ROWS]
    rows = pl.BlockSpec((DS, FS), lambda n, s: (n, 0))
    return pl.pallas_call(
        body,
        grid_spec=pltpu.PrefetchScalarGridSpec(
            num_scalar_prefetch=1,
            grid=(4,),
            in_specs=whole * 2 + [ANY_SPEC] * len(deps),
            out_specs=[
                rows,
                rows,
                pl.BlockSpec((FS, DS), lambda n, s: (0, n)),
                pl.BlockSpec((DS, DS), lambda n, s: (0, n ^ (n >> 1))),
            ],
            scratch_shapes=[pltpu.VMEM((4 * OUT_ROWS, 128), F32)],
        ),
        out_shape=[sds((D, FS), F32), sds((D, FS), F32), sds((FS, D), F32), sds((DS, D), F32)],
        compiler_params=PARAMS,
        cost_estimate=cost(60),
    )(sc, *owns, *gots, *deps)


def out_grads_kernel(o, b0, b1, b2, b3, d_gain, pieces, tmp):
    bs = jnp.concatenate([b0[...], b1[...], b2[...], b3[...]], axis=0)
    for j in range(2):
        oj = jnp.concatenate([unfolded(o[2 * k + j]) for k in range(4)], axis=0)
        tmp[192 * j : 192 * (j + 1), :] = t_dot(oj, bs)
    for s in range(16):
        pieces[s, OUT_ROWS:, :] = d_gain[...]
        start, at = OUT_ROWS * s, 0
        while start < OUT_ROWS * (s + 1):
            lane, r = 128 * (start // DS), start % DS
            size = min(DS - r, OUT_ROWS * (s + 1) - start)
            pieces[s, at : at + size, :] = tmp[r : r + size, lane : lane + 128].astype(BF)
            at += size
            start += size


def sum_kernel(parts, out):
    out[...] = jnp.sum(parts[...].astype(F32), axis=0).astype(BF)


def sum_shards_kernel(parts, gains, out):
    for g in range(4):
        total = parts[0, g].astype(F32)
        for n in range(1, 32):
            total += parts[n, g].astype(F32)
        rows = [total, gains[3 * g : 3 * g + 3, :], jnp.zeros((5, 128), F32)]
        out[g] = jnp.concatenate(rows, axis=0).astype(BF)


def repeat_kernel(parts, out, gain):
    whole = parts[...].astype(F32)
    gain[...] = jnp.sum(whole[:, QKV_ROWS:], axis=0)
    mine = whole[:, :QKV_ROWS].astype(BF)
    for n in range(32):
        out[n] = mine


QKV_ROWS = 72


def d_xa_kernel(sc, d_q, d_kv, q0, q1, q2, q3, k0, k1, k2, k3, cos, sin, lin, keep, send, dq, dkv):
    f = sc[0]
    co, si = cos[...], sin[...]

    def back(g):
        w = g * si
        turned = jnp.concatenate([w[:, HALF:], -w[:, :HALF]], axis=1)
        return (g * co + turned).astype(BF)

    for k in range(4):
        rows = slice(ROWS * k, ROWS * (k + 1))
        for j in range(2):
            i = 2 * k + j
            gq = unfold(d_q[i].astype(F32))
            gkv = d_kv[4 * i].astype(F32)
            for z in range(1, 4):
                gkv += d_kv[4 * i + z].astype(F32)
            gkv = unfold(gkv)
            for n in range(2):
                g = back(gq[:, 96 * n : 96 * (n + 1)])
                lin[rows, 384 * j + 96 * n : 384 * j + 96 * (n + 1)] = g
                dq[rows, 192 * j + 96 * n : 192 * j + 96 * (n + 1)] = g
            g = back(gkv[:, 0:96])
            lin[rows, 384 * j + 192 : 384 * j + 288] = g
            dkv[rows, 96 * j : 96 * (j + 1)] = g
            g = gkv[:, 96:192].astype(BF)
            lin[rows, 384 * j + 288 : 384 * j + 384] = g
            dkv[rows, 192 + 96 * j : 192 + 96 * (j + 1)] = g
    for k, (wq, wkv) in enumerate(((q0, k0), (q1, k1), (q2, k2), (q3, k3))):
        cols = pl.ds(pl.multiple_of((f ^ k) * DS, 128), DS)
        total = (dot_t(dq[...], wq[...]) + dot_t(dkv[...], wkv[0:DS])).astype(BF)
        for s in range(4):
            (keep, send)[s % 2][s // 2, :, cols] = total[ROWS * s : ROWS * (s + 1)]


def flat_pieces(n):
    out, start = [], QKV_ROWS * n
    while start < QKV_ROWS * (n + 1):
        r = start % DS
        size = min(DS - r, QKV_ROWS * (n + 1) - start)
        out.append((128 * (start // DS), r, size))
        start += size
    return out


def qkv_grads_kernel(xa, lin, pieces, tmp):
    for g in range(4):
        tmp[...] = t_dot(xa[:, DS * g : DS * (g + 1)], lin[...])
        for n in range(32):
            tiles = [tmp[r : r + size, lane : lane + 128] for lane, r, size in flat_pieces(n)]
            pieces[n, g] = jnp.concatenate(tiles, axis=0).astype(BF)


def attn_place_kernel(got, wq, wk, wv, gain_in, q, k, v, gain, tmp):
    for g in range(4):
        for n in range(32):
            tile, at = got[n, g].astype(F32), 0
            for lane, r, size in flat_pieces(n):
                tmp[r : r + size, lane : lane + 128] = tile[at : at + size]
                at += size
        for j in range(2):
            at = 384 * j
            q[:, 384 * g + 192 * j : 384 * g + 192 * (j + 1)] = tmp[:, at : at + 192]
            k[:, 192 * g + 96 * j : 192 * g + 96 * (j + 1)] = tmp[:, at + 192 : at + 288]
            v[:, 192 * g + 96 * j : 192 * g + 96 * (j + 1)] = tmp[:, at + 288 : at + 384]
    total = jnp.sum(wq[...].astype(F32) * q[...], axis=1, keepdims=True)
    total += jnp.sum(wk[...].astype(F32) * k[...], axis=1, keepdims=True)
    total += jnp.sum(wv[...].astype(F32) * v[...], axis=1, keepdims=True)
    gain[...] = jnp.broadcast_to(total, (DS, 128)).T[0:1] / gain_in[...]


def rope_tables(positions):
    freqs = ROPE_BASE ** (-jnp.arange(HALF).astype(F32) * 2.0 / HEAD_DIM)
    angles = positions.astype(F32)[:, None] * freqs[None, :]
    angles = jnp.concatenate([angles, angles], axis=1)
    return jnp.cos(angles), jnp.sin(angles)


def body(
    tokens,
    block_order,
    gain_attn,
    gain_mlp,
    w_query,
    w_key,
    w_value,
    w_out,
    w_gate,
    w_up,
    w_down,
    cotangent,
):
    y, xh, z = lax.axis_index("y"), lax.axis_index("xh"), lax.axis_index("z")
    xl, c = lax.axis_index("xl"), lax.axis_index("c")
    f = xl * 2 + c
    gy, gz = y ^ (y >> 1), z ^ (z >> 1)
    sc = jnp.stack([f, gy, gz]).astype(jnp.int32)
    own_x, own_dy = tokens[0], cotangent[0]

    place = (y * 2 + xh) * 4 + z
    own_blocks = lax.dynamic_slice_in_dim(block_order, 2 * place, 2)
    positions = (own_blocks[:, None] * BLOCK + jnp.arange(BLOCK)).reshape(-1)
    cos, sin = rope_tables(positions)
    blocks = block_order.reshape(8, 4, 2)
    key_blocks = jnp.stack(
        [
            lax.dynamic_index_in_dim(blocks, (z + m) % 4, axis=1, keepdims=False).reshape(-1)
            for m in range(4)
        ]
    ).reshape(-1)
    query_blocks = key_blocks[:16]

    xs = gather_slots(own_x)
    packs = call(
        pack_kernel,
        [sds((DS, DS))] * 4 + [sds((DS + 16, DS))] * 4,
        [sc],
        [w_query, w_key, w_value, jnp.pad(jnp.stack([gain_attn, gain_mlp]), ((0, 14), (0, 0)))],
        3,
        [pltpu.VMEM((4, DS, DS), BF)],
    )
    wkvs = (packs[4], swap_c(packs[5]), swap_xl(packs[6]), swap_far(packs[7], 1))
    wqs = (packs[0], swap_c(packs[1]), swap_far(packs[2], 0), swap_far(packs[3], 1))

    folded, heads = (8, 192, 128), ("y", "xh")
    xa, kv, gain_a, gain_m = call(
        kv_kernel,
        [sds((TOK, D)), sds(folded), sds((1, D), F32), sds((1, D), F32)],
        [sc],
        [*xs, *wkvs, cos, sin],
        5,
    )
    q = call(q_kernel, sds(folded), [sc], [xa, *wqs, cos, sin], 4)
    kv = exchange(kv, heads)
    kvs = shifts(kv, "z")
    q = exchange(q, heads)
    o, o2, q2, lse, kv_sorted = call(
        attention_kernel,
        [
            sds(folded),
            sds((16, ROWS, 128)),
            sds((16, ROWS, 128)),
            sds((16, ROWS, 8), F32),
            sds((SEQ, 256)),
        ],
        [query_blocks, key_blocks],
        [q, kv, *kvs],
        13,
    )
    o_tok = exchange(o, heads)

    dys = gather_slots(own_dy)
    d_act = call(d_act_kernel, sds((TOK, FS), F32), [], [*dys, w_down], 4, deps=[o])
    side = [sds((2, ROWS, D))] * 2
    keep, send = call(out_kernel, side, [], [o_tok, w_out], 2, deps=[d_act])
    terms, _ = scatter_slots(keep, send)
    hidden, xm = call(
        hidden_kernel, [sds((ROWS, D), F32), sds((ROWS, D))], [], [own_x, *terms, gain_m], 2
    )
    xms = gather_slots(xm)
    act, dg, du, keep, send = ffn(sc, xms, d_act, w_gate, w_up)
    terms, moving = scatter_slots(keep, send)

    grads = call(
        ffn_grads_kernel,
        [sds((8, 576, 128))] * 8,
        [sc],
        [*xms, *dys, act, dg, du],
        9,
        [pltpu.VMEM((TOK, D), BF)],
        [moving],
    )
    keeps, sends = grads[:4], grads[4:]
    gots = [swap_cube(s, p) for p, s in enumerate(sends)]
    d_hidden, d_br, d_gain = call(
        d_hidden_kernel,
        [sds((ROWS, D), F32), sds((ROWS, D)), sds((16, 128))],
        [],
        [own_dy, *terms, hidden, gain_m],
        2,
        deps=[sends[0]],
    )
    d_brs = gather_slots(d_br)
    d_o = call(d_o_kernel, sds(folded), [], [*d_brs, w_out], 2)
    d_o_att = exchange(d_o, heads)
    out_pieces = call(
        out_grads_kernel,
        sds((16, OUT_ROWS + 16, 128)),
        [],
        [o_tok, *d_brs, d_gain],
        2,
        [pltpu.VMEM((DS, D), F32)],
        [d_o],
    )
    sends = first_step(keeps, gots, [out_pieces], 4)
    more = [swap_cube(s, p + 1) for p, s in enumerate(sends)]
    out_got = exchange(out_pieces, ("y", "z"))
    dq2, dkv = call(
        attention_back_kernel,
        [sds((16, ROWS, 128)), sds((32, 192, 128))],
        [query_blocks, block_order],
        [q2, d_o_att, o2, lse, kv_sorted],
        24,
        [pltpu.VMEM((SEQ, 256), F32), pltpu.VMEM((16, ROWS, 96), BF)],
        [sends[0]],
    )
    dkv_tok = exchange(dkv, CTX)
    keeps, sends = cube_step(list(zip(keeps, gots, more)), [dq2], 5)
    gots = [swap_cube(s, p + 2) for p, s in enumerate(sends)]
    out_sum = call(
        sum_kernel, sds((OUT_ROWS + 16, 128)), [], [out_got], 40, deps=[sends[0]]
    )
    dq = call(fold_dq_kernel, sds(folded), [], [dq2], 2, deps=[out_sum, dkv_tok])
    dq_tok = exchange(dq, heads)
    keeps, sends = cube_step(list(zip(keeps, gots)), [out_sum], 3)
    gots = [swap_cube(s, p + 3) for p, s in enumerate(sends)]
    total = call(
        last_step_kernel, sds((GAIN_AT + 16, 128)), [], [*keeps, *gots, out_sum], 2
    )
    total_got = swap_e(total)

    lin, keep, send = call(
        d_xa_kernel,
        [sds((TOK, 768)), *side],
        [sc],
        [dq_tok, dkv_tok, *wqs, *wkvs, cos, sin],
        7,
        [pltpu.VMEM((TOK, DS), BF), pltpu.VMEM((TOK, DS), BF)],
        [total],
    )
    *owns, gains_sum = call(
        join_kernel,
        [sds((1, n, 128)) for n in PART_ROWS] + [sds((16, 128), F32)],
        [],
        [total, total_got],
        2,
        deps=[lin],
    )
    gots = [swap_cube(o, p + 3) for p, o in enumerate(owns)]
    pieces = call(
        qkv_grads_kernel,
        sds((32, 4, QKV_ROWS, 128)),
        [],
        [xa, lin],
        5,
        [pltpu.VMEM((DS, 768), F32)],
        [owns[0]],
    )
    pieces_got = exchange(pieces, CTX)
    owns = cube_gather(owns, gots, 3, [pieces])
    gots = [swap_cube(o, p + 2) for p, o in enumerate(owns)]
    keep, send = call(
        mlp_out_kernel,
        [sds((4, ROWS, D))] * 2,
        [sc],
        [act, w_down, keep, send],
        6,
        deps=[owns[0]],
    )
    got = swap_c(send)
    owns = cube_gather(owns, gots, 4, [keep])
    gots = [swap_cube(o, p + 1) for p, o in enumerate(owns)]
    owns = cube_gather(owns, gots, 60, [])
    gots = [swap_cube(o, p) for p, o in enumerate(owns)]
    part = call(
        sum_shards_kernel,
        sds((4, QKV_ROWS + 8, 128)),
        [],
        [pieces_got, gains_sum],
        0.5,
        deps=[owns[0]],
    )
    parts, g_gain_m = call(
        repeat_kernel,
        [sds((32, 4, QKV_ROWS, 128)), sds((8, 128), F32)],
        [],
        [exchange(part, FSDP)],
        0.5,
    )
    parts_got = exchange(parts, CTX)
    far = swap_xl(call(pair_kernel, sds((2, ROWS, D)), [], [keep, got], 0.5, deps=[part]))
    layer_out, d_tokens = call(
        last_kernel,
        [sds((ROWS, D)), sds((ROWS, D), F32)],
        [],
        [own_x, keep, got, far, hidden, d_hidden, gain_a],
        0.5,
        deps=[parts],
    )
    g_gate, g_up, g_down, g_out = ffn_place(sc, owns, gots, [d_tokens])
    g_query, g_key, g_value, g_gain_a = call(
        attn_place_kernel,
        [sds((DS, D), F32), sds((DS, 768), F32), sds((DS, 768), F32), sds((1, DS), F32)],
        [],
        [parts_got, w_query, w_key, w_value, gain_attn.astype(F32).reshape(1, DS)],
        6,
        [pltpu.VMEM((DS, 768), F32)],
        [g_out],
    )

    return (
        layer_out[None],
        d_tokens[None],
        g_gain_a.reshape(DS),
        g_gain_m[0:3].reshape(DS),
        g_query,
        g_key,
        g_value,
        g_out,
        g_gate,
        g_up,
        g_down,
    )


def solution(mesh):
    cube = Mesh(mesh.devices.reshape(4, 2, 4, 2, 2), ("y", "xh", "z", "xl", "c"))
    fsdp, ctx = ("xl", "c"), ("y", "xh", "z")
    return jax.shard_map(
        body,
        mesh=cube,
        in_specs=(
            P(fsdp, ctx, None),
            P(),
            P(fsdp),
            P(fsdp),
            P(fsdp, None),
            P(fsdp, None),
            P(fsdp, None),
            P(fsdp, None),
            P(None, fsdp),
            P(None, fsdp),
            P(fsdp, None),
            P(fsdp, ctx, None),
        ),
        out_specs=(
            P(fsdp, ctx, None),
            P(fsdp, ctx, None),
            P(fsdp),
            P(fsdp),
            P(fsdp, None),
            P(fsdp, None),
            P(fsdp, None),
            P(fsdp, None),
            P(None, fsdp),
            P(None, fsdp),
            P(fsdp, None),
        ),
        check_vma=False,
    )
```

```python
import functools

import jax
import jax.numpy as jnp
from jax import lax
from jax.experimental import pallas as pl
from jax.experimental.pallas import tpu as pltpu
from jax.sharding import Mesh, PartitionSpec as P

D = 1536
HEADS = 16
KV_HEADS = 8
HEAD_DIM = 96
HALF = HEAD_DIM // 2
FF = 4096
BLOCK = 64
SEQ = 4096
WINDOW_BLOCKS = 32
SHARDS = 4
ROWS = 128
TOK = SHARDS * ROWS
DS = D // SHARDS
FS = FF // SHARDS
EPS = 1e-05
ROPE_BASE = 10000.0
MASKED = -1e30
SCALE = HEAD_DIM ** (-0.5)
LOG2E = 1.4426950408889634
BF = jnp.bfloat16
F32 = jnp.float32

CHUNK_BLOCKS = 8
CHUNK = CHUNK_BLOCKS * BLOCK

SMEM_SPEC = pl.BlockSpec(memory_space=pltpu.SMEM)
VMEM_SPEC = pl.BlockSpec(memory_space=pltpu.VMEM)
ANY_SPEC = pl.BlockSpec(memory_space=pl.ANY)
PARAMS = pltpu.CompilerParams(vmem_limit_bytes=60 * 1024 * 1024)
SMALL = pltpu.CompilerParams(vmem_limit_bytes=32 * 1024 * 1024)


def cost(us):
    flops, nbytes = int(us * 1_100_000_000), int(us * 3_000_000)
    return pl.CostEstimate(flops=flops, bytes_accessed=nbytes, transcendentals=0)


def call(kernel, outs, smem, vmem, us, scratch=(), deps=()):
    n, d = len(smem) + len(vmem), len(deps)

    def body(*refs):
        kernel(*refs[:n], *refs[n + d :])

    return pl.pallas_call(
        body,
        out_shape=outs,
        in_specs=[SMEM_SPEC] * len(smem) + [VMEM_SPEC] * len(vmem) + [ANY_SPEC] * d,
        out_specs=jax.tree.map(lambda _: VMEM_SPEC, outs),
        scratch_shapes=list(scratch),
        compiler_params=SMALL if us <= 3 else PARAMS,
        cost_estimate=cost(us),
        name=getattr(kernel, "__name__", "part"),
    )(*smem, *vmem, *deps)


def sds(shape, dtype=BF):
    return jax.ShapeDtypeStruct(shape, dtype)


def dot(a, b):
    return jnp.dot(a, b, preferred_element_type=F32)


def dot_t(a, b):
    return lax.dot_general(a, b, (((1,), (1,)), ((), ())), preferred_element_type=F32)


def t_dot(a, b):
    return lax.dot_general(a, b, (((0,), (0,)), ((), ())), preferred_element_type=F32)


def swap_c(x):
    return lax.ppermute(x, "c", [(0, 1), (1, 0)])


def swap_xl(x):
    return lax.ppermute(x, "xl", [(0, 1), (1, 0)])


def swap_both(x):
    return lax.ppermute(x, ("xl", "c"), [(i, i ^ 3) for i in range(4)])


def swap_far(x, core):
    pairs = []
    for place in range(4):
        other = (place + 1) % 4 if place % 2 else (place + 3) % 4
        for c in range(2):
            pairs.append((place * 2 + c, other * 2 + (c ^ core)))
    return lax.ppermute(x, ("xh", "xl", "c"), pairs)


def swap_e(x):
    return lax.ppermute(x, "xh", [(0, 1), (1, 0)])


NEAR = [(0, 1), (1, 0), (2, 3), (3, 2)]
AROUND = [(1, 2), (2, 1), (0, 3), (3, 0)]
CUBE = (("y", NEAR), ("y", AROUND), ("z", NEAR), ("z", AROUND))


def swap_cube(x, dim):
    axis, pairs = CUBE[dim % 4]
    return lax.ppermute(x, axis, pairs)


def from_z(x, m):
    return lax.ppermute(x, "z", [((i + m) % 4, i) for i in range(4)])


def to_z(x, m):
    return lax.ppermute(x, "z", [(i, (i + m) % 4) for i in range(4)])


def gather_slots(own):
    far = swap_xl(own)
    return own, swap_c(own), far, swap_c(far)


def scatter_slots(keep, send):
    got = swap_c(send)
    other = (keep[1].astype(F32) + got[1].astype(F32)).astype(BF)
    return (keep, got, swap_xl(other)), other


CTX = ("y", "xh", "z")
FSDP = ("xl", "c")


def after(x, other):
    return lax.optimization_barrier((x, other))[0]


def shifts(x, axis):
    return [lax.ppermute(x, axis, [((i + m) % 4, i) for i in range(4)]) for m in (1, 2, 3)]


def exchange(x, axes):
    return lax.all_to_all(x, axes, 0, 0, tiled=True)


def cube_index(portion, bits):
    out = 0
    for t in range(4):
        out = out * 2 + bits[(portion + t) % 4]
    return out


def fold(x):
    tail = jnp.concatenate([x[0:64, 128:192], x[64:128, 128:192]], axis=1)
    return jnp.concatenate([x[:, 0:128], tail], axis=0)


def unfold(x):
    tail = jnp.concatenate([x[128:192, 0:64], x[128:192, 64:128]], axis=0)
    return jnp.concatenate([x[0:128], tail], axis=1)


def pack_kernel(sc, wq, wk, wv, gains, q0, q1, q2, q3, k0, k1, k2, k3, tmp):
    f = sc[0]
    for g in range(4):
        tmp[g, :, 0:192] = wk[:, 192 * g : 192 * (g + 1)]
        tmp[g, :, 192:384] = wv[:, 192 * g : 192 * (g + 1)]
    for k, (q, kv) in enumerate(((q0, k0), (q1, k1), (q2, k2), (q3, k3))):
        q[...] = wq[:, pl.ds(pl.multiple_of((f ^ k) * DS, 128), DS)]
        kv[0:DS] = tmp[f ^ k]
        kv[DS:] = gains[...]


def project(f, xa, ws):
    total = jnp.zeros((TOK, DS), F32)
    for k, w in enumerate(ws):
        at = pl.multiple_of((f ^ k) * DS, 128)
        total = total + dot(xa[:, pl.ds(at, DS)], w[0:DS])
    return total


def rotate(u, co, si):
    turned = jnp.concatenate([-u[:, HALF:], u[:, :HALF]], axis=1)
    return u * co + turned * si


def kv_kernel(sc, x0, x1, x2, x3, k0, k1, k2, k3, cos, sin, xa, kv, gain_a, gain_m):
    f = sc[0]
    for k, w in enumerate((k0, k1, k2, k3)):
        at = pl.ds(pl.multiple_of((f ^ k) * DS, 128), DS)
        rows = w[DS:].astype(F32)
        gain_a[:, at] = rows[0:1]
        gain_m[:, at] = rows[1:2]
    for k, x in enumerate((x0, x1, x2, x3)):
        u = x[...].astype(F32)
        r = lax.rsqrt(jnp.mean(u * u, axis=-1, keepdims=True) + EPS)
        xa[ROWS * k : ROWS * (k + 1), :] = (u * r * gain_a[...]).astype(BF)
    lin = project(f, xa, [w[0:DS] for w in (k0, k1, k2, k3)])
    co, si = cos[...], sin[...]
    for k in range(4):
        part = lin[ROWS * k : ROWS * (k + 1)]
        for j in range(2):
            key = rotate(part[:, 96 * j : 96 * (j + 1)], co, si)
            value = part[:, 192 + 96 * j : 192 + 96 * (j + 1)]
            kv[2 * k + j] = fold(jnp.concatenate([key, value], axis=1)).astype(BF)


def q_kernel(sc, xa, w0, w1, w2, w3, cos, sin, q):
    lin = project(sc[0], xa, (w0, w1, w2, w3))
    co, si = cos[...], sin[...]
    for k in range(4):
        part = lin[ROWS * k : ROWS * (k + 1)]
        heads = [rotate(part[:, 96 * h : 96 * (h + 1)], co, si) for h in range(4)]
        for j in range(2):
            q[2 * k + j] = fold(jnp.concatenate(heads[2 * j : 2 * j + 2], axis=1)).astype(BF)


def widen(x, *tail):
    zeros = jnp.zeros((x.shape[0], 128 - x.shape[1] - len(tail)), x.dtype)
    return jnp.concatenate([x, *tail, zeros], axis=1)


def stacked(x, t):
    rows = slice(BLOCK * t, BLOCK * (t + 1))
    return jnp.concatenate([x[rows, 0:96], x[rows, 96:192]], axis=0)


def side_by_side(a, b):
    rows = [jnp.concatenate([x[0:BLOCK, 0:96], x[BLOCK:, 0:96]], axis=1) for x in (a, b)]
    return fold(jnp.concatenate(rows, axis=0))


def low_high(qb, n):
    swapped = (qb[2 * n] >= WINDOW_BLOCKS).astype(jnp.int32)
    return 2 * n + swapped, 2 * n + 1 - swapped


def attention_kernel(qb, kb, q, kv0, kv1, kv2, kv3, o, o2, q2, lse, kv):
    ones = (lax.broadcasted_iota(jnp.int32, (BLOCK, 32), 1) < 4).astype(F32)

    def place(s, _):
        for m, ref in enumerate((kv0, kv1, kv2, kv3)):
            x = unfold(ref[s].astype(F32))
            for t in range(2):
                dst = pl.ds(pl.multiple_of(kb[m * 16 + 2 * s + t] * BLOCK, BLOCK), BLOCK)
                part = x[BLOCK * t : BLOCK * (t + 1)]
                both = jnp.concatenate([part[:, 0:96], ones, part[:, 96:192], ones], axis=1)
                kv[dst, :] = both.astype(BF)
        x = unfold(q[s].astype(F32))
        for t in range(2):
            q2[2 * s + t] = widen(stacked(x, t)).astype(BF)
        return 0

    lax.fori_loop(0, 8, place, 0)
    two = SCALE * LOG2E

    def scores(n, spans):
        return [dot_t(q2[n], kv[span, 0:128]) for span in spans]

    def finish(n, parts, spans):
        tops = [jnp.max(s, axis=1, keepdims=True) for s in parts]
        top = functools.reduce(jnp.maximum, tops) * two
        acc = jnp.zeros((ROWS, 128), F32)
        for s, span in zip(parts, spans):
            acc += dot(jnp.exp2(s * two - top).astype(BF), kv[span, 128:256])
        total = acc[:, 96:97]
        o2[n] = (acc / total).astype(BF)
        lse[n] = jnp.broadcast_to(top + jnp.log2(total), (ROWS, 8))

    def pair(n, _):
        low, high = low_high(qb, n)
        i_low, i_high = qb[low], qb[high]
        for count in range(1, 5):

            @pl.when(i_low // CHUNK_BLOCKS == count - 1)
            def _():
                edge = pl.ds(pl.multiple_of((i_high - WINDOW_BLOCKS) * BLOCK, BLOCK), BLOCK)
                at = pl.multiple_of((i_high - WINDOW_BLOCKS + 1) * BLOCK, BLOCK)
                spans_h = [edge] + [pl.ds(at + CHUNK * t, CHUNK) for t in range(4)]
                spans_l = [pl.ds(CHUNK * t, CHUNK) for t in range(count)]
                high_s = scores(high, spans_h)
                low_s = scores(low, spans_l)
                key = lax.broadcasted_iota(jnp.int32, (ROWS, BLOCK), 1)
                query = lax.broadcasted_iota(jnp.int32, (ROWS, BLOCK), 0) % BLOCK
                high_s[0] = jnp.where(key > query, high_s[0], MASKED)
                key = lax.broadcasted_iota(jnp.int32, (ROWS, CHUNK), 1)
                limit = (i_low + 1) * BLOCK - CHUNK * (count - 1)
                low_s[-1] = jnp.where(key < limit, low_s[-1], MASKED)
                finish(high, high_s, spans_h)
                finish(low, low_s, spans_l)

        return 0

    lax.fori_loop(0, 8, pair, 0)

    def gather(s, _):
        o[s] = side_by_side(o2[2 * s].astype(F32), o2[2 * s + 1].astype(F32)).astype(BF)
        return 0

    lax.fori_loop(0, 8, gather, 0)


def attention_back_kernel(qb, kb, q2s, d_o, o2s, lse, kv, dq2s, g, dkv, do2s):
    dkv[...] = jnp.zeros_like(dkv)

    def place(s, _):
        x = unfold(d_o[s].astype(F32))
        for t in range(2):
            do2s[2 * s + t] = stacked(x, t).astype(BF)
        return 0

    lax.fori_loop(0, 8, place, 0)
    two = SCALE * LOG2E

    def split(x):
        parts = []
        for _ in range(3):
            parts.append(x.astype(BF))
            x = x - parts[-1].astype(F32)
        return parts

    def weights(n):
        do2 = do2s[n]
        inner = do2.astype(F32) * o2s[n][:, 0:96].astype(F32)
        inner = jnp.sum(inner, axis=1, keepdims=True)
        q2 = widen(q2s[n][:, 0:96], *split(lse[n][:, 0:1] * (-1.0 / two)))
        do2 = widen(do2, *split(-inner))
        none = jnp.zeros((ROWS, 128), BF)
        return jnp.concatenate(
            [jnp.concatenate([q2, none], axis=1), jnp.concatenate([none, do2], axis=1)], axis=0
        )

    def factors(w, spans, masks):
        pairs = []
        for span, mask in zip(spans, masks):
            s = dot_t(kv[span, :], w)
            p = jnp.exp2(s[:, 0:128] * two)
            if mask is not None:
                p = jnp.where(mask, p, 0.0)
            ds = (p * s[:, 128:256]).astype(BF)
            pairs.append(jnp.concatenate([ds, p.astype(BF)], axis=1))
        return pairs

    def add(n, w, spans, pairs):
        acc = jnp.zeros((ROWS, 128), F32)
        for span, both in zip(spans, pairs):
            dkv[span, :] += dot(both, w)
            acc += t_dot(both[:, 0:128], kv[span, 0:128])
        dq2s[n] = (acc * SCALE).astype(BF)

    def pair(n, _):
        low, high = low_high(qb, n)
        i_low, i_high = qb[low], qb[high]
        for count in range(1, 5):

            @pl.when(i_low // CHUNK_BLOCKS == count - 1)
            def _():
                edge = pl.ds(pl.multiple_of((i_high - WINDOW_BLOCKS) * BLOCK, BLOCK), BLOCK)
                at = pl.multiple_of((i_high - WINDOW_BLOCKS + 1) * BLOCK, BLOCK)
                key = lax.broadcasted_iota(jnp.int32, (BLOCK, ROWS), 0)
                query = lax.broadcasted_iota(jnp.int32, (BLOCK, ROWS), 1) % BLOCK
                spans_h = [edge] + [pl.ds(at + CHUNK * t, CHUNK) for t in range(4)]
                masks_h = [key > query] + [None] * 4
                spans_l = [pl.ds(CHUNK * t, CHUNK) for t in range(count)]
                key = lax.broadcasted_iota(jnp.int32, (CHUNK, ROWS), 0)
                limit = (i_low + 1) * BLOCK - CHUNK * (count - 1)
                masks_l = [None] * (count - 1) + [key < limit]
                w_h, w_l = weights(high), weights(low)
                pairs_h = factors(w_h, spans_h, masks_h)
                pairs_l = factors(w_l, spans_l, masks_l)
                add(high, w_h, spans_h, pairs_h)
                add(low, w_l, spans_l, pairs_l)

        return 0

    lax.fori_loop(0, 8, pair, 0)

    def keys(s, _):
        parts = []
        for t in range(2):
            src = pl.ds(pl.multiple_of(kb[2 * s + t] * BLOCK, BLOCK), BLOCK)
            both = dkv[src, :]
            parts.append(jnp.concatenate([both[:, 0:96] * SCALE, both[:, 128:224]], axis=1))
        g[s] = fold(jnp.concatenate(parts, axis=0)).astype(BF)
        return 0

    lax.fori_loop(0, 32, keys, 0)


def fold_dq_kernel(dq2s, dq):
    for s in range(8):
        dq[s] = side_by_side(dq2s[2 * s].astype(F32), dq2s[2 * s + 1].astype(F32)).astype(BF)


def unfolded(o):
    return unfold(o.astype(F32)).astype(BF)


def out_kernel(o, w, keep, send):
    for k in range(4):
        total = dot(unfolded(o[2 * k]), w[0:192, :]) + dot(unfolded(o[2 * k + 1]), w[192:384, :])
        (keep, send)[k % 2][k // 2] = total.astype(BF)


def hidden_kernel(x, keep, got, far, gain, hidden, xm):
    h = x[...].astype(F32) + keep[0].astype(F32) + got[0].astype(F32) + far[...].astype(F32)
    hidden[...] = h
    r = lax.rsqrt(jnp.mean(h * h, axis=-1, keepdims=True) + EPS)
    xm[...] = (h * r * gain[...]).astype(BF)


def norm_back(values, gain, grads):
    factor = lax.rsqrt(jnp.mean(values * values, axis=-1, keepdims=True) + EPS)
    weighted = grads * gain
    inner = jnp.mean(weighted * values, axis=-1, keepdims=True)
    return factor * weighted - values * (factor * factor * factor) * inner


def d_hidden_kernel(dy, keep, got, far, hidden, gain, d_hidden, d_br, d_gain):
    grads = keep[0].astype(F32) + got[0].astype(F32) + far[...].astype(F32)
    h = hidden[...]
    d = dy[...].astype(F32) + norm_back(h, gain[...], grads)
    d_hidden[...] = d
    d_br[...] = d.astype(BF)
    r = lax.rsqrt(jnp.mean(h * h, axis=-1, keepdims=True) + EPS)
    total = jnp.sum(grads * h * r, axis=0, keepdims=True)
    rows = [total[:, 128 * t : 128 * (t + 1)] for t in range(12)]
    d_gain[...] = jnp.concatenate(rows + [jnp.zeros((4, 128), F32)], axis=0).astype(BF)


def pair_kernel(keep, got, out):
    out[...] = (keep[2:].astype(F32) + got[2:].astype(F32)).astype(BF)


def last_kernel(x, keep, got, far, hidden, d_hidden, gain, layer_out, d_tokens):
    total = keep[0].astype(F32) + got[0].astype(F32) + far[0].astype(F32)
    layer_out[...] = (hidden[...] + total).astype(BF)
    grads = keep[1].astype(F32) + got[1].astype(F32) + far[1].astype(F32)
    d_tokens[...] = d_hidden[...] + norm_back(x[...].astype(F32), gain[...], grads)


def d_o_kernel(b0, b1, b2, b3, w, d_o):
    for k, b in enumerate((b0, b1, b2, b3)):
        d = dot_t(b[...], w[...])
        d_o[2 * k] = fold(d[:, 0:192]).astype(BF)
        d_o[2 * k + 1] = fold(d[:, 192:384]).astype(BF)


FBLOCK = 512


def d_act_kernel(y0, y1, y2, y3, wd, da):
    ys = jnp.concatenate([y0[...], y1[...], y2[...], y3[...]], axis=0)
    da[...] = dot_t(ys, wd[...])


def ffn_kernel(sc, x0, x1, x2, x3, da, wg, wu, act, dg, du, keep, send, xs, acc):
    n = pl.program_id(0)

    @pl.when(n == 0)
    def _():
        for k, x in enumerate((x0, x1, x2, x3)):
            xs[ROWS * k : ROWS * (k + 1), :] = x[...]

    gate = dot(xs[...], wg[...])
    up = dot(xs[...], wu[...])
    d = da[...]
    sg = jax.nn.sigmoid(gate)
    both = gate * sg
    a = (both * up).astype(BF)
    d_gate = (d * up * sg * (1.0 + gate * (1.0 - sg))).astype(BF)
    d_up = (d * both).astype(BF)
    for h in range(2):
        at = pl.multiple_of((h ^ (sc[2] & 1)) * 256, 256)
        for ref, tile in ((act, a), (dg, d_gate), (du, d_up)):
            ref[:, pl.ds(at, 256)] = tile[:, 256 * h : 256 * (h + 1)]
    dx = dot_t(d_gate, wg[...]) + dot_t(d_up, wu[...])

    @pl.when(n == 0)
    def _():
        acc[...] = dx

    @pl.when(n > 0)
    def _():
        total = acc[...] + dx
        for k in range(4):
            (keep, send)[k % 2][k // 2] = total[ROWS * k : ROWS * (k + 1), :].astype(BF)


def ffn(sc, xs, da, wg, wu):
    full = pl.BlockSpec((ROWS, D), lambda n, s: (0, 0))
    side = pl.BlockSpec((2, ROWS, D), lambda n, s: (0, 0, 0))
    cols = pl.BlockSpec((D, FBLOCK), lambda n, s: (0, n))
    rel = pl.BlockSpec((TOK, FBLOCK), lambda n, s: (0, n ^ (s[2] >> 1)))
    return pl.pallas_call(
        ffn_kernel,
        grid_spec=pltpu.PrefetchScalarGridSpec(
            num_scalar_prefetch=1,
            grid=(FS // FBLOCK,),
            in_specs=[full] * 4 + [pl.BlockSpec((TOK, FBLOCK), lambda n, s: (0, n)), cols, cols],
            out_specs=[rel, rel, rel, side, side],
            scratch_shapes=[pltpu.VMEM((TOK, D), BF), pltpu.VMEM((TOK, D), F32)],
        ),
        out_shape=[sds((TOK, FS))] * 3 + [sds((2, ROWS, D))] * 2,
        compiler_params=PARAMS,
        cost_estimate=cost(11),
    )(sc, *xs, da, wg, wu)


def mlp_out_kernel(sc, act, wd, keep_in, send_in, keep, send):
    gz = sc[2]
    acts = [
        act[:, pl.ds(pl.multiple_of((b ^ gz) * 256, 256), 256)] for b in range(FS // 256)
    ]
    total = dot(jnp.concatenate(acts, axis=1), wd[...])
    for k in range(4):
        (keep, send)[k % 2][2 * (k // 2)] = total[ROWS * k : ROWS * (k + 1)].astype(BF)
    for k in range(2):
        keep[2 * k + 1] = keep_in[k]
        send[2 * k + 1] = send_in[k]


def ffn_grads_kernel(sc, x0, x1, x2, x3, y0, y1, y2, y3, act, dg, du, *refs):
    gy = sc[1]
    keeps, sends, ys = refs[:4], refs[4:8], refs[8]

    def put(p, ra, rb, at, tile):
        index = cube_index(p, (ra & 1, ra >> 1, rb & 1, rb >> 1))
        ref = (keeps, sends)[index >> 3][p]
        ref[index & 7, at : at + tile.shape[0], :] = tile.astype(BF)

    for ra in range(4):
        cols = pl.ds(pl.multiple_of((ra ^ gy) * DS, 128), DS)
        xa = jnp.concatenate([x[:, cols] for x in (x0, x1, x2, x3)], axis=0)
        for k, y in enumerate((y0, y1, y2, y3)):
            ys[ROWS * k : ROWS * (k + 1), DS * ra : DS * (ra + 1)] = y[:, cols]
        for n, d in enumerate((dg, du)):
            wide = t_dot(xa, d[...])
            for rb in range(4):
                for p in range(4):
                    lane, row = 256 * rb + 128 * (p // 2), 192 * (p % 2)
                    put(p, ra, rb, 192 * n, wide[row : row + 192, lane : lane + 128])
    for rb in range(4):
        wide = t_dot(act[:, 256 * rb : 256 * (rb + 1)], ys[...])
        for ra in range(4):
            for p in range(4):
                at = 384
                row = 192 * p
                while row < 192 * (p + 1):
                    lane, r = DS * ra + 128 * (row // 256), row % 256
                    size = min(256 - r, 192 * (p + 1) - row)
                    put(p, ra, rb, at, wide[r : r + size, lane : lane + 128])
                    at += size
                    row += size


OUT_ROWS = 288
OUT_SPLIT = (80, 80, 64, 64)
OUT_AT = (0, 80, 160, 224)
PART_ROWS = tuple(576 + n for n in OUT_SPLIT)
PART_AT = (0, 656, 1312, 1952)
GAIN_AT = 2592


def first_step(keeps, gots, deps, us):
    def body(*refs):
        for p in range(4):
            k, g, out = refs[2 * p], refs[2 * p + 1], refs[8 + len(deps) + p]
            out[...] = (k[...].astype(F32) + g[...].astype(F32)).astype(BF)

    args = [x for pair in zip(keeps, gots) for x in pair]
    return pl.pallas_call(
        body,
        grid=(4,),
        in_specs=[pl.BlockSpec((1, 576, 128), lambda n: (n + 4, 0, 0))] * 8
        + [ANY_SPEC] * len(deps),
        out_specs=[pl.BlockSpec((1, 576, 128), lambda n: (n, 0, 0))] * 4,
        out_shape=[sds((4, 576, 128))] * 4,
        compiler_params=PARAMS,
        cost_estimate=cost(us),
    )(*args, *deps)


def cube_step(terms, deps, us):
    count = len(terms[0])
    half = terms[0][-1].shape[0] // 2
    lower = pl.BlockSpec((1, 576, 128), lambda n: (n, 0, 0))
    upper = pl.BlockSpec((1, 576, 128), lambda n: (n + half, 0, 0))
    used = 8 * count

    def body(*refs):
        outs = refs[used + len(deps) :]
        for p in range(4):
            mine = refs[2 * count * p : 2 * count * (p + 1)]
            for side in range(2):
                total = mine[side][...].astype(F32)
                for t in range(1, count):
                    total += mine[2 * t + side][...].astype(F32)
                outs[2 * p + side][...] = total.astype(BF)

    args = [x for portion in terms for term in portion for x in (term, term)]
    outs = pl.pallas_call(
        body,
        grid=(half,),
        in_specs=[lower, upper] * (4 * count) + [ANY_SPEC] * len(deps),
        out_specs=[lower] * 8,
        out_shape=[sds((half, 576, 128))] * 8,
        compiler_params=PARAMS,
        cost_estimate=cost(us),
    )(*args, *deps)
    return outs[0::2], outs[1::2]


def last_step_kernel(k0, k1, k2, k3, g0, g1, g2, g3, out, total):
    for p, (k, g) in enumerate(((k0, g0), (k1, g1), (k2, g2), (k3, g3))):
        at = PART_AT[p]
        total[at : at + 576, :] = (k[0].astype(F32) + g[0].astype(F32)).astype(BF)
        total[at + 576 : at + PART_ROWS[p], :] = out[OUT_AT[p] : OUT_AT[p] + OUT_SPLIT[p]]
    total[GAIN_AT:, :] = out[OUT_ROWS:]


def join_kernel(own, got, p0, p1, p2, p3, gains):
    total = own[...].astype(F32) + got[...].astype(F32)
    for p, ref in enumerate((p0, p1, p2, p3)):
        ref[0] = total[PART_AT[p] : PART_AT[p] + PART_ROWS[p]].astype(BF)
    gains[...] = total[GAIN_AT:]


def stack_kernel(a0, a1, a2, a3, b0, b1, b2, b3, o0, o1, o2, o3):
    for a, b, o in ((a0, b0, o0), (a1, b1, o1), (a2, b2, o2), (a3, b3, o3)):
        o[0 : a.shape[0]] = a[...]
        o[a.shape[0] :] = b[...]


def cube_gather(owns, gots, us, deps):
    outs = [sds((2 * o.shape[0], *o.shape[1:])) for o in owns]
    return call(stack_kernel, outs, [], [*owns, *gots], us, deps=deps)


def pick(owns, gots, p, bits, rows):
    index = cube_index(p, bits)
    rest = index & 7
    return jnp.where(index >= 8, gots[p][rest, rows, :], owns[p][rest, rows, :])


def ffn_place_kernel(sc, *refs):
    owns, gots = refs[0:4], refs[4:8]
    gate, up, down, out, tmp = refs[8:]
    gy, gz = sc[1], sc[2]
    ra = pl.program_id(0) ^ gy
    for bb in range(4):
        rb = bb ^ gz
        bits = (ra & 1, ra >> 1, rb & 1, rb >> 1)
        for p in range(4):
            lane, row = 256 * bb + 128 * (p // 2), 192 * (p % 2)
            for n, ref in enumerate((gate, up)):
                tile = pick(owns, gots, p, bits, slice(192 * n, 192 * (n + 1)))
                ref[row : row + 192, lane : lane + 128] = tile.astype(F32)
            at, row = 384, 192 * p
            while row < 192 * (p + 1):
                lane, r = row // 256, row % 256
                size = min(256 - r, 192 * (p + 1) - row)
                tile = pick(owns, gots, p, bits, slice(at, at + size))
                down[256 * bb + r : 256 * bb + r + size, 128 * lane : 128 * (lane + 1)] = (
                    tile.astype(F32)
                )
                at += size
                row += size
            at = OUT_ROWS * (bb ^ (bb >> 1)) + OUT_AT[p]
            tile = pick(owns, gots, p, bits, slice(576, PART_ROWS[p]))
            tmp[at : at + OUT_SPLIT[p], :] = tile.astype(F32)
    for t in range(3):
        out[:, 128 * t : 128 * (t + 1)] = tmp[DS * t : DS * (t + 1), :]


def ffn_place(sc, owns, gots, deps):
    def body(*refs):
        ffn_place_kernel(*refs[:9], *refs[9 + len(deps) :])

    whole = [pl.BlockSpec((8, n, 128), lambda n, s: (0, 0, 0)) for n in PART_ROWS]
    rows = pl.BlockSpec((DS, FS), lambda n, s: (n, 0))
    return pl.pallas_call(
        body,
        grid_spec=pltpu.PrefetchScalarGridSpec(
            num_scalar_prefetch=1,
            grid=(4,),
            in_specs=whole * 2 + [ANY_SPEC] * len(deps),
            out_specs=[
                rows,
                rows,
                pl.BlockSpec((FS, DS), lambda n, s: (0, n)),
                pl.BlockSpec((DS, DS), lambda n, s: (0, n ^ (n >> 1))),
            ],
            scratch_shapes=[pltpu.VMEM((4 * OUT_ROWS, 128), F32)],
        ),
        out_shape=[sds((D, FS), F32), sds((D, FS), F32), sds((FS, D), F32), sds((DS, D), F32)],
        compiler_params=PARAMS,
        cost_estimate=cost(60),
    )(sc, *owns, *gots, *deps)


def out_grads_kernel(o, b0, b1, b2, b3, d_gain, pieces, tmp):
    bs = jnp.concatenate([b0[...], b1[...], b2[...], b3[...]], axis=0)
    for j in range(2):
        oj = jnp.concatenate([unfolded(o[2 * k + j]) for k in range(4)], axis=0)
        tmp[192 * j : 192 * (j + 1), :] = t_dot(oj, bs)
    for s in range(16):
        pieces[s, OUT_ROWS:, :] = d_gain[...]
        start, at = OUT_ROWS * s, 0
        while start < OUT_ROWS * (s + 1):
            lane, r = 128 * (start // DS), start % DS
            size = min(DS - r, OUT_ROWS * (s + 1) - start)
            pieces[s, at : at + size, :] = tmp[r : r + size, lane : lane + 128].astype(BF)
            at += size
            start += size


def sum_kernel(parts, out):
    out[...] = jnp.sum(parts[...].astype(F32), axis=0).astype(BF)


def sum_shards_kernel(parts, gains, out):
    for g in range(4):
        total = parts[0, g].astype(F32)
        for n in range(1, 32):
            total += parts[n, g].astype(F32)
        rows = [total, gains[3 * g : 3 * g + 3, :], jnp.zeros((5, 128), F32)]
        out[g] = jnp.concatenate(rows, axis=0).astype(BF)


def repeat_kernel(parts, out, gain):
    whole = parts[...].astype(F32)
    gain[...] = jnp.sum(whole[:, QKV_ROWS:], axis=0)
    mine = whole[:, :QKV_ROWS].astype(BF)
    for n in range(32):
        out[n] = mine


QKV_ROWS = 72


def d_xa_kernel(sc, d_q, d_kv, q0, q1, q2, q3, k0, k1, k2, k3, cos, sin, lin, keep, send, dq, dkv):
    f = sc[0]
    co, si = cos[...], sin[...]

    def back(g):
        w = g * si
        turned = jnp.concatenate([w[:, HALF:], -w[:, :HALF]], axis=1)
        return (g * co + turned).astype(BF)

    for k in range(4):
        rows = slice(ROWS * k, ROWS * (k + 1))
        for j in range(2):
            i = 2 * k + j
            gq = unfold(d_q[i].astype(F32))
            gkv = d_kv[4 * i].astype(F32)
            for z in range(1, 4):
                gkv += d_kv[4 * i + z].astype(F32)
            gkv = unfold(gkv)
            for n in range(2):
                g = back(gq[:, 96 * n : 96 * (n + 1)])
                lin[rows, 384 * j + 96 * n : 384 * j + 96 * (n + 1)] = g
                dq[rows, 192 * j + 96 * n : 192 * j + 96 * (n + 1)] = g
            g = back(gkv[:, 0:96])
            lin[rows, 384 * j + 192 : 384 * j + 288] = g
            dkv[rows, 96 * j : 96 * (j + 1)] = g
            g = gkv[:, 96:192].astype(BF)
            lin[rows, 384 * j + 288 : 384 * j + 384] = g
            dkv[rows, 192 + 96 * j : 192 + 96 * (j + 1)] = g
    for k, (wq, wkv) in enumerate(((q0, k0), (q1, k1), (q2, k2), (q3, k3))):
        cols = pl.ds(pl.multiple_of((f ^ k) * DS, 128), DS)
        total = (dot_t(dq[...], wq[...]) + dot_t(dkv[...], wkv[0:DS])).astype(BF)
        for s in range(4):
            (keep, send)[s % 2][s // 2, :, cols] = total[ROWS * s : ROWS * (s + 1)]


def flat_pieces(n):
    out, start = [], QKV_ROWS * n
    while start < QKV_ROWS * (n + 1):
        r = start % DS
        size = min(DS - r, QKV_ROWS * (n + 1) - start)
        out.append((128 * (start // DS), r, size))
        start += size
    return out


def qkv_grads_kernel(xa, lin, pieces, tmp):
    for g in range(4):
        tmp[...] = t_dot(xa[:, DS * g : DS * (g + 1)], lin[...])
        for n in range(32):
            tiles = [tmp[r : r + size, lane : lane + 128] for lane, r, size in flat_pieces(n)]
            pieces[n, g] = jnp.concatenate(tiles, axis=0).astype(BF)


def attn_place_kernel(got, wq, wk, wv, gain_in, q, k, v, gain, tmp):
    for g in range(4):
        for n in range(32):
            tile, at = got[n, g].astype(F32), 0
            for lane, r, size in flat_pieces(n):
                tmp[r : r + size, lane : lane + 128] = tile[at : at + size]
                at += size
        for j in range(2):
            at = 384 * j
            q[:, 384 * g + 192 * j : 384 * g + 192 * (j + 1)] = tmp[:, at : at + 192]
            k[:, 192 * g + 96 * j : 192 * g + 96 * (j + 1)] = tmp[:, at + 192 : at + 288]
            v[:, 192 * g + 96 * j : 192 * g + 96 * (j + 1)] = tmp[:, at + 288 : at + 384]
    total = jnp.sum(wq[...].astype(F32) * q[...], axis=1, keepdims=True)
    total += jnp.sum(wk[...].astype(F32) * k[...], axis=1, keepdims=True)
    total += jnp.sum(wv[...].astype(F32) * v[...], axis=1, keepdims=True)
    gain[...] = jnp.broadcast_to(total, (DS, 128)).T[0:1] / gain_in[...]


def rope_tables(positions):
    freqs = ROPE_BASE ** (-jnp.arange(HALF).astype(F32) * 2.0 / HEAD_DIM)
    angles = positions.astype(F32)[:, None] * freqs[None, :]
    angles = jnp.concatenate([angles, angles], axis=1)
    return jnp.cos(angles), jnp.sin(angles)


def body(
    tokens,
    block_order,
    gain_attn,
    gain_mlp,
    w_query,
    w_key,
    w_value,
    w_out,
    w_gate,
    w_up,
    w_down,
    cotangent,
):
    y, xh, z = lax.axis_index("y"), lax.axis_index("xh"), lax.axis_index("z")
    xl, c = lax.axis_index("xl"), lax.axis_index("c")
    f = xl * 2 + c
    gy, gz = y ^ (y >> 1), z ^ (z >> 1)
    sc = jnp.stack([f, gy, gz]).astype(jnp.int32)
    own_x, own_dy = tokens[0], cotangent[0]

    place = (y * 2 + xh) * 4 + z
    own_blocks = lax.dynamic_slice_in_dim(block_order, 2 * place, 2)
    positions = (own_blocks[:, None] * BLOCK + jnp.arange(BLOCK)).reshape(-1)
    cos, sin = rope_tables(positions)
    blocks = block_order.reshape(8, 4, 2)
    key_blocks = jnp.stack(
        [
            lax.dynamic_index_in_dim(blocks, (z + m) % 4, axis=1, keepdims=False).reshape(-1)
            for m in range(4)
        ]
    ).reshape(-1)
    query_blocks = key_blocks[:16]

    xs = gather_slots(own_x)
    packs = call(
        pack_kernel,
        [sds((DS, DS))] * 4 + [sds((DS + 16, DS))] * 4,
        [sc],
        [w_query, w_key, w_value, jnp.pad(jnp.stack([gain_attn, gain_mlp]), ((0, 14), (0, 0)))],
        3,
        [pltpu.VMEM((4, DS, DS), BF)],
    )
    wkvs = (packs[4], swap_c(packs[5]), swap_xl(packs[6]), swap_far(packs[7], 1))
    wqs = (packs[0], swap_c(packs[1]), swap_far(packs[2], 0), swap_far(packs[3], 1))

    folded, heads = (8, 192, 128), ("y", "xh")
    xa, kv, gain_a, gain_m = call(
        kv_kernel,
        [sds((TOK, D)), sds(folded), sds((1, D), F32), sds((1, D), F32)],
        [sc],
        [*xs, *wkvs, cos, sin],
        5,
    )
    q = call(q_kernel, sds(folded), [sc], [xa, *wqs, cos, sin], 4)
    kv = exchange(kv, heads)
    kvs = shifts(kv, "z")
    q = exchange(q, heads)
    o, o2, q2, lse, kv_sorted = call(
        attention_kernel,
        [
            sds(folded),
            sds((16, ROWS, 128)),
            sds((16, ROWS, 128)),
            sds((16, ROWS, 8), F32),
            sds((SEQ, 256)),
        ],
        [query_blocks, key_blocks],
        [q, kv, *kvs],
        13,
    )
    o_tok = exchange(o, heads)

    dys = gather_slots(own_dy)
    d_act = call(d_act_kernel, sds((TOK, FS), F32), [], [*dys, w_down], 4, deps=[o])
    side = [sds((2, ROWS, D))] * 2
    keep, send = call(out_kernel, side, [], [o_tok, w_out], 2, deps=[d_act])
    terms, _ = scatter_slots(keep, send)
    hidden, xm = call(
        hidden_kernel, [sds((ROWS, D), F32), sds((ROWS, D))], [], [own_x, *terms, gain_m], 2
    )
    xms = gather_slots(xm)
    act, dg, du, keep, send = ffn(sc, xms, d_act, w_gate, w_up)
    terms, moving = scatter_slots(keep, send)

    grads = call(
        ffn_grads_kernel,
        [sds((8, 576, 128))] * 8,
        [sc],
        [*xms, *dys, act, dg, du],
        9,
        [pltpu.VMEM((TOK, D), BF)],
        [moving],
    )
    keeps, sends = grads[:4], grads[4:]
    gots = [swap_cube(s, p) for p, s in enumerate(sends)]
    d_hidden, d_br, d_gain = call(
        d_hidden_kernel,
        [sds((ROWS, D), F32), sds((ROWS, D)), sds((16, 128))],
        [],
        [own_dy, *terms, hidden, gain_m],
        2,
        deps=[sends[0]],
    )
    d_brs = gather_slots(d_br)
    d_o = call(d_o_kernel, sds(folded), [], [*d_brs, w_out], 2)
    d_o_att = exchange(d_o, heads)
    out_pieces = call(
        out_grads_kernel,
        sds((16, OUT_ROWS + 16, 128)),
        [],
        [o_tok, *d_brs, d_gain],
        2,
        [pltpu.VMEM((DS, D), F32)],
        [d_o],
    )
    sends = first_step(keeps, gots, [out_pieces], 4)
    more = [swap_cube(s, p + 1) for p, s in enumerate(sends)]
    out_got = exchange(out_pieces, ("y", "z"))
    dq2, dkv = call(
        attention_back_kernel,
        [sds((16, ROWS, 128)), sds((32, 192, 128))],
        [query_blocks, block_order],
        [q2, d_o_att, o2, lse, kv_sorted],
        24,
        [pltpu.VMEM((SEQ, 256), F32), pltpu.VMEM((16, ROWS, 96), BF)],
        [sends[0]],
    )
    dkv_tok = exchange(dkv, CTX)
    keeps, sends = cube_step(list(zip(keeps, gots, more)), [dq2], 5)
    gots = [swap_cube(s, p + 2) for p, s in enumerate(sends)]
    out_sum = call(
        sum_kernel, sds((OUT_ROWS + 16, 128)), [], [out_got], 40, deps=[sends[0]]
    )
    dq = call(fold_dq_kernel, sds(folded), [], [dq2], 2, deps=[out_sum, dkv_tok])
    dq_tok = exchange(dq, heads)
    keeps, sends = cube_step(list(zip(keeps, gots)), [out_sum], 3)
    gots = [swap_cube(s, p + 3) for p, s in enumerate(sends)]
    total = call(
        last_step_kernel, sds((GAIN_AT + 16, 128)), [], [*keeps, *gots, out_sum], 2
    )
    total_got = swap_e(total)

    lin, keep, send = call(
        d_xa_kernel,
        [sds((TOK, 768)), *side],
        [sc],
        [dq_tok, dkv_tok, *wqs, *wkvs, cos, sin],
        7,
        [pltpu.VMEM((TOK, DS), BF), pltpu.VMEM((TOK, DS), BF)],
        [total],
    )
    *owns, gains_sum = call(
        join_kernel,
        [sds((1, n, 128)) for n in PART_ROWS] + [sds((16, 128), F32)],
        [],
        [total, total_got],
        2,
        deps=[lin],
    )
    gots = [swap_cube(o, p + 3) for p, o in enumerate(owns)]
    pieces = call(
        qkv_grads_kernel,
        sds((32, 4, QKV_ROWS, 128)),
        [],
        [xa, lin],
        5,
        [pltpu.VMEM((DS, 768), F32)],
        [owns[0]],
    )
    pieces_got = exchange(pieces, CTX)
    owns = cube_gather(owns, gots, 3, [pieces])
    gots = [swap_cube(o, p + 2) for p, o in enumerate(owns)]
    keep, send = call(
        mlp_out_kernel,
        [sds((4, ROWS, D))] * 2,
        [sc],
        [act, w_down, keep, send],
        6,
        deps=[owns[0]],
    )
    got = swap_c(send)
    owns = cube_gather(owns, gots, 4, [keep])
    gots = [swap_cube(o, p + 1) for p, o in enumerate(owns)]
    owns = cube_gather(owns, gots, 60, [])
    gots = [swap_cube(o, p) for p, o in enumerate(owns)]
    part = call(
        sum_shards_kernel,
        sds((4, QKV_ROWS + 8, 128)),
        [],
        [pieces_got, gains_sum],
        0.5,
        deps=[owns[0]],
    )
    parts, g_gain_m = call(
        repeat_kernel,
        [sds((32, 4, QKV_ROWS, 128)), sds((8, 128), F32)],
        [],
        [exchange(part, FSDP)],
        0.5,
    )
    parts_got = exchange(parts, CTX)
    far = swap_xl(call(pair_kernel, sds((2, ROWS, D)), [], [keep, got], 0.5, deps=[part]))
    layer_out, d_tokens = call(
        last_kernel,
        [sds((ROWS, D)), sds((ROWS, D), F32)],
        [],
        [own_x, keep, got, far, hidden, d_hidden, gain_a],
        0.5,
        deps=[parts],
    )
    g_gate, g_up, g_down, g_out = ffn_place(sc, owns, gots, [d_tokens])
    g_query, g_key, g_value, g_gain_a = call(
        attn_place_kernel,
        [sds((DS, D), F32), sds((DS, 768), F32), sds((DS, 768), F32), sds((1, DS), F32)],
        [],
        [parts_got, w_query, w_key, w_value, gain_attn.astype(F32).reshape(1, DS)],
        6,
        [pltpu.VMEM((DS, 768), F32)],
        [g_out],
    )

    return (
        layer_out[None],
        d_tokens[None],
        g_gain_a.reshape(DS),
        g_gain_m[0:3].reshape(DS),
        g_query,
        g_key,
        g_value,
        g_out,
        g_gate,
        g_up,
        g_down,
    )


def solution(mesh):
    cube = Mesh(mesh.devices.reshape(4, 2, 4, 2, 2), ("y", "xh", "z", "xl", "c"))
    fsdp, ctx = ("xl", "c"), ("y", "xh", "z")
    return jax.shard_map(
        body,
        mesh=cube,
        in_specs=(
            P(fsdp, ctx, None),
            P(),
            P(fsdp),
            P(fsdp),
            P(fsdp, None),
            P(fsdp, None),
            P(fsdp, None),
            P(fsdp, None),
            P(None, fsdp),
            P(None, fsdp),
            P(fsdp, None),
            P(fsdp, ctx, None),
        ),
        out_specs=(
            P(fsdp, ctx, None),
            P(fsdp, ctx, None),
            P(fsdp),
            P(fsdp),
            P(fsdp, None),
            P(fsdp, None),
            P(fsdp, None),
            P(fsdp, None),
            P(None, fsdp),
            P(None, fsdp),
            P(fsdp, None),
        ),
        check_vma=False,
    )
```
